32 devices in a mesh: dp: 8 (over y, x, core), tensor: 4 (over z).
Axes of the slice: x: 2, y: 2, z: 4, core: 2. Of those that a mesh axis runs over, the one named last changes fastest.
Arguments:
- query_stream: bfloat16 [16384, 512], P(('dp', 'tensor')), may hold values from -6 to 6
- token_stream: bfloat16 [16384, 512], P(('dp', 'tensor')), may hold values from -6 to 6
- encoder_states: bfloat16 [24576, 512], P(('dp', 'tensor')), may hold values from -6 to 6
- token_segment: int32 [16, 1024], P('dp'), may hold values from 0 to 7, never falling along the last dimension, each value on 1 to 512 neighbouring positions
- token_rank: int32 [16, 1024], P('dp'), may hold values from 1 to 1023
- source_segment: int32 [16, 1536], P('dp'), may hold values from 0 to 7, never falling along the last dimension, each value on 1 to 768 neighbouring positions
- query_map: bfloat16 [512, 512], P('dp', 'tensor'), may hold values from -0.25 to 0.25
- key_map: bfloat16 [512, 512], P('dp', 'tensor'), may hold values from -0.25 to 0.25
- value_map: bfloat16 [512, 512], P('dp', 'tensor'), may hold values from -0.25 to 0.25
- merge_map: bfloat16 [512, 512], P('dp', 'tensor'), may hold values from -1 to 1
- cross_query: bfloat16 [512, 512], P('dp', 'tensor'), may hold values from -0.25 to 0.25
- cross_key: bfloat16 [512, 512], P('dp', 'tensor'), may hold values from -0.25 to 0.25
- cross_value: bfloat16 [512, 512], P('dp', 'tensor'), may hold values from -0.25 to 0.25
- cross_merge: bfloat16 [512, 512], P('dp', 'tensor'), may hold values from -1.5 to 1.5
- expand_map: bfloat16 [512, 2048], P('dp', 'tensor'), may hold values from -0.25 to 0.25
- reduce_map: bfloat16 [512, 2048], P('dp', 'tensor'), may hold values from -0.1875 to 0.1875
- expand_bias: bfloat16 [2048], replicated, may hold values from -1.5 to 1.5
- reduce_bias: bfloat16 [512], replicated, may hold values from -1 to 1
- gain_first: bfloat16 [512], replicated, may hold values from 0.5 to 1.5
- bias_first: bfloat16 [512], replicated, may hold values from -1 to 1
- gain_second: bfloat16 [512], replicated, may hold values from 0.5 to 1.5
- bias_second: bfloat16 [512], replicated, may hold values from -1 to 1
- gain_third: bfloat16 [512], replicated, may hold values from 0.5 to 1.5
- bias_third: bfloat16 [512], replicated, may hold values from -1 to 1
- cotangent: bfloat16 [16384, 512], P(('dp', 'tensor')), may hold values from -6 to 6
Outputs:
- hidden_states: bfloat16 [16384, 512], P(('dp', 'tensor'))
- grad_query_stream: bfloat16 [16384, 512], P(('dp', 'tensor'))
- grad_token_stream: bfloat16 [16384, 512], P(('dp', 'tensor'))
- grad_encoder: bfloat16 [24576, 512], P(('dp', 'tensor'))
- grad_query_map: float32 [512, 512], P('dp', 'tensor')
- grad_key_map: float32 [512, 512], P('dp', 'tensor')
- grad_value_map: float32 [512, 512], P('dp', 'tensor')
- grad_merge_map: float32 [512, 512], P('dp', 'tensor')
- grad_cross_query: float32 [512, 512], P('dp', 'tensor')
- grad_cross_key: float32 [512, 512], P('dp', 'tensor')
- grad_cross_value: float32 [512, 512], P('dp', 'tensor')
- grad_cross_merge: float32 [512, 512], P('dp', 'tensor')
- grad_expand_map: float32 [512, 2048], P('dp', 'tensor')
- grad_reduce_map: float32 [512, 2048], P('dp', 'tensor')
- grad_expand_bias: float32 [2048], replicated
- grad_reduce_bias: float32 [512], replicated
- grad_gain_first: float32 [512], replicated
- grad_bias_first: float32 [512], replicated
- grad_gain_second: float32 [512], replicated
- grad_bias_second: float32 [512], replicated
- grad_gain_third: float32 [512], replicated
- grad_bias_third: float32 [512], replicated
The draws below stay inside these ranges and needn't reach their ends.
Inputs may be any that keep to these rules, and one draw needn't show every extreme that they name: token_segment never falls along a sequence; every number of 0 to 7 occurs in every sequence; a document has at most 512 tokens. source_segment never falls along a sequence; every number of 0 to 7 occurs in every sequence; a document has at most 768 encoder states.
All inputs are finite; a program needn't handle non-finite values.
Results may differ from the reference program's by a relative error of at most 0.035.
Values may be sent and summed in bfloat16 or wider, within the bound.
No kernel may reach another device: no remote copies, remote signals or barrier semaphores. Data moves between devices by JAX's collectives and lax.ppermute only.
A program may use at most 128 MiB of HBM per device.

```python
import math
import jax
import jax.numpy as jnp
import numpy as np
from jax import lax

D = 512
HEADS = 8
HEAD_DIM = 64
FF = 2048
LEN = 1024
ELEN = 1536
DOCS = 8
SEQS = 16
TOKENS = 16384
SOURCE_TOKENS = 24576
MOST = 512
SOURCE_MOST = 768


def place_ends(result, rng, low, top_value):
    spot = [jax.random.randint(jax.random.fold_in(rng, axis), (), 0, length) for axis, length in enumerate(result.shape)]
    longest = result.shape.index(max(result.shape))
    neighbour = spot[:longest] + [(spot[longest] + 1) % result.shape[longest]] + spot[longest + 1:]
    return result.at[tuple(spot)].set(low).at[tuple(neighbour)].set(top_value)


def raised(entries, rng, source, target, shards_of, factor):
    def block_of(dim):
        return (jnp.arange(entries.shape[dim]) // (entries.shape[dim] // shards_of)).reshape((-1,) + (1,) * (entries.ndim - 1 - dim))

    one_side = jax.random.permutation(rng, shards_of)[block_of(target)]
    far = (block_of(target) + shards_of // 2) % shards_of
    return jnp.where((block_of(source) == one_side) | (block_of(source) == far), factor * entries, entries)


def level_of(stream_key, shape, cuts, least, largest):
    def one(position, blocks):
        heights = jax.random.uniform(jax.random.fold_in(jax.random.fold_in(stream_key, 6), position), (blocks,), jnp.float32, least / len(cuts), largest / len(cuts))
        return jnp.repeat(jnp.exp(heights), shape[position] // blocks).reshape((-1,) + (1,) * (len(shape) - position - 1))

    gain = one(*cuts[0])
    for cut in cuts[1:]:
        gain = gain * one(*cut)
    return gain


def length_profile(amount, total, limit, lean):
    loads = [(1 << 20) // math.isqrt(grade ** lean) + 1 for grade in range(2, amount + 1)]
    surplus, given = total - limit - (amount - 1), [1] * (amount - 1)
    while surplus > 0:
        candidates = [i for i in range(amount - 1) if given[i] < limit]
        pool, remaining = sum([loads[i] for i in candidates]), surplus
        for i in candidates:
            more = min(limit - given[i], max(1, remaining * loads[i] // pool), surplus)
            given[i] = given[i] + more
            surplus = surplus - more
    return np.array([limit] + given)


def ragged(rng, amount, total, reach, slope):
    if amount == 2:
        one = jax.random.randint(rng, (), max(1, total - reach), min(reach, total - 1) + 1)
        return jnp.stack([one, total - one])
    sizes = jnp.asarray(length_profile(amount, total, reach, slope), jnp.int32)
    couples = (amount - 1) // 2
    giver, sink = sizes[1:1 + 2 * couples:2], sizes[2:2 + 2 * couples:2]
    slack = jnp.minimum(giver - 1, reach - sink)
    shifted = jax.random.randint(jax.random.fold_in(rng, 1), (couples,), 0, 1 << 20) % (slack + 1)
    sizes = sizes.at[1:1 + 2 * couples:2].set(giver - shifted).at[2:2 + 2 * couples:2].set(sink + shifted)
    return sizes[jax.random.permutation(jax.random.fold_in(rng, 2), amount)]


def scatter_about(own_key, dims, scale, reach, shards=(), held_as=jnp.bfloat16):
    array = scale * jax.random.normal(own_key, dims, jnp.float32)
    if shards:
        array = array * level_of(own_key, dims, shards, -0.22, 0.18)
    return jnp.clip(array, -reach, reach).astype(held_as)


def gaussian_with(rng, dims, width, most, shards, heavy, held_as=jnp.bfloat16):
    array = width * jax.random.normal(rng, dims, jnp.float32)
    if shards:
        array = array * level_of(rng, dims, shards, -0.22, 0.18)
    return jnp.clip(raised(array, jax.random.fold_in(rng, 3), *heavy), -most, most).astype(held_as)


def setup_inputs(seed: int = 0) -> dict:
    seeds = jax.random.split(jax.random.key(seed), 26)
    return {
        "query_stream": gaussian_with(seeds[0], (TOKENS, D), 1.0, 6.0, ((0, 32),), (0, 1, 32, 2.75)),
        "token_stream": gaussian_with(seeds[1], (TOKENS, D), 1.0, 6.0, ((0, 32),), (0, 1, 32, 2.75)),
        "encoder_states": scatter_about(seeds[2], (SOURCE_TOKENS, D), 1.0, 6.0, ((0, 32),)),
        "token_segment": jax.vmap(lambda own: jnp.searchsorted(jnp.cumsum(ragged(own, DOCS, LEN, MOST, 2)), jnp.arange(LEN), side="right"))(jax.random.split(seeds[3], SEQS)).reshape((SEQS, LEN)).astype(jnp.int32),
        "token_rank": place_ends(jax.random.randint(seeds[4], (SEQS, LEN), 1, LEN), jax.random.fold_in(seeds[4], 1), 1, LEN - 1).astype(jnp.int32),
        "source_segment": jax.vmap(lambda own: jnp.searchsorted(jnp.cumsum(ragged(own, DOCS, ELEN, SOURCE_MOST, 2)), jnp.arange(ELEN), side="right"))(jax.random.split(seeds[5], SEQS)).reshape((SEQS, ELEN)).astype(jnp.int32),
        "query_map": scatter_about(seeds[6], (D, D), D ** -0.5, 0.25, ((0, 8), (1, 4))),
        "key_map": scatter_about(seeds[7], (D, D), D ** -0.5, 0.25, ((0, 8), (1, 4))),
        "value_map": scatter_about(seeds[8], (D, D), D ** -0.5, 0.25, ((0, 8), (1, 4))),
        "merge_map": scatter_about(seeds[9], (D, D), (max(D // 16, D * 32 // LEN)) ** -0.5, 1.0, ((0, 8), (1, 4))),
        "cross_query": scatter_about(seeds[10], (D, D), D ** -0.5, 0.25, ((0, 8), (1, 4))),
        "cross_key": scatter_about(seeds[11], (D, D), D ** -0.5, 0.25, ((0, 8), (1, 4))),
        "cross_value": scatter_about(seeds[12], (D, D), D ** -0.5, 0.25, ((0, 8), (1, 4))),
        "cross_merge": scatter_about(seeds[13], (D, D), (max(D // 32, D * 48 // ELEN)) ** -0.5, 1.5, ((0, 8), (1, 4))),
        "expand_map": scatter_about(seeds[14], (D, FF), D ** -0.5, 0.25, ((0, 8), (1, 4))),
        "reduce_map": scatter_about(seeds[15], (D, FF), (FF // 2) ** -0.5, 0.1875, ((0, 8), (1, 4))),
        "expand_bias": scatter_about(seeds[16], (FF,), 0.3, 1.5),
        "reduce_bias": scatter_about(seeds[17], (D,), 0.2, 1.0),
        "gain_first": jnp.clip(1.0 + 0.1 * jax.random.normal(seeds[18], (D,), jnp.float32), 0.5, 1.5).astype(jnp.bfloat16),
        "bias_first": scatter_about(seeds[19], (D,), 0.2, 1.0),
        "gain_second": jnp.clip(1.0 + 0.1 * jax.random.normal(seeds[20], (D,), jnp.float32), 0.5, 1.5).astype(jnp.bfloat16),
        "bias_second": scatter_about(seeds[21], (D,), 0.2, 1.0),
        "gain_third": jnp.clip(1.0 + 0.1 * jax.random.normal(seeds[22], (D,), jnp.float32), 0.5, 1.5).astype(jnp.bfloat16),
        "bias_third": scatter_about(seeds[23], (D,), 0.2, 1.0),
        "cotangent": gaussian_with(seeds[24], (TOKENS, D), 1.0, 6.0, ((0, 32),), (0, 1, 32, 2.75)),
    }


@jax.custom_vjp
def low(v):
    return lax.optimization_barrier(v.astype(jnp.bfloat16)).astype(jnp.float32)

@jax.custom_vjp
def low_back(v):
    return v

def low_keep(v):
    return (low(v), None)

def low_pass(kept, grad):
    return (grad,)

def back_keep(v):
    return (v, None)

def back_low(kept, grad):
    return (low(grad),)
low.defvjp(low_keep, low_pass)
low_back.defvjp(back_keep, back_low)

def product(left_side, right_side):
    return jnp.dot(left_side, right_side, precision=lax.Precision.HIGHEST, preferred_element_type=jnp.float32)

def product_back(left_side, right_side):
    return lax.dot_general(left_side, right_side, (((1,), (1,)), ((), ())), precision=lax.Precision.HIGHEST, preferred_element_type=jnp.float32)

def smooth_gate(values):
    return 0.5 * values * (1.0 + jnp.tanh(0.7978845608028654 * (values + 0.044715 * values * values * values)))

def layer_norm(matrix, gains, offset):
    average = lax.optimization_barrier(jnp.mean(matrix, -1, keepdims=True))
    centred = matrix - average
    inverse = lax.rsqrt(lax.optimization_barrier(jnp.mean(centred * centred, -1, keepdims=True)) + 1e-05)
    return centred * inverse * gains + offset

def attend(queries, key_rows, values, allowed):
    query_heads = queries.reshape(queries.shape[0], HEADS, HEAD_DIM)
    key_heads = key_rows.reshape(key_rows.shape[0], HEADS, HEAD_DIM)
    value_heads = values.reshape(values.shape[0], HEADS, HEAD_DIM)
    scores = jnp.einsum('lhd,ehd->hle', query_heads, key_heads, precision=lax.Precision.HIGHEST) * 0.125
    scores = low_back(scores)
    scores = jnp.where(allowed[None], scores, -1e+30)
    peak = lax.optimization_barrier(jnp.max(scores, -1, keepdims=True))
    powers = jnp.exp(scores - peak)
    weights = low(powers / lax.optimization_barrier(jnp.sum(powers, -1, keepdims=True)))
    mixture = jnp.einsum('hle,ehd->lhd', weights, value_heads, precision=lax.Precision.HIGHEST)
    return low_back(low(mixture.reshape(queries.shape[0], HEADS * HEAD_DIM)))

def self_block(pieces):
    queries, key_rows, values, segment, ranking = pieces
    starts = jnp.concatenate([jnp.ones((1,), jnp.bool_), segment[1:] != segment[:-1]])
    allowed = (segment[:, None] == segment[None, :]) & ((ranking[None, :] < ranking[:, None]) | starts[None, :])
    return attend(queries, key_rows, values, allowed)

def cross_block(pieces):
    queries, key_rows, values, segment, source = pieces
    allowed = segment[:, None] == source[None, :]
    return attend(queries, key_rows, values, allowed)

def reference(query_stream, token_stream, encoder_states, token_segment, token_rank, source_segment, query_map, key_map, value_map, merge_map, cross_query, cross_key, cross_value, cross_merge, expand_map, reduce_map, expand_bias, reduce_bias, gain_first, bias_first, gain_second, bias_second, gain_third, bias_third, cotangent):

    def layer(query_in, token_in, source_in, query_w, key_w, value_w, merge_w, cquery_w, ckey_w, cvalue_w, cmerge_w, expand_w, reduce_w, expand_b, reduce_b, gain_one, offset_one, gain_two, offset_two, gain_three, offset_three):
        queries = low_back(low(product(query_in, query_w)))
        key_rows = low_back(low(product(token_in, key_w)))
        values = low_back(low(product(token_in, value_w)))
        mixture = lax.map(jax.checkpoint(self_block), (queries.reshape(SEQS, LEN, D), key_rows.reshape(SEQS, LEN, D), values.reshape(SEQS, LEN, D), token_segment, token_rank)).reshape(TOKENS, D)
        first_out = layer_norm(query_in + low_back(product_back(mixture, merge_w)), gain_one, offset_one)
        cross_rows = low_back(low(product(low(first_out), cquery_w)))
        source_keys = low_back(low(product(source_in, ckey_w)))
        source_values = low_back(low(product(source_in, cvalue_w)))
        cross_mix = lax.map(jax.checkpoint(cross_block), (cross_rows.reshape(SEQS, LEN, D), source_keys.reshape(SEQS, ELEN, D), source_values.reshape(SEQS, ELEN, D), token_segment, source_segment)).reshape(TOKENS, D)
        second_out = layer_norm(first_out + low_back(product_back(cross_mix, cmerge_w)), gain_two, offset_two)
        hidden_pre = low_back(product(low(second_out), expand_w) + expand_b)
        active = low(smooth_gate(hidden_pre))
        return layer_norm(second_out + low_back(product_back(active, reduce_w) + reduce_b), gain_three, offset_three)
    floats = tuple((argument.astype(jnp.float32) for argument in (query_stream, token_stream, encoder_states, query_map, key_map, value_map, merge_map, cross_query, cross_key, cross_value, cross_merge, expand_map, reduce_map, expand_bias, reduce_bias, gain_first, bias_first, gain_second, bias_second, gain_third, bias_third)))
    hidden, pullback = jax.vjp(layer, *floats)
    gradients = pullback(cotangent.astype(jnp.float32))
    return (hidden.astype(jnp.bfloat16), gradients[0].astype(jnp.bfloat16), gradients[1].astype(jnp.bfloat16), gradients[2].astype(jnp.bfloat16), gradients[3], gradients[4], gradients[5], gradients[6], gradients[7], gradients[8], gradients[9], gradients[10], gradients[11], gradients[12], gradients[13], gradients[14], gradients[15], gradients[16], gradients[17], gradients[18], gradients[19], gradients[20])
```

```python
import jax
import jax.numpy as jnp
from jax import lax
from jax.sharding import PartitionSpec as P
from jax.experimental import pallas as pl
from jax.experimental.pallas import tpu as pltpu

HEAD_DIM = 64
EPSILON = 1e-05
GATE = 0.7978845608028654
CUBIC = 0.044715
UNIT = 128
BOTH = ("dp", "tensor")


def smooth_gate(values):
    return (
        0.5
        * values
        * (1.0 + jnp.tanh(GATE * (values + CUBIC * values * values * values)))
    )


def gate_slope(values):
    bent = jnp.tanh(GATE * (values + CUBIC * values * values * values))
    return 0.5 * (1.0 + bent) + 0.5 * values * (1.0 - bent * bent) * GATE * (
        1.0 + 3.0 * CUBIC * values * values
    )


def norm_rows(matrix, gains, offset):
    average = jnp.mean(matrix, -1, keepdims=True)
    centred = matrix - average
    inverse = lax.rsqrt(jnp.mean(centred * centred, -1, keepdims=True) + EPSILON)
    normed = centred * inverse
    return (normed * gains + offset, normed, inverse)


def norm_back(outer_grad, normed, inverse, gains):
    spread = outer_grad * gains
    inner_grad = inverse * (
        spread
        - jnp.mean(spread, -1, keepdims=True)
        - normed * jnp.mean(spread * normed, -1, keepdims=True)
    )
    return (inner_grad, jnp.sum(outer_grad * normed, 0), jnp.sum(outer_grad, 0))


def mul(left_side, right_side):
    return jnp.dot(left_side, right_side, preferred_element_type=jnp.float32)


def contract_last(left_side, right_side):
    return lax.dot_general(
        left_side, right_side, (((1,), (1,)), ((), ())), preferred_element_type=jnp.float32
    )


def contract_first(left_side, right_side):
    return lax.dot_general(
        left_side, right_side, (((0,), (0,)), ((), ())), preferred_element_type=jnp.float32
    )


def head_view(matrix):
    return matrix.reshape(matrix.shape[0], -1, HEAD_DIM)


def flatten(matrix):
    return matrix.reshape(matrix.shape[0], -1).astype(jnp.bfloat16)


def masked_scores(queries, key_rows, allowed):
    scores = (
        jnp.einsum(
            "lhd,ehd->hle",
            head_view(queries),
            head_view(key_rows),
            preferred_element_type=jnp.float32,
        )
        * 0.125
    )
    return jnp.where(allowed[None], scores, -1e30)


def attend(queries, key_rows, values, allowed):
    scores = masked_scores(queries, key_rows, allowed)
    peak = jnp.max(scores, -1, keepdims=True)
    powers = jnp.exp(scores - peak)
    row_total = jnp.sum(powers, -1, keepdims=True)
    weights = (powers / row_total).astype(jnp.bfloat16)
    mixture = jnp.einsum(
        "hle,ehd->lhd", weights, head_view(values), preferred_element_type=jnp.float32
    )
    return (flatten(mixture), (peak + jnp.log(row_total))[..., 0])


def attend_back(queries, key_rows, values, allowed, log_total, mixture_grad):
    scores = masked_scores(queries, key_rows, allowed)
    weights = jnp.exp(scores - log_total[..., None])
    outer_grad = head_view(mixture_grad)
    value_grad = jnp.einsum(
        "hle,lhd->ehd", weights.astype(jnp.bfloat16), outer_grad, preferred_element_type=jnp.float32
    )
    weight_grad = jnp.einsum(
        "lhd,ehd->hle", outer_grad, head_view(values), preferred_element_type=jnp.float32
    )
    score_grad = (
        weights * (weight_grad - jnp.sum(weights * weight_grad, -1, keepdims=True))
    ).astype(jnp.bfloat16)
    query_grad = (
        jnp.einsum(
            "hle,ehd->lhd", score_grad, head_view(key_rows), preferred_element_type=jnp.float32
        )
        * 0.125
    )
    key_grad = (
        jnp.einsum(
            "hle,lhd->ehd", score_grad, head_view(queries), preferred_element_type=jnp.float32
        )
        * 0.125
    )
    return (flatten(query_grad), flatten(key_grad), flatten(value_grad))


def over_dp(matrix, flip, size):
    return lax.ppermute(matrix, "dp", [(i, i ^ flip) for i in range(size)])


def over_tensor(matrix, flip, size):
    return lax.ppermute(matrix, "tensor", [(i, i ^ flip) for i in range(size)])


def units_of(block):
    rows, columns = block.shape
    return block.reshape(rows, columns // UNIT, UNIT).transpose(1, 0, 2)


def place_kernel(counts, spots_ref, *refs):
    n = len(counts)
    pieces, outs = refs[:-n], refs[-n:]
    me_dp, me_t = spots_ref[0], spots_ref[1]
    rows = pieces[0].shape[2]
    at = 0
    for piece, (dp_flips, t_flips) in zip(pieces, PIECES):
        for a, dp_flip in enumerate(dp_flips):
            d = jnp.bitwise_xor(me_dp, dp_flip)
            row = pl.multiple_of(d * rows, rows)
            for b, t_flip in enumerate(t_flips):
                t = jnp.bitwise_xor(me_t, t_flip)
                unit = 0
                for out, count in zip(outs, counts):
                    for k in range(count):
                        column = pl.multiple_of((t * count + k) * UNIT, UNIT)
                        out[pl.ds(row, rows), pl.ds(column, UNIT)] = piece[
                            a * len(t_flips) + b, unit
                        ]
                        unit += 1


PIECES = (
    ((0,), (0, 1, 2, 3)),
    ((2,), (0, 1, 2, 3)),
    ((4,), (0, 1, 2, 3)),
    ((6,), (0, 1)),
    ((6,), (2, 3)),
    ((1,), (0, 1, 2, 3)),
    ((3,), (0, 1, 2, 3)),
    ((5,), (0, 1, 2, 3)),
    ((7,), (0, 1)),
    ((7,), (2, 3)),
)


def gather_weights(blocks, spots):
    counts = [block.shape[1] // UNIT for block in blocks]
    rows = blocks[0].shape[0]
    own = jnp.concatenate([units_of(block) for block in blocks], 0)
    line = jnp.stack([own] + [over_tensor(own, flip, 4) for flip in (1, 2, 3)])
    along_x = over_dp(line, 2, 8)
    along_y = over_dp(line, 4, 8)
    far_low = over_dp(along_x[:2], 4, 8)
    far_high = over_dp(along_y[2:], 2, 8)
    near = [line, along_x, along_y, far_low, far_high]
    pieces = near + [over_dp(piece, 1, 8) for piece in near]
    return pl.pallas_call(
        lambda *refs: place_kernel(counts, *refs),
        out_shape=[
            jax.ShapeDtypeStruct((8 * rows, 4 * count * UNIT), jnp.bfloat16) for count in counts
        ],
        in_specs=[pl.BlockSpec(memory_space=pltpu.SMEM)]
        + [pl.BlockSpec(memory_space=pltpu.VMEM)] * len(pieces),
        out_specs=[pl.BlockSpec(memory_space=pltpu.VMEM)] * len(blocks),
        compiler_params=pltpu.CompilerParams(vmem_limit_bytes=32 * 1024 * 1024),
    )(spots, *pieces)


def gather_plain(blocks, spots):
    return [
        lax.all_gather(
            lax.all_gather(block, "dp", axis=0, tiled=True), "tensor", axis=1, tiled=True
        )
        for block in blocks
    ]


def pick(array, index, axis):
    return lax.dynamic_index_in_dim(array, index, axis, keepdims=False)


def reduce_weights(grads):
    counts = [grad.shape[1] // (4 * UNIT) for grad in grads]
    rows = grads[0].shape[0] // 8
    full = jnp.concatenate(
        [
            grad.astype(jnp.bfloat16)
            .reshape(2, 2, 2, rows, 4, count, UNIT)
            .transpose(0, 1, 2, 4, 5, 3, 6)
            for grad, count in zip(grads, counts)
        ],
        4,
    )
    me_dp, me_t = lax.axis_index("dp"), lax.axis_index("tensor")
    core, x, y = me_dp % 2, (me_dp // 2) % 2, me_dp // 4
    low = jnp.bfloat16
    kept = pick(full, core, 2).astype(jnp.float32) + over_dp(pick(full, 1 - core, 2), 1, 8)
    low_half, high_half = kept[:, :, :2], kept[:, :, 2:]
    low_half = pick(low_half, x, 1) + over_dp(pick(low_half, 1 - x, 1).astype(low), 2, 8)
    high_half = pick(high_half, y, 0) + over_dp(pick(high_half, 1 - y, 0).astype(low), 4, 8)
    low_half = pick(low_half, y, 0) + over_dp(pick(low_half, 1 - y, 0).astype(low), 4, 8)
    high_half = pick(high_half, x, 0) + over_dp(pick(high_half, 1 - x, 0).astype(low), 2, 8)
    kept = jnp.concatenate([low_half, high_half], 0)
    total = pick(kept, me_t, 0)
    for flip in (1, 2, 3):
        total = total + over_tensor(pick(kept, me_t ^ flip, 0).astype(low), flip, 4)
    results, at = [], 0
    for count in counts:
        part = total[at : at + count]
        results.append(part.transpose(1, 0, 2).reshape(rows, count * UNIT))
        at += count
    return results


def reduce_plain(grads):
    return [
        lax.psum_scatter(
            lax.psum_scatter(grad, "dp", scatter_dimension=0, tiled=True),
            "tensor",
            scatter_dimension=1,
            tiled=True,
        )
        for grad in grads
    ]


def sum_small(terms):
    sizes = [term.shape[0] for term in terms]
    packed = jnp.concatenate(terms).reshape(-1, UNIT)
    for flip in (1, 2, 4):
        packed = packed + over_dp(packed, flip, 8)
    packed = packed + over_tensor(packed, 1, 4)
    packed = packed + over_tensor(packed, 2, 4)
    packed = packed.reshape(-1)
    results, at = [], 0
    for size in sizes:
        results.append(packed[at : at + size])
        at += size
    return results


def body(
    query_stream,
    token_stream,
    encoder_states,
    token_segment,
    token_rank,
    source_segment,
    query_map,
    key_map,
    value_map,
    merge_map,
    cross_query,
    cross_key,
    cross_value,
    cross_merge,
    expand_map,
    reduce_map,
    expand_bias,
    reduce_bias,
    gain_first,
    bias_first,
    gain_second,
    bias_second,
    gain_third,
    bias_third,
    cotangent,
    fast,
    tensor_size,
):
    low = jnp.bfloat16
    gather = gather_weights if fast else gather_plain
    reduce = reduce_weights if fast else reduce_plain
    rows, source_count = query_stream.shape[0], encoder_states.shape[0]
    me_dp, me_t = lax.axis_index("dp"), lax.axis_index("tensor")
    spots = jnp.stack([me_dp, me_t]).astype(jnp.int32)
    sequence, half = me_t // 2, me_t % 2

    other_tokens = over_tensor(token_stream, 1, tensor_size)
    w_query, w_key, w_value = gather([query_map, key_map, value_map], spots)
    other_source = over_tensor(encoder_states, 1, tensor_size)
    w_merge, w_cquery, w_ckey, w_cvalue = gather(
        [merge_map, cross_query, cross_key, cross_value], spots
    )
    w_cmerge, w_expand = gather([cross_merge, expand_map], spots)
    (w_reduce,) = gather([reduce_map], spots)

    def halves(row, size):
        return lax.dynamic_slice_in_dim(row, half * size, size), lax.dynamic_slice_in_dim(
            row, (1 - half) * size, size
        )

    segment_row = pick(token_segment, sequence, 0)
    starts_row = jnp.concatenate([jnp.ones((1,), jnp.bool_), segment_row[1:] != segment_row[:-1]])
    own_segment, far_segment = halves(segment_row, rows)
    own_rank, far_rank = halves(pick(token_rank, sequence, 0), rows)
    key_segment = jnp.concatenate([own_segment, far_segment])
    key_rank = jnp.concatenate([own_rank, far_rank])
    key_start = jnp.concatenate(halves(starts_row, rows))
    source_row = jnp.concatenate(halves(pick(source_segment, sequence, 0), source_count))
    self_allowed = (own_segment[:, None] == key_segment[None, :]) & (
        (key_rank[None, :] < own_rank[:, None]) | key_start[None, :]
    )
    cross_allowed = own_segment[:, None] == source_row[None, :]

    gains_one, gains_two, gains_three = (
        gain.astype(jnp.float32) for gain in (gain_first, gain_second, gain_third)
    )
    offset_one, offset_two, offset_three = (
        bias.astype(jnp.float32) for bias in (bias_first, bias_second, bias_third)
    )

    token_rows = jnp.concatenate([token_stream, other_tokens], 0)
    source_rows = jnp.concatenate([encoder_states, other_source], 0)
    queries = mul(query_stream, w_query).astype(low)
    key_rows = mul(token_rows, w_key).astype(low)
    values = mul(token_rows, w_value).astype(low)
    mixture, self_total = attend(queries, key_rows, values, self_allowed)
    first_out, first_normed, first_inverse = norm_rows(
        query_stream.astype(jnp.float32) + contract_last(mixture, w_merge), gains_one, offset_one
    )
    first_low = first_out.astype(low)
    cross_rows = mul(first_low, w_cquery).astype(low)
    source_keys = mul(source_rows, w_ckey).astype(low)
    source_values = mul(source_rows, w_cvalue).astype(low)
    cross_mix, cross_total = attend(cross_rows, source_keys, source_values, cross_allowed)
    second_out, second_normed, second_inverse = norm_rows(
        first_out + contract_last(cross_mix, w_cmerge), gains_two, offset_two
    )
    second_low = second_out.astype(low)
    hidden_pre = mul(second_low, w_expand) + expand_bias.astype(jnp.float32)
    active = smooth_gate(hidden_pre).astype(low)
    third_out, third_normed, third_inverse = norm_rows(
        second_out + contract_last(active, w_reduce) + reduce_bias.astype(jnp.float32),
        gains_three,
        offset_three,
    )
    hidden_states = third_out.astype(low)

    third_grad, gain_third_grad, bias_third_grad = norm_back(
        cotangent.astype(jnp.float32), third_normed, third_inverse, gains_three
    )
    output_grad = third_grad.astype(low)
    reduce_bias_grad = jnp.sum(output_grad.astype(jnp.float32), 0)
    reduce_grad = contract_first(output_grad, active)
    (reduce_sum,) = reduce([reduce_grad])
    pre_grad = (mul(output_grad, w_reduce) * gate_slope(hidden_pre)).astype(low)
    expand_bias_grad = jnp.sum(pre_grad.astype(jnp.float32), 0)
    expand_grad = contract_first(second_low, pre_grad)
    (expand_sum,) = reduce([expand_grad])
    second_grad = third_grad + contract_last(pre_grad, w_expand)
    second_in_grad, gain_second_grad, bias_second_grad = norm_back(
        second_grad, second_normed, second_inverse, gains_two
    )
    cross_out = second_in_grad.astype(low)
    cross_merge_grad = contract_first(cross_out, cross_mix)
    cross_mix_grad = mul(cross_out, w_cmerge).astype(low)
    cross_rows_grad, source_keys_grad, source_values_grad = attend_back(
        cross_rows, source_keys, source_values, cross_allowed, cross_total, cross_mix_grad
    )
    source_part = contract_last(source_keys_grad, w_ckey) + contract_last(
        source_values_grad, w_cvalue
    )
    source_back = over_tensor(source_part[source_count:].astype(low), 1, tensor_size)
    cross_query_grad = contract_first(first_low, cross_rows_grad)
    cross_key_grad = contract_first(source_rows, source_keys_grad)
    cross_value_grad = contract_first(source_rows, source_values_grad)
    cross_sums = reduce([cross_query_grad, cross_key_grad, cross_value_grad, cross_merge_grad])
    first_grad = second_in_grad + contract_last(cross_rows_grad, w_cquery)
    stream_grad, gain_first_grad, bias_first_grad = norm_back(
        first_grad, first_normed, first_inverse, gains_one
    )
    self_out = stream_grad.astype(low)
    merge_grad = contract_first(self_out, mixture)
    (merge_sum,) = reduce([merge_grad])
    small_terms = (
        expand_bias_grad,
        reduce_bias_grad,
        gain_first_grad,
        bias_first_grad,
        gain_second_grad,
        bias_second_grad,
        gain_third_grad,
        bias_third_grad,
    )
    small = sum_small(small_terms) if fast else lax.psum(small_terms, BOTH)
    mixture_grad = mul(self_out, w_merge).astype(low)
    queries_grad, keys_grad, values_grad = attend_back(
        queries, key_rows, values, self_allowed, self_total, mixture_grad
    )
    token_part = contract_last(keys_grad, w_key) + contract_last(values_grad, w_value)
    token_back = over_tensor(token_part[rows:].astype(low), 1, tensor_size)
    self_sums = reduce(
        [
            contract_first(query_stream, queries_grad),
            contract_first(token_rows, keys_grad),
            contract_first(token_rows, values_grad),
        ]
    )
    return (
        hidden_states,
        (stream_grad + contract_last(queries_grad, w_query)).astype(low),
        (token_part[:rows] + token_back).astype(low),
        (source_part[:source_count] + source_back).astype(low),
        self_sums[0],
        self_sums[1],
        self_sums[2],
        merge_sum,
        cross_sums[0],
        cross_sums[1],
        cross_sums[2],
        cross_sums[3],
        expand_sum,
        reduce_sum,
        *small,
    )


def solution(mesh):
    fast = mesh.shape["dp"] == 8 and mesh.shape["tensor"] == 4
    rows = P(BOTH, None)
    block = P("dp", "tensor")

    def program(*arguments):
        return body(*arguments, fast, mesh.shape["tensor"])

    return jax.shard_map(
        program,
        mesh=mesh,
        in_specs=(rows,) * 3 + (P("dp", None),) * 3 + (block,) * 10 + (P(),) * 8 + (rows,),
        out_specs=(rows,) * 4 + (block,) * 10 + (P(),) * 8,
        check_vma=False,
    )
```

```python
import functools

import jax
import jax.numpy as jnp
from jax import lax
from jax.sharding import PartitionSpec as P
from jax.experimental import pallas as pl
from jax.experimental.pallas import tpu as pltpu

EPSILON = 1e-05
GATE = 0.7978845608028654
CUBIC = 0.044715
LOG2E = 1.4426950408889634
UNIT = 128
PAIR = 128
SELF_TILE = (512, 256)
CROSS_TILE = (256, 256)
BOTH = ("dp", "tensor")
ANY = pl.BlockSpec(memory_space=pl.ANY)
WHOLE = pl.BlockSpec(memory_space=pltpu.VMEM)
SCALARS = pl.BlockSpec(memory_space=pltpu.SMEM)
LOW = jnp.bfloat16


def params(mib):
    return pltpu.CompilerParams(vmem_limit_bytes=mib * 1024 * 1024)


def lasting(us):
    return pl.CostEstimate(flops=int(us * 1.1e9), bytes_accessed=0, transcendentals=0)


def smooth_gate(values):
    return (
        0.5
        * values
        * (1.0 + jnp.tanh(GATE * (values + CUBIC * values * values * values)))
    )


def gate_slope(values):
    bent = jnp.tanh(GATE * (values + CUBIC * values * values * values))
    return 0.5 * (1.0 + bent) + 0.5 * values * (1.0 - bent * bent) * GATE * (
        1.0 + 3.0 * CUBIC * values * values
    )


def norm_rows(matrix, gains, offset):
    average = jnp.mean(matrix, -1, keepdims=True)
    centred = matrix - average
    inverse = lax.rsqrt(jnp.mean(centred * centred, -1, keepdims=True) + EPSILON)
    normed = centred * inverse
    return (normed * gains + offset, normed, inverse)


def norm_back(outer_grad, normed, inverse, gains):
    spread = outer_grad * gains
    inner_grad = inverse * (
        spread
        - jnp.mean(spread, -1, keepdims=True)
        - normed * jnp.mean(spread * normed, -1, keepdims=True)
    )
    return (inner_grad, jnp.sum(outer_grad * normed, 0), jnp.sum(outer_grad, 0))


def dot_nn(a, b):
    return lax.dot_general(a, b, (((1,), (0,)), ((), ())), preferred_element_type=jnp.float32)


def dot_nt(a, b):
    return lax.dot_general(a, b, (((1,), (1,)), ((), ())), preferred_element_type=jnp.float32)


def dot_tn(a, b):
    return lax.dot_general(a, b, (((0,), (0,)), ((), ())), preferred_element_type=jnp.float32)


def split_heads(rows):
    lane = lax.broadcasted_iota(jnp.int32, rows.shape, 1)
    zero = jnp.zeros_like(rows)
    return jnp.concatenate(
        [jnp.where(lane < PAIR // 2, rows, zero), jnp.where(lane < PAIR // 2, zero, rows)], 0
    )


def twice(row):
    return jnp.concatenate([row, row], 1)


def forward_kernel(
    near_ref, q_ref, k_ref, v_ref, bias_ref, *refs, tile_q, tile_k
):
    out_ref, lse_ref, turned, top, total, acc = refs[-6:]
    nq, nk = q_ref.shape[0] // tile_q, k_ref.shape[0] // tile_k
    half = PAIR // 2
    turned[...] = v_ref[...].T
    for i in range(nq):
        q_rows = slice(i * tile_q, (i + 1) * tile_q)
        stacked = split_heads(q_ref[q_rows])
        top[...] = jnp.full(top.shape, -3e30, jnp.float32)
        total[...] = jnp.zeros(total.shape, jnp.float32)
        acc[...] = jnp.zeros(acc.shape, jnp.float32)
        for j in range(nk):

            @pl.when(near_ref[i, j] != 0)
            def _(j=j, stacked=stacked, q_rows=q_rows):
                k_rows = slice(j * tile_k, (j + 1) * tile_k)
                scores = dot_nt(k_ref[k_rows], stacked) + twice(bias_ref[k_rows, q_rows])
                old = top[...]
                peak = jnp.maximum(old, jnp.max(scores, 0, keepdims=True))
                fade = jnp.exp2((old - peak) * LOG2E)
                powers = jnp.exp2((scores - peak) * LOG2E)
                top[...] = peak
                total[...] = total[...] * fade + jnp.sum(powers, 0, keepdims=True)
                acc[...] = acc[...] * fade + dot_nn(turned[:, k_rows], powers.astype(LOW))

        full = total[...]
        scaled = acc[...] * (1.0 / full)
        mixed = jnp.concatenate([scaled[:half, :tile_q], scaled[half:, tile_q:]], 0)
        out_ref[q_rows] = mixed.T.astype(LOW)
        log_total = top[...] * LOG2E + jnp.log2(full)
        lse_ref[0, 0:1, q_rows] = log_total[:, :tile_q]
        lse_ref[0, 1:2, q_rows] = log_total[:, tile_q:]


def attend_part(near, queries, key_rows, values, bias, tile, base, count, before, after, us):
    lq, width = queries.shape
    lk = key_rows.shape[0]
    tile_q, tile_k = tile
    column = lambda p: (0, p + base)
    before = list(before)
    extra = before + list(after)
    return pl.pallas_call(
        functools.partial(forward_kernel, tile_q=tile_q, tile_k=tile_k),
        grid=(count,),
        in_specs=[
            SCALARS,
            pl.BlockSpec((lq, PAIR), column),
            pl.BlockSpec((lk, PAIR), column),
            pl.BlockSpec((lk, PAIR), column),
            pl.BlockSpec((lk, lq), lambda p: (0, 0)),
        ]
        + [ANY] * len(extra),
        out_specs=[
            pl.BlockSpec((lq, PAIR), column),
            pl.BlockSpec((1, 2, lq), lambda p: (p + base, 0, 0)),
        ],
        out_shape=[
            jax.ShapeDtypeStruct((lq, width), LOW),
            jax.ShapeDtypeStruct((width // PAIR, 2, lq), jnp.float32),
        ],
        scratch_shapes=[
            pltpu.VMEM((PAIR, lk), LOW),
            pltpu.VMEM((1, 2 * tile_q), jnp.float32),
            pltpu.VMEM((1, 2 * tile_q), jnp.float32),
            pltpu.VMEM((PAIR, 2 * tile_q), jnp.float32),
        ],
        input_output_aliases={5: 0, 6: 1} if before else {},
        compiler_params=params(40),
        cost_estimate=lasting(us),
        name="attend",
    )(near, queries, key_rows, values, bias, *extra)


def backward_kernel(
    near_ref, q_ref, k_ref, v_ref, m_ref, o_ref, lse_ref, bias_ref, *refs, tile_q, tile_k
):
    dq_ref, dk_ref, dv_ref, dq_acc, dk_acc, dv_acc = refs[-6:]
    nq, nk = q_ref.shape[0] // tile_q, k_ref.shape[0] // tile_k
    half = PAIR // 2
    dk_acc[...] = jnp.zeros(dk_acc.shape, jnp.float32)
    dv_acc[...] = jnp.zeros(dv_acc.shape, jnp.float32)
    for i in range(nq):
        q_rows = slice(i * tile_q, (i + 1) * tile_q)
        stacked = split_heads(q_ref[q_rows])
        grads = split_heads(m_ref[q_rows])
        turned = (m_ref[q_rows].astype(jnp.float32) * o_ref[q_rows].astype(jnp.float32)).T
        delta = jnp.concatenate(
            [jnp.sum(turned[:half], 0, keepdims=True), jnp.sum(turned[half:], 0, keepdims=True)], 1
        )
        log_total = jnp.concatenate([lse_ref[0, 0:1, q_rows], lse_ref[0, 1:2, q_rows]], 1)
        dq_acc[...] = jnp.zeros(dq_acc.shape, jnp.float32)
        for j in range(nk):

            @pl.when(near_ref[i, j] != 0)
            def _(
                j=j, stacked=stacked, grads=grads, delta=delta, log_total=log_total, q_rows=q_rows
            ):
                k_rows = slice(j * tile_k, (j + 1) * tile_k)
                keys = k_ref[k_rows]
                scores = dot_nt(keys, stacked)
                weights = jnp.exp2(
                    scores * LOG2E + (twice(bias_ref[k_rows, q_rows]) - log_total)
                )
                outer = dot_nt(v_ref[k_rows], grads)
                slope = (weights * (outer - delta)).astype(LOW)
                dv_acc[k_rows] += dot_nn(weights.astype(LOW), grads)
                dk_acc[k_rows] += dot_nn(slope, stacked)
                dq_acc[...] += dot_tn(slope, keys)

        lane = lax.broadcasted_iota(jnp.int32, (tile_q, PAIR), 1)
        dq_ref[q_rows] = (
            jnp.where(lane < half, dq_acc[:tile_q], dq_acc[tile_q:]) * 0.125
        ).astype(LOW)
    dk_ref[...] = dk_acc[...].astype(LOW)
    dv_ref[...] = dv_acc[...].astype(LOW)


def attend_back_part(
    near, queries, key_rows, values, outer, mixed, lse, bias, tile, base, count, before, after, us
):
    lq, width = queries.shape
    lk = key_rows.shape[0]
    tile_q, tile_k = tile
    column = lambda p: (0, p + base)
    q_spec, k_spec = pl.BlockSpec((lq, PAIR), column), pl.BlockSpec((lk, PAIR), column)
    before = list(before)
    extra = before + list(after)
    return pl.pallas_call(
        functools.partial(backward_kernel, tile_q=tile_q, tile_k=tile_k),
        grid=(count,),
        in_specs=[
            SCALARS,
            q_spec,
            k_spec,
            k_spec,
            q_spec,
            q_spec,
            pl.BlockSpec((1, 2, lq), lambda p: (p + base, 0, 0)),
            pl.BlockSpec((lk, lq), lambda p: (0, 0)),
        ]
        + [ANY] * len(extra),
        out_specs=[q_spec, k_spec, k_spec],
        out_shape=[
            jax.ShapeDtypeStruct((lq, width), LOW),
            jax.ShapeDtypeStruct((lk, width), LOW),
            jax.ShapeDtypeStruct((lk, width), LOW),
        ],
        scratch_shapes=[
            pltpu.VMEM((2 * tile_q, PAIR), jnp.float32),
            pltpu.VMEM((lk, PAIR), jnp.float32),
            pltpu.VMEM((lk, PAIR), jnp.float32),
        ],
        input_output_aliases={8: 0, 9: 1, 10: 2} if before else {},
        compiler_params=params(40),
        cost_estimate=lasting(us),
        name="attend_back",
    )(near, queries, key_rows, values, outer, mixed, lse, bias, *extra)


def near_tiles(own, keys, tile):
    own, keys = own.reshape(-1, tile[0]), keys.reshape(-1, tile[1])
    return (
        (keys.min(1)[None] <= own.max(1)[:, None]) & (keys.max(1)[None] >= own.min(1)[:, None])
    ).astype(jnp.int32)


def over_dp(matrix, flip):
    return lax.ppermute(matrix, "dp", [(i, i ^ flip) for i in range(8)])


def over_tensor(matrix, flip):
    return lax.ppermute(matrix, "tensor", [(i, i ^ flip) for i in range(4)])


def ordered(value, *earlier):
    return lax.optimization_barrier((value, *earlier))[0]


SMALL_PIECES = (((0, 2, 4, 6), (0, 1, 2, 3)), ((1, 3, 5, 7), (0, 1, 2, 3)))
LARGE_PIECES = tuple(
    (tuple(flip + core for flip in flips), ts)
    for core in (0, 1)
    for flips, ts in (((0, 2, 4), (0, 1, 2, 3)), ((6,), (0, 1)), ((6,), (2, 3)))
)


def place_kernel(counts, layout, spots_ref, *refs):
    n = len(counts)
    pieces, outs = refs[:-n], refs[-n:]
    me_dp, me_t = spots_ref[0], spots_ref[1]
    rows = pieces[0].shape[2]
    for piece, (dp_flips, t_flips) in zip(pieces, layout):
        for a, dp_flip in enumerate(dp_flips):
            row = pl.multiple_of(jnp.bitwise_xor(me_dp, dp_flip) * rows, rows)
            for b, t_flip in enumerate(t_flips):
                t = jnp.bitwise_xor(me_t, t_flip)
                at = 0
                for out, count in zip(outs, counts):
                    size = count * UNIT
                    column = pl.multiple_of(t * size, UNIT)
                    out[pl.ds(row, rows), pl.ds(column, size)] = piece[a, b, :, at : at + size]
                    at += size


def spread_line(blocks, *earlier):
    own = jnp.concatenate(blocks, 1)
    if earlier:
        own = ordered(own, *earlier)
    return jnp.stack([own] + [over_tensor(own, flip) for flip in (1, 2, 3)])


def spread_small(line):
    near = jnp.stack([line] + [over_dp(line, flip) for flip in (2, 4, 6)])
    return [near, over_dp(near, 1)], SMALL_PIECES


def spread_large(line):
    along_x = over_dp(line, 2)
    along_y = over_dp(line, 4)
    far_low = over_dp(along_x[:2], 4)[None]
    far_high = over_dp(along_y[2:], 2)[None]
    near = [jnp.stack([line, along_x, along_y]), far_low, far_high]
    return near + [over_dp(piece, 1) for piece in near], LARGE_PIECES


def place(blocks, spread, spots):
    pieces, layout = spread
    counts = [block.shape[1] // UNIT for block in blocks]
    rows = blocks[0].shape[0]
    return pl.pallas_call(
        functools.partial(place_kernel, counts, layout),
        out_shape=[jax.ShapeDtypeStruct((8 * rows, 4 * count * UNIT), LOW) for count in counts],
        in_specs=[SCALARS] + [WHOLE] * len(pieces),
        out_specs=[WHOLE] * len(blocks),
        compiler_params=params(32),
        name="place",
    )(spots, *pieces)


def gather_plain(blocks):
    return [
        lax.all_gather(
            lax.all_gather(block, "dp", axis=0, tiled=True), "tensor", axis=1, tiled=True
        )
        for block in blocks
    ]


def grad_kernel(counts, n_small, spots_ref, *refs):
    n = len(counts)
    lefts, rights, (keep_ref, send_ref) = refs[:n], refs[n : 2 * n], refs[-2:]
    me_dp, me_t = spots_ref[0], spots_ref[1]
    core = me_dp % 2
    rows = (keep_ref.shape[0] - n_small) // 16
    if n_small:
        small = refs[2 * n][...].astype(LOW)
        keep_ref[16 * rows :] = small
        send_ref[16 * rows :] = small
    at = 0
    for left, right, count in zip(lefts, rights, counts):
        full = dot_tn(left[...], right[...]).astype(LOW)
        size = count * UNIT

        def store(flipped, at=at, size=size, full=full):
            for d in range(8):
                target = send_ref if (d % 2) != flipped else keep_ref
                near = jnp.bitwise_xor(me_dp, d) // 2
                for t in range(4):
                    row = pl.multiple_of((near * 4 + jnp.bitwise_xor(me_t, t)) * rows, rows)
                    target[pl.ds(row, rows), at : at + size] = full[
                        d * rows : (d + 1) * rows, t * size : (t + 1) * size
                    ]

        pl.when(core == 0)(functools.partial(store, 0))
        pl.when(core == 1)(functools.partial(store, 1))
        at += size


def grad_blocks(pairs, small, spots, us):
    counts = [right.shape[1] // (4 * UNIT) for _, right in pairs]
    rows = 2 * pairs[0][0].shape[1]
    n_small = sum(term.shape[0] for term in small)
    shape = jax.ShapeDtypeStruct((rows + n_small, sum(counts) * UNIT), LOW)
    return pl.pallas_call(
        functools.partial(grad_kernel, counts, n_small),
        out_shape=[shape, shape],
        in_specs=[SCALARS] + [WHOLE] * (2 * len(pairs) + len(small)),
        out_specs=[WHOLE, WHOLE],
        compiler_params=params(40),
        cost_estimate=lasting(us),
        name="grads",
    )(spots, *[left for left, _ in pairs], *[right for _, right in pairs], *small)


def up(value):
    return value.astype(jnp.float32)


class Reduction:
    def __init__(self, pairs, spots, us, small=()):
        self.widths = [right.shape[1] // 4 for _, right in pairs]
        self.rows = pairs[0][0].shape[1] // 8
        self.keep, send = grad_blocks(pairs, small, spots, us)
        self.core = over_dp(send, 1)

    def message(self, blocks):
        flat = blocks.reshape(-1, blocks.shape[-1]).astype(LOW)
        return jnp.concatenate([flat, self.small], 0) if self.small.shape[0] else flat

    def split(self, message, count):
        cut = message.shape[0] - self.small.shape[0]
        blocks = up(message[:cut]).reshape(*count, self.rows, -1)
        return blocks, message[cut:]

    def first(self):
        near = up(self.keep) + up(self.core)
        cut = 16 * self.rows
        self.small = near[cut:].astype(LOW)
        near = near[:cut].reshape(2, 2, 4, self.rows, -1)
        self.low, self.high = near[:, :, :2], near[:, :, 2:]
        self.low_in = over_dp(self.message(self.low[:, 1]), 2)
        self.high_in = over_dp(self.high[1].astype(LOW), 4)
        return self.low_in, self.high_in

    def second(self):
        blocks, small = self.split(self.low_in, (2, 2))
        self.small = (up(self.small) + up(small)).astype(LOW)
        self.low = self.low[:, 0] + blocks
        self.high = self.high[0] + up(self.high_in)
        self.low_in = over_dp(self.message(self.low[1]), 4)
        self.high_in = over_dp(self.high[1].astype(LOW), 2)
        return self.low_in, self.high_in

    def third(self):
        blocks, small = self.split(self.low_in, (2,))
        self.small = (up(self.small) + up(small)).astype(LOW)
        low = self.low[0] + blocks
        high = self.high[0] + up(self.high_in)
        self.own = low[0]
        self.line = (
            over_tensor(self.message(low[1]), 1),
            over_tensor(self.message(high[0]), 2),
            over_tensor(self.message(high[1]), 3),
        )
        return self.line

    def result(self):
        parts = [self.split(message, ()) for message in self.line]
        (one, small_one), (two, small_two), (three, small_three) = parts
        total = (self.own + one) + (two + three)
        small = (up(self.small) + up(small_one)) + (up(small_two) + up(small_three))
        results, at = [], 0
        for width in self.widths:
            results.append(total[:, at : at + width])
            at += width
        return results, small.reshape(-1)


class PlainReduction:
    def __init__(self, pairs, spots, us, small=()):
        self.small = lax.psum(small[0], BOTH).reshape(-1) if small else None
        self.parts = [
            lax.psum_scatter(
                lax.psum_scatter(dot_tn(left, right), "dp", scatter_dimension=0, tiled=True),
                "tensor",
                scatter_dimension=1,
                tiled=True,
            )
            for left, right in pairs
        ]
        self.core = jnp.zeros((8, 128), LOW)

    def first(self):
        return ()

    second = third = first

    def result(self):
        return self.parts, self.small


def pick(array, index, axis):
    return lax.dynamic_index_in_dim(array, index, axis, keepdims=False)


def body(
    query_stream,
    token_stream,
    encoder_states,
    token_segment,
    token_rank,
    source_segment,
    query_map,
    key_map,
    value_map,
    merge_map,
    cross_query,
    cross_key,
    cross_value,
    cross_merge,
    expand_map,
    reduce_map,
    expand_bias,
    reduce_bias,
    gain_first,
    bias_first,
    gain_second,
    bias_second,
    gain_third,
    bias_third,
    cotangent,
    fast,
):
    rows, source_count = query_stream.shape[0], encoder_states.shape[0]
    me_dp, me_t = lax.axis_index("dp"), lax.axis_index("tensor")
    spots = jnp.stack([me_dp, me_t]).astype(jnp.int32)
    sequence, half = me_t // 2, me_t % 2

    groups = (
        (query_map, key_map, value_map),
        (merge_map, cross_query, cross_key, cross_value),
        (cross_merge, expand_map, reduce_map),
    )
    if fast:
        line_one = spread_line(groups[0])
        other_tokens = over_tensor(token_stream, 1)
        line_two = spread_line(groups[1], line_one, other_tokens)
        spread_one = spread_small(line_one)
        w_query, w_key, w_value = place(groups[0], spread_one, spots)
        other_source = over_tensor(ordered(encoder_states, line_two), 1)
        spread_two = spread_small(ordered(line_two, spread_one[0][0]))
        line_three = spread_line(groups[2], line_two)
        w_merge, w_cquery, w_ckey, w_cvalue = place(groups[1], spread_two, spots)
        spread_three = spread_large(ordered(line_three, spread_two[0][0]))
        w_cmerge, w_expand, w_reduce = place(groups[2], spread_three, spots)
    else:
        other_tokens = over_tensor(token_stream, 1)
        other_source = over_tensor(encoder_states, 1)
        w_query, w_key, w_value = gather_plain(groups[0])
        w_merge, w_cquery, w_ckey, w_cvalue = gather_plain(groups[1])
        w_cmerge, w_expand, w_reduce = gather_plain(groups[2])
    reduction = Reduction if fast else PlainReduction

    def halves(row, size):
        return lax.dynamic_slice_in_dim(row, half * size, size), lax.dynamic_slice_in_dim(
            row, (1 - half) * size, size
        )

    segment_row = pick(token_segment, sequence, 0)
    starts_row = jnp.concatenate([jnp.ones((1,), jnp.bool_), segment_row[1:] != segment_row[:-1]])
    own_segment, far_segment = halves(segment_row, rows)
    own_rank, far_rank = halves(pick(token_rank, sequence, 0), rows)
    key_segment = jnp.concatenate([own_segment, far_segment])
    key_rank = jnp.concatenate([own_rank, far_rank])
    key_start = jnp.concatenate(halves(starts_row, rows))
    source_row = jnp.concatenate(halves(pick(source_segment, sequence, 0), source_count))
    self_allowed = (own_segment[None, :] == key_segment[:, None]) & (
        (key_rank[:, None] < own_rank[None, :]) | key_start[:, None]
    )
    cross_allowed = own_segment[None, :] == source_row[:, None]
    self_bias = jnp.where(self_allowed, 0.0, -1e30).astype(jnp.float32)
    cross_bias = jnp.where(cross_allowed, 0.0, -1e30).astype(jnp.float32)
    self_near = near_tiles(own_segment, key_segment, SELF_TILE)
    cross_near = near_tiles(own_segment, source_row, CROSS_TILE)

    gains_one, gains_two, gains_three = (up(gain) for gain in (gain_first, gain_second, gain_third))
    offset_one, offset_two, offset_three = (up(bias) for bias in (bias_first, bias_second, bias_third))

    token_rows = jnp.concatenate([token_stream, other_tokens], 0)
    source_rows = jnp.concatenate([encoder_states, other_source], 0)
    queries = (dot_nn(query_stream, w_query) * 0.125).astype(LOW)
    key_rows = dot_nn(token_rows, w_key).astype(LOW)
    values = dot_nn(token_rows, w_value).astype(LOW)
    part = attend_part(
        self_near, queries, key_rows, values, self_bias, SELF_TILE, 0, 2, (), (), 7
    )
    mixture, self_total = attend_part(
        self_near, queries, key_rows, values, self_bias, SELF_TILE, 2, 2, part, (), 7
    )
    first_out, first_normed, first_inverse = norm_rows(
        up(query_stream) + dot_nt(mixture, w_merge), gains_one, offset_one
    )
    first_low = first_out.astype(LOW)
    cross_rows = (dot_nn(first_low, w_cquery) * 0.125).astype(LOW)
    source_keys = dot_nn(source_rows, w_ckey).astype(LOW)
    source_values = dot_nn(source_rows, w_cvalue).astype(LOW)
    part = attend_part(
        cross_near, cross_rows, source_keys, source_values, cross_bias, CROSS_TILE, 0, 2, (), (), 9
    )
    cross_mix, cross_total = attend_part(
        cross_near, cross_rows, source_keys, source_values, cross_bias, CROSS_TILE, 2, 2, part, (), 9
    )
    second_out, second_normed, second_inverse = norm_rows(
        first_out + dot_nt(cross_mix, w_cmerge), gains_two, offset_two
    )
    second_low = second_out.astype(LOW)
    hidden_pre = dot_nn(second_low, w_expand) + up(expand_bias)
    active = smooth_gate(hidden_pre).astype(LOW)
    third_out, third_normed, third_inverse = norm_rows(
        second_out + dot_nt(active, w_reduce) + up(reduce_bias), gains_three, offset_three
    )
    hidden_states = third_out.astype(LOW)

    third_grad, gain_third_grad, bias_third_grad = norm_back(
        up(cotangent), third_normed, third_inverse, gains_three
    )
    output_grad = third_grad.astype(LOW)
    reduce_bias_grad = jnp.sum(up(output_grad), 0)
    pre_grad = (dot_nn(output_grad, w_reduce) * gate_slope(hidden_pre)).astype(LOW)
    expand_bias_grad = jnp.sum(up(pre_grad), 0)
    hidden_sum = reduction([(second_low, pre_grad), (output_grad, active)], spots, 5)
    second_grad = third_grad + dot_nt(pre_grad, w_expand)
    second_in_grad, gain_second_grad, bias_second_grad = norm_back(
        second_grad, second_normed, second_inverse, gains_two
    )
    cross_out = second_in_grad.astype(LOW)
    cross_mix_grad = dot_nn(cross_out, w_cmerge).astype(LOW)
    cross_set = (
        cross_near, cross_rows, source_keys, source_values, cross_mix_grad, cross_mix, cross_total,
        cross_bias, CROSS_TILE,
    )
    part = attend_back_part(*cross_set, 0, 2, (), (hidden_sum.core,), 11)
    steps = hidden_sum.first()
    cross_rows_grad, source_keys_grad, source_values_grad = attend_back_part(
        *cross_set, 2, 2, part, steps, 11
    )
    hidden_sum.second()
    cross_sum = reduction(
        [
            (first_low, cross_rows_grad),
            (source_rows, source_keys_grad),
            (source_rows, source_values_grad),
            (cross_out, cross_mix),
        ],
        spots,
        4,
    )
    source_part = dot_nt(source_keys_grad, w_ckey) + dot_nt(source_values_grad, w_cvalue)
    source_back = over_tensor(source_part[source_count:].astype(LOW), 1)
    first_grad = second_in_grad + dot_nt(cross_rows_grad, w_cquery)
    stream_grad, gain_first_grad, bias_first_grad = norm_back(
        first_grad, first_normed, first_inverse, gains_one
    )
    self_out = stream_grad.astype(LOW)
    small_terms = (
        expand_bias_grad,
        reduce_bias_grad,
        gain_first_grad,
        bias_first_grad,
        gain_second_grad,
        bias_second_grad,
        gain_third_grad,
        bias_third_grad,
    )
    packed = jnp.concatenate(small_terms).reshape(-1, query_stream.shape[1])
    packed = jnp.pad(packed, ((0, -packed.shape[0] % 16), (0, 0)))
    mixture_grad = dot_nn(self_out, w_merge).astype(LOW)
    self_set = (
        self_near, queries, key_rows, values, mixture_grad, mixture, self_total, self_bias, SELF_TILE
    )
    steps = cross_sum.first()
    part = attend_back_part(*self_set, 0, 2, (), (cross_sum.core,), 9)
    hidden_sum.third()
    queries_grad, keys_grad, values_grad = attend_back_part(*self_set, 2, 2, part, (), 9)
    self_sum = reduction(
        [
            (query_stream, queries_grad),
            (token_rows, keys_grad),
            (token_rows, values_grad),
            (self_out, mixture),
        ],
        spots,
        4,
        (packed,),
    )
    cross_sum.second()
    token_part = dot_nt(keys_grad, w_key) + dot_nt(values_grad, w_value)
    token_back = over_tensor(token_part[rows:].astype(LOW), 1)
    self_sum.first()
    cross_sum.third()
    self_sum.second()
    self_sum.third()
    (expand_part, reduce_part), _ = hidden_sum.result()
    cross_parts, _ = cross_sum.result()
    self_parts, summed = self_sum.result()
    small, at = [], 0
    for term in small_terms:
        small.append(summed[at : at + term.shape[0]])
        at += term.shape[0]
    return (
        hidden_states,
        (stream_grad + dot_nt(queries_grad, w_query)).astype(LOW),
        (token_part[:rows] + up(token_back)).astype(LOW),
        (source_part[:source_count] + up(source_back)).astype(LOW),
        *self_parts,
        *cross_parts,
        expand_part,
        reduce_part,
        *small,
    )


def solution(mesh):
    fast = mesh.shape["dp"] == 8 and mesh.shape["tensor"] == 4
    rows = P(BOTH, None)
    block = P("dp", "tensor")

    def program(*arguments):
        return body(*arguments, fast)

    return jax.shard_map(
        program,
        mesh=mesh,
        in_specs=(rows,) * 3 + (P("dp", None),) * 3 + (block,) * 10 + (P(),) * 8 + (rows,),
        out_specs=(rows,) * 4 + (block,) * 10 + (P(),) * 8,
        check_vma=False,
    )
```

```python
import functools

import jax
import jax.numpy as jnp
from jax import lax
from jax.sharding import PartitionSpec as P
from jax.experimental import pallas as pl
from jax.experimental.pallas import tpu as pltpu

EPSILON = 1e-05
GATE = 0.7978845608028654
CUBIC = 0.044715
LOG2E = 1.4426950408889634
UNIT = 128
PAIR = 128
SELF_TILE = (512, 256)
CROSS_TILE = (256, 256)
BOTH = ("dp", "tensor")
ANY = pl.BlockSpec(memory_space=pl.ANY)
WHOLE = pl.BlockSpec(memory_space=pltpu.VMEM)
SCALARS = pl.BlockSpec(memory_space=pltpu.SMEM)
LOW = jnp.bfloat16


def params(mib):
    return pltpu.CompilerParams(vmem_limit_bytes=mib * 1024 * 1024)


def lasting(us):
    return pl.CostEstimate(flops=int(us * 1.1e7), bytes_accessed=0, transcendentals=0)


def far_memory(value):
    return pltpu.with_memory_space_constraint(value, pltpu.HBM)


def up(value):
    return value.astype(jnp.float32)


def dot_nn(a, b):
    return lax.dot_general(a, b, (((1,), (0,)), ((), ())), preferred_element_type=jnp.float32)


def dot_nt(a, b):
    return lax.dot_general(a, b, (((1,), (1,)), ((), ())), preferred_element_type=jnp.float32)


def dot_tn(a, b):
    return lax.dot_general(a, b, (((0,), (0,)), ((), ())), preferred_element_type=jnp.float32)


REDUCE_BIAS, GAIN_ONE, BIAS_ONE, GAIN_TWO, BIAS_TWO, GAIN_THREE, BIAS_THREE = range(-7, 0)


def norm_rows(matrix):
    centred = matrix - jnp.mean(matrix, -1, keepdims=True)
    inverse = lax.rsqrt(jnp.mean(centred * centred, -1, keepdims=True) + EPSILON)
    return centred * inverse, inverse


def norm_back(outer_grad, normed, inverse, gains):
    spread = outer_grad * gains
    return inverse * (
        spread
        - jnp.mean(spread, -1, keepdims=True)
        - normed * jnp.mean(spread * normed, -1, keepdims=True)
    )


def down(matrix):
    return jnp.sum(matrix, 0, keepdims=True)


def table_row(table_ref, row):
    row += table_ref.shape[0]
    return table_ref[row : row + 1]


def hidden_kernel(
    fast, spots_ref, mix_ref, merge_ref, first_ref, table_ref, expand_ref, reduce_ref, cotangent_ref, *refs
):
    states_ref, third_ref, pre_ref, normed_ref, inverse_ref, small_ref, *grads = refs[:8]
    active_ref, slope_ref = refs[8:]
    row = functools.partial(table_row, table_ref)
    first_out = first_ref[...] * row(GAIN_ONE) + row(BIAS_ONE)
    normed, inverse = norm_rows(first_out + dot_nt(mix_ref[...], merge_ref[...]))
    normed_ref[...] = normed
    inverse_ref[...] = inverse
    second_out = normed * row(GAIN_TWO) + row(BIAS_TWO)
    second_low = second_out.astype(LOW)
    width = mix_ref.shape[1]
    chunks = expand_ref.shape[1] // width
    output = second_out + row(REDUCE_BIAS)
    for c in range(chunks):
        columns = slice(c * width, (c + 1) * width)
        x = dot_nn(second_low, expand_ref[:, columns]) + table_ref[c : c + 1]
        square = x * x
        bent = jnp.tanh(x * (GATE + (GATE * CUBIC) * square))
        halved = 0.5 + 0.5 * bent
        active = (x * halved).astype(LOW)
        slope_ref[:, columns] = halved + (0.5 * x) * (1.0 - bent * bent) * (
            GATE + (3.0 * GATE * CUBIC) * square
        )
        active_ref[:, columns] = active
        output = output + dot_nt(active, reduce_ref[:, columns])
    normed, inverse = norm_rows(output)
    states_ref[...] = (normed * row(GAIN_THREE) + row(BIAS_THREE)).astype(LOW)
    outer = up(cotangent_ref[...])
    third = norm_back(outer, normed, inverse, row(GAIN_THREE))
    third_ref[...] = third
    output_grad = third.astype(LOW)
    small_ref[...] = jnp.zeros(small_ref.shape, jnp.float32)
    at = table_ref.shape[0]
    small_ref[at + GAIN_THREE : at + GAIN_THREE + 1] = down(outer * normed)
    small_ref[at + BIAS_THREE : at + BIAS_THREE + 1] = down(outer)
    small_ref[at + REDUCE_BIAS : at + REDUCE_BIAS + 1] = down(up(output_grad))
    for c in range(chunks):
        columns = slice(c * width, (c + 1) * width)
        pre_grad = (dot_nn(output_grad, reduce_ref[:, columns]) * slope_ref[:, columns]).astype(LOW)
        pre_ref[:, columns] = pre_grad
        small_ref[c : c + 1] = down(up(pre_grad))
        parts = (dot_tn(second_low, pre_grad), dot_tn(output_grad, active_ref[:, columns]))
        for i, part in enumerate(parts):
            if fast:
                store_blocks(spots_ref, *grads, part.astype(LOW), (c,), i * width)
            else:
                grads[i][:, columns] = part


def hidden_back_kernel(
    third_ref, pre_ref, expand_ref, normed_ref, inverse_ref, table_ref, merge_ref, *refs
):
    inner_ref, low_ref, mix_ref, small_ref = refs
    normed = normed_ref[...]
    outer = third_ref[...] + dot_nt(pre_ref[...], expand_ref[...])
    inner = norm_back(outer, normed, inverse_ref[...], table_row(table_ref, GAIN_TWO))
    inner_ref[...] = inner
    low = inner.astype(LOW)
    low_ref[...] = low
    mix_ref[...] = dot_nn(low, merge_ref[...]).astype(LOW)
    small_ref[0:1] = down(outer * normed)
    small_ref[1:2] = down(outer)


def first_back_kernel(
    second_ref, rows_ref, query_ref, normed_ref, inverse_ref, table_ref, merge_ref, one_ref, two_ref, *refs
):
    inner_ref, low_ref, mix_ref, small_ref = refs
    normed = normed_ref[...]
    outer = second_ref[...] + dot_nt(rows_ref[...], query_ref[...])
    inner = norm_back(outer, normed, inverse_ref[...], table_row(table_ref, GAIN_ONE))
    inner_ref[...] = inner
    low = inner.astype(LOW)
    low_ref[...] = low
    mix_ref[...] = dot_nn(low, merge_ref[...]).astype(LOW)
    at = table_ref.shape[0]
    small_ref[...] = one_ref[...]
    small_ref[at + GAIN_TWO : at + BIAS_TWO + 1] = two_ref[0:2]
    small_ref[at + GAIN_ONE : at + GAIN_ONE + 1] = down(outer * normed)
    small_ref[at + BIAS_ONE : at + BIAS_ONE + 1] = down(outer)


def kernel_call(kernel, outs, mib, us, name, *operands, scalars=0, scratch=()):
    return pl.pallas_call(
        kernel,
        out_shape=[jax.ShapeDtypeStruct(*out) for out in outs],
        in_specs=[SCALARS] * scalars + [WHOLE] * (len(operands) - scalars),
        out_specs=[WHOLE] * len(outs),
        scratch_shapes=list(scratch),
        compiler_params=params(mib),
        cost_estimate=lasting(us),
        name=name,
    )(*operands)


def split_heads(rows):
    lane = lax.broadcasted_iota(jnp.int32, rows.shape, 1)
    zero = jnp.zeros_like(rows)
    return jnp.concatenate(
        [jnp.where(lane < PAIR // 2, rows, zero), jnp.where(lane < PAIR // 2, zero, rows)], 0
    )


def twice(row):
    return jnp.concatenate([row, row], 1)


def attend_pair(near_ref, bias_ref, q_ref, sides, out_ref, lse_ref, scratch, tile):
    k_near, k_far, v_near, v_far = sides
    turned, top, total, acc = scratch
    tile_q, tile_k = tile
    nq, nk = q_ref.shape[0] // tile_q, k_near.shape[0] // tile_k
    half = PAIR // 2
    turned[0] = v_near[...].T
    turned[1] = v_far[...].T
    for i in range(nq):
        q_rows = slice(i * tile_q, (i + 1) * tile_q)
        stacked = split_heads(q_ref[q_rows])
        top[...] = jnp.full(top.shape, -3e30, jnp.float32)
        total[...] = jnp.zeros(total.shape, jnp.float32)
        acc[...] = jnp.zeros(acc.shape, jnp.float32)
        for j in range(2 * nk):

            @pl.when(near_ref[i, j] != 0)
            def _(j=j, stacked=stacked, q_rows=q_rows):
                k_ref = k_far if j >= nk else k_near
                k_rows = slice(j % nk * tile_k, (j % nk + 1) * tile_k)
                bias = bias_ref[j * tile_k : (j + 1) * tile_k, q_rows]
                scores = dot_nt(k_ref[k_rows], stacked) + twice(bias)
                old = top[...]
                peak = jnp.maximum(old, jnp.max(scores, 0, keepdims=True))
                fade = jnp.exp2((old - peak) * LOG2E)
                powers = jnp.exp2((scores - peak) * LOG2E)
                top[...] = peak
                total[...] = total[...] * fade + jnp.sum(powers, 0, keepdims=True)
                acc[...] = acc[...] * fade + dot_nn(turned[j // nk, :, k_rows], powers.astype(LOW))

        full = total[...]
        scaled = acc[...] * (1.0 / full)
        mixed = jnp.concatenate([scaled[:half, :tile_q], scaled[half:, tile_q:]], 0)
        out_ref[q_rows] = mixed.T.astype(LOW)
        log_total = top[...] * LOG2E + jnp.log2(full)
        lse_ref[0, 0:1, q_rows] = log_total[:, :tile_q]
        lse_ref[0, 1:2, q_rows] = log_total[:, tile_q:]


def attend_scratch(lk, tile):
    return [
        pltpu.VMEM((2, PAIR, lk), LOW),
        pltpu.VMEM((1, 2 * tile[0]), jnp.float32),
        pltpu.VMEM((1, 2 * tile[0]), jnp.float32),
        pltpu.VMEM((PAIR, 2 * tile[0]), jnp.float32),
    ]


def place_block(spots_ref, pieces, out, t, at):
    me_dp, flip = spots_ref[0], jnp.bitwise_xor(spots_ref[1], t)
    rows = pieces[0].shape[2]
    for piece, (dp_flips, _) in zip(pieces, PIECES):
        for a, dp_flip in enumerate(dp_flips):
            row = pl.multiple_of(jnp.bitwise_xor(me_dp, dp_flip) * rows, rows)
            out[pl.ds(row, rows)] = piece[a, flip, :, at : at + out.shape[1]]


def place_whole(spots_ref, pieces, out, at):
    for t in range(out.shape[1] // PAIR):
        place_block(spots_ref, pieces, out.at[:, t * PAIR : (t + 1) * PAIR], t, at)


def self_kernel(
    fast, tile, spots_ref, near_ref, bias_ref, query_ref, token_ref, far_ref, *refs
):
    cut = 2 if fast else 3
    pieces, outs, scratch = refs[:cut], refs[cut:-4], refs[-4:]
    out_ref, lse_ref, q_ref, *rest = outs
    sides, weights = rest[:4], rest[4:]
    if fast:
        for i, weight in enumerate(weights):
            place_block(spots_ref, pieces, weight, pl.program_id(0), i * PAIR)
    else:
        weights = pieces
    w_query, w_key, w_value = (weight[...] for weight in weights)
    q_ref[...] = (dot_nn(query_ref[...], w_query) * 0.125).astype(LOW)
    for out, rows, weight in zip(
        sides, (token_ref, far_ref, token_ref, far_ref), (w_key, w_key, w_value, w_value)
    ):
        out[...] = dot_nn(rows[...], weight).astype(LOW)
    attend_pair(near_ref, bias_ref, q_ref, sides, out_ref, lse_ref, scratch, tile)


def self_forward(fast, spots, near, bias, streams, gathered, tile, us):
    lq, width = streams[0].shape
    lk = streams[1].shape[0]
    column = lambda p: (0, p)
    q_spec, k_spec = pl.BlockSpec((lq, PAIR), column), pl.BlockSpec((lk, PAIR), column)
    w_spec = pl.BlockSpec((width, PAIR), column)
    rows, keys, square = (((n, width), LOW) for n in (lq, lk, width))
    outs = [rows, ((width // PAIR, 2, lq), jnp.float32), rows] + [keys] * 4
    specs = [q_spec, pl.BlockSpec((1, 2, lq), lambda p: (p, 0, 0)), q_spec] + [k_spec] * 4
    if fast:
        outs, specs = outs + [square] * 3, specs + [w_spec] * 3
    results = pl.pallas_call(
        functools.partial(self_kernel, fast, tile),
        grid=(width // PAIR,),
        in_specs=[SCALARS, SCALARS] + [WHOLE] * 4
        + ([WHOLE] * 2 if fast else [w_spec] * 3),
        out_specs=specs,
        out_shape=[jax.ShapeDtypeStruct(*out) for out in outs[:1]]
        + [pltpu.HBM(*out) for out in outs[1:]],
        scratch_shapes=attend_scratch(lk, tile),
        compiler_params=params(24),
        cost_estimate=lasting(us),
        name="self_forward",
    )(spots, near, bias, *map(far_memory, streams), *gathered)
    mixture, lse, queries = results[:3]
    return mixture, lse, queries, results[3:7], results[7:] if fast else gathered


def cross_kernel(
    fast, tile, spots_ref, near_ref, bias_ref, mix_ref, stream_ref, near_rows, far_rows, table_ref, *refs
):
    cut = 2 if fast else 4
    pieces, outs, scratch = refs[:cut], refs[cut:-5], refs[-5:]
    out_ref, lse_ref, rows_ref, normed_ref, inverse_ref, low_ref, *rest = outs
    sides, weights = rest[:4], rest[4:]
    p = pl.program_id(0)
    if fast:
        w_merge, w_query, w_key, w_value = weights
        place_block(spots_ref, pieces, w_key, p, 2 * PAIR)
        place_block(spots_ref, pieces, w_value, p, 3 * PAIR)
    else:
        w_merge, w_query, w_key, w_value = pieces

    @pl.when(p == 0)
    def _():
        if fast:
            place_whole(spots_ref, pieces, w_merge, 0)
            place_whole(spots_ref, pieces, w_query, PAIR)
        normed, inverse = norm_rows(up(stream_ref[...]) + dot_nt(mix_ref[...], w_merge[...]))
        normed_ref[...] = normed
        inverse_ref[...] = inverse
        low = (normed * table_row(table_ref, GAIN_ONE) + table_row(table_ref, BIAS_ONE)).astype(LOW)
        low_ref[...] = low
        all_rows = (dot_nn(low, w_query[...]) * 0.125).astype(LOW)
        for t in range(all_rows.shape[1] // PAIR):
            scratch[0][t] = all_rows[:, t * PAIR : (t + 1) * PAIR]

    rows_ref[...] = scratch[0][p]
    for out, rows, weight in zip(
        sides, (near_rows, far_rows, near_rows, far_rows), (w_key, w_key, w_value, w_value)
    ):
        out[...] = dot_nn(rows[...], weight[...]).astype(LOW)
    attend_pair(near_ref, bias_ref, rows_ref, sides, out_ref, lse_ref, scratch[1:], tile)


def cross_forward(fast, spots, near, bias, mixture, stream, sources, table, gathered, tile, us):
    lq, width = mixture.shape
    lk = sources[0].shape[0]
    column = lambda p: (0, p)
    q_spec, k_spec = pl.BlockSpec((lq, PAIR), column), pl.BlockSpec((lk, PAIR), column)
    w_spec = pl.BlockSpec((width, PAIR), column)
    rows, keys, square = (((n, width), LOW) for n in (lq, lk, width))
    outs = [
        rows, ((width // PAIR, 2, lq), jnp.float32), rows,
        ((lq, width), jnp.float32), ((lq, 1), jnp.float32), rows,
    ] + [keys] * 4
    specs = [q_spec, pl.BlockSpec((1, 2, lq), lambda p: (p, 0, 0)), q_spec] + [WHOLE] * 3 + [k_spec] * 4
    w_specs = [WHOLE, WHOLE, w_spec, w_spec]
    if fast:
        outs, specs = outs + [square] * 4, specs + w_specs
    results = pl.pallas_call(
        functools.partial(cross_kernel, fast, tile),
        grid=(width // PAIR,),
        in_specs=[SCALARS, SCALARS] + [WHOLE] * 6 + ([WHOLE] * 2 if fast else w_specs),
        out_specs=specs,
        out_shape=[jax.ShapeDtypeStruct(*out) for out in outs[:1]]
        + [pltpu.HBM(*out) for out in outs[1:]],
        scratch_shapes=[pltpu.VMEM((width // PAIR, lq, PAIR), LOW)] + attend_scratch(lk, tile),
        compiler_params=params(30),
        cost_estimate=lasting(us),
        name="cross_forward",
    )(spots, near, bias, mixture, far_memory(stream), *map(far_memory, sources), table, *gathered)
    return results[:6], results[6:10], results[10:] if fast else gathered


def backward_kernel(near_ref, bias_ref, q_ref, m_ref, o_ref, lse_ref, *refs, tile_q, tile_k):
    k_near, k_far, v_near, v_far = refs[:4]
    dq_ref, *outs, dq_acc, dk_acc, dv_acc = refs[-8:]
    nq, nk = q_ref.shape[0] // tile_q, k_near.shape[0] // tile_k
    half = PAIR // 2
    dk_acc[...] = jnp.zeros(dk_acc.shape, jnp.float32)
    dv_acc[...] = jnp.zeros(dv_acc.shape, jnp.float32)
    for i in range(nq):
        q_rows = slice(i * tile_q, (i + 1) * tile_q)
        stacked = split_heads(q_ref[q_rows])
        grads = split_heads(m_ref[q_rows])
        turned = (m_ref[q_rows].astype(jnp.float32) * o_ref[q_rows].astype(jnp.float32)).T
        delta = jnp.concatenate(
            [jnp.sum(turned[:half], 0, keepdims=True), jnp.sum(turned[half:], 0, keepdims=True)], 1
        )
        log_total = jnp.concatenate([lse_ref[0, 0:1, q_rows], lse_ref[0, 1:2, q_rows]], 1)
        dq_acc[...] = jnp.zeros(dq_acc.shape, jnp.float32)
        for j in range(2 * nk):

            @pl.when(near_ref[i, j] != 0)
            def _(
                j=j, stacked=stacked, grads=grads, delta=delta, log_total=log_total, q_rows=q_rows
            ):
                k_ref, v_ref = (k_far, v_far) if j >= nk else (k_near, v_near)
                k_rows = slice(j % nk * tile_k, (j % nk + 1) * tile_k)
                all_rows = slice(j * tile_k, (j + 1) * tile_k)
                keys = k_ref[k_rows]
                scores = dot_nt(keys, stacked)
                weights = jnp.exp2(
                    scores * LOG2E + (twice(bias_ref[all_rows, q_rows]) - log_total)
                )
                outer = dot_nt(v_ref[k_rows], grads)
                slope = (weights * (outer - delta)).astype(LOW)
                dv_acc[all_rows] += dot_nn(weights.astype(LOW), grads)
                dk_acc[all_rows] += dot_nn(slope, stacked)
                dq_acc[...] += dot_tn(slope, keys)

        lane = lax.broadcasted_iota(jnp.int32, (tile_q, PAIR), 1)
        dq_ref[q_rows] = (
            jnp.where(lane < half, dq_acc[:tile_q], dq_acc[tile_q:]) * 0.125
        ).astype(LOW)
    size = k_near.shape[0]
    for out, acc, side in zip(outs, (dk_acc, dk_acc, dv_acc, dv_acc), (0, 1, 0, 1)):
        out[...] = acc[side * size : (side + 1) * size].astype(LOW)


def attend_back_part(near, bias, queries, sides, outer, mixed, lse, tile, base, count, before, us):
    lq, width = queries.shape
    lk = sides[0].shape[0]
    tile_q, tile_k = tile
    column = lambda p: (0, p + base)
    q_spec, k_spec = pl.BlockSpec((lq, PAIR), column), pl.BlockSpec((lk, PAIR), column)
    return pl.pallas_call(
        functools.partial(backward_kernel, tile_q=tile_q, tile_k=tile_k),
        grid=(count,),
        in_specs=[SCALARS, WHOLE, q_spec, q_spec, q_spec]
        + [pl.BlockSpec((1, 2, lq), lambda p: (p + base, 0, 0))]
        + [k_spec] * 4
        + [ANY] * len(before),
        out_specs=[q_spec] + [k_spec] * 4,
        out_shape=[jax.ShapeDtypeStruct((lq, width), LOW)]
        + [jax.ShapeDtypeStruct((lk, width), LOW)] * 4,
        scratch_shapes=[
            pltpu.VMEM((2 * tile_q, PAIR), jnp.float32),
            pltpu.VMEM((2 * lk, PAIR), jnp.float32),
            pltpu.VMEM((2 * lk, PAIR), jnp.float32),
        ],
        input_output_aliases={10 + i: i for i in range(len(before))},
        compiler_params=params(18),
        cost_estimate=lasting(us),
        name="attend_back",
    )(near, bias, queries, outer, mixed, lse, *sides, *before)


def near_tiles(own, keys, tile):
    own, keys = own.reshape(-1, tile[0]), keys.reshape(-1, tile[1])
    return (
        (keys.min(1)[None] <= own.max(1)[:, None]) & (keys.max(1)[None] >= own.min(1)[:, None])
    ).astype(jnp.int32)


def over_dp(matrix, flip):
    return lax.ppermute(matrix, "dp", [(i, i ^ flip) for i in range(8)])


def over_tensor(matrix, flip):
    return lax.ppermute(matrix, "tensor", [(i, i ^ flip) for i in range(4)])


def ordered(value, *earlier):
    return lax.optimization_barrier((value, *earlier))[0] if earlier else value


PIECES = (((0, 2, 4, 6), (0, 1, 2, 3)), ((1, 3, 5, 7), (0, 1, 2, 3)))


def place_kernel(counts, spots_ref, *refs):
    n = len(counts)
    pieces, outs = refs[:-n], refs[-n:]
    me_dp, me_t = spots_ref[0], spots_ref[1]
    rows = pieces[0].shape[2]
    for piece, (dp_flips, t_flips) in zip(pieces, PIECES):
        for a, dp_flip in enumerate(dp_flips):
            row = pl.multiple_of(jnp.bitwise_xor(me_dp, dp_flip) * rows, rows)
            for b, t_flip in enumerate(t_flips):
                t = jnp.bitwise_xor(me_t, t_flip)
                at = 0
                for out, count in zip(outs, counts):
                    size = count * UNIT
                    column = pl.multiple_of(t * size, UNIT)
                    out[pl.ds(row, rows), pl.ds(column, size)] = piece[a, b, :, at : at + size]
                    at += size


def load_kernel(counts, *refs):
    n, n_vectors = sum(counts), 8
    blocks, vectors = list(refs[:n]), refs[n : n + n_vectors]
    outs, held, sems = refs[n + n_vectors : -2], refs[-2], refs[-1]
    copies = []

    def copy(source, target):
        copies.append(pltpu.make_async_copy(source, target, sems.at[len(copies)]))
        copies[-1].start()

    for out, count in zip(outs, counts):
        at = 0
        for _ in range(count):
            block = blocks.pop(0)
            copy(block, out.at[:, at : at + block.shape[1]])
            at += block.shape[1]
    at = 0
    for vector in vectors:
        copy(vector, held.at[at : at + vector.shape[0]])
        at += vector.shape[0]
    for one in copies:
        one.wait()
    table = outs[-1]
    width = table.shape[1]
    for i in range(table.shape[0]):
        table[i : i + 1] = up(held[i * width : (i + 1) * width]).reshape(1, width)


def load(groups, vectors, width):
    blocks = [block for group in groups for block in group]
    total = sum(vector.shape[0] for vector in vectors)
    return pl.pallas_call(
        functools.partial(load_kernel, [len(group) for group in groups]),
        out_shape=[
            jax.ShapeDtypeStruct((group[0].shape[0], sum(block.shape[1] for block in group)), LOW)
            for group in groups
        ]
        + [jax.ShapeDtypeStruct((total // width, width), jnp.float32)],
        in_specs=[ANY] * (len(blocks) + len(vectors)),
        out_specs=[WHOLE] * (len(groups) + 1),
        scratch_shapes=[
            pltpu.VMEM((total,), LOW),
            pltpu.SemaphoreType.DMA((len(blocks) + len(vectors),)),
        ],
        compiler_params=params(4),
        name="load",
    )(*map(far_memory, blocks), *map(far_memory, vectors))


def table_kernel(*refs):
    *vectors, out = refs
    width, at = out.shape[1], 0
    for vector in vectors:
        row = up(vector[...])
        for i in range(vector.shape[0] // width):
            out[at : at + 1] = row[i * width : (i + 1) * width].reshape(1, width)
            at += 1


def combine_kernel(keep_ref, core_ref, *outs):
    own, *messages, small = outs
    size = own.shape[0]
    n_small = keep_ref.shape[0] - 4 * size
    if n_small:
        total = (up(keep_ref[4 * size :]) + up(core_ref[4 * size :])).astype(LOW)
        small[...] = total
    own[...] = up(keep_ref[:size]) + up(core_ref[:size])
    for i, message in enumerate(messages, 1):
        rows = slice(i * size, (i + 1) * size)
        message[:size] = (up(keep_ref[rows]) + up(core_ref[rows])).astype(LOW)
        if n_small:
            message[size:] = total


def spread_line(own):
    return [own] + [over_tensor(own, flip) for flip in (1, 2, 3)]


def spread_plane(line):
    line = jnp.stack(line)
    return [line] + [over_dp(line, flip) for flip in (2, 4, 6)]


def join(near):
    near = jnp.stack(near)
    return [near, over_dp(near, 1)]


def place(blocks, pieces, spots):
    counts = [block.shape[1] // UNIT for block in blocks]
    rows = blocks[0].shape[0]
    outs = [((8 * rows, 4 * count * UNIT), LOW) for count in counts]
    return kernel_call(
        functools.partial(place_kernel, counts), outs, 18, 1, "place", spots, *pieces, scalars=1
    )


def gather_plain(blocks):
    return [
        lax.all_gather(
            lax.all_gather(block, "dp", axis=0, tiled=True), "tensor", axis=1, tiled=True
        )
        for block in blocks
    ]


def store_blocks(spots_ref, keep_ref, send_ref, full, ts, at):
    me_dp, me_t = spots_ref[0], spots_ref[1]
    rows, size = full.shape[0] // 8, full.shape[1] // len(ts)

    def store(flipped):
        for d in range(8):
            target = send_ref if (d % 2) != flipped else keep_ref
            near = jnp.bitwise_xor(me_dp, d) // 2
            for i, t in enumerate(ts):
                row = pl.multiple_of((near * 4 + jnp.bitwise_xor(me_t, t)) * rows, rows)
                target[pl.ds(row, rows), at : at + size] = full[
                    d * rows : (d + 1) * rows, i * size : (i + 1) * size
                ]

    pl.when(me_dp % 2 == 0)(functools.partial(store, 0))
    pl.when(me_dp % 2 == 1)(functools.partial(store, 1))


def grad_kernel(layout, n_small, spots_ref, *refs):
    keep_ref, send_ref = refs[-2:]
    refs = list(refs[:-2])
    if n_small:
        small = refs.pop()[...].astype(LOW)
        used = small.shape[1]
        for target in (keep_ref, send_ref):
            target[-n_small:] = jnp.zeros((n_small, target.shape[1]), LOW)
            target[-n_small:, :used] = small
    at = 0
    for n_products, n_right in layout:
        full = None
        for _ in range(n_products):
            left = refs.pop(0)[...]
            right = [refs.pop(0)[...] for _ in range(n_right)]
            product = dot_tn(left, jnp.concatenate(right, 1) if n_right > 1 else right[0])
            full = product if full is None else full + product
        full = full.astype(LOW)
        width = full.shape[1] // n_right
        for i in range(n_right):
            part = full[:, i * width : (i + 1) * width]
            store_blocks(spots_ref, keep_ref, send_ref, part, range(4), at)
            at += width // 4


def grad_blocks(sums, small, spots, us):
    layout = [(len(products), len(products[0][1])) for products in sums]
    rows = 2 * sums[0][0][0].shape[1]
    n_small = sum(term.shape[0] for term in small)
    width = sum(right.shape[1] for products in sums for right in products[0][1])
    operands = [
        matrix for products in sums for left, rights in products for matrix in (left, *rights)
    ]
    out = ((rows + n_small, width // 4), LOW)
    return kernel_call(
        functools.partial(grad_kernel, layout, n_small),
        [out, out],
        28,
        us,
        "grads",
        spots,
        *operands,
        *small,
        scalars=1,
    )


class Reduction:
    def __init__(self, keep, send, widths, n_small=0):
        self.keep, self.widths, self.n_small = keep, widths, n_small
        self.rows = (keep.shape[0] - n_small) // 16
        self.core = over_dp(send, 1)

    def split(self, matrix):
        cut = matrix.shape[0] - self.n_small
        return matrix[:cut], matrix[cut:]

    def message(self, blocks, small):
        return jnp.concatenate([blocks.astype(LOW), small], 0) if self.n_small else blocks.astype(LOW)

    def first(self, *earlier):
        size, width = 4 * self.rows, self.keep.shape[1]
        message = ((size + self.n_small, width), LOW)
        self.own, *messages, self.small = kernel_call(
            combine_kernel,
            [((size, width), jnp.float32)] + [message] * 3 + [((max(self.n_small, 16), width), LOW)],
            8, 1, "combine",
            self.keep, ordered(self.core, *earlier),
        )
        self.small = self.small[: self.n_small]
        self.plane = [over_dp(piece, 2 * i) for i, piece in enumerate(messages, 1)]

    def add(self, messages):
        (one, small_one), (two, small_two), (three, small_three) = map(self.split, messages)
        total = (self.own + up(one)) + (up(two) + up(three))
        small = (up(self.small) + up(small_one)) + (up(small_two) + up(small_three))
        return total, small

    def second(self, *earlier):
        line, small = self.add([ordered(message, *earlier) for message in self.plane])
        self.small = small.astype(LOW)
        size = self.rows
        self.own = line[:size]
        self.line = [
            over_tensor(self.message(line[i * size : (i + 1) * size], self.small), i)
            for i in (1, 2, 3)
        ]

    def result(self, *earlier):
        total, small = self.add([ordered(message, *earlier) for message in self.line])
        results, at = [], 0
        for width in self.widths:
            results.append(total[:, at : at + width])
            at += width
        return results, small


class PlainReduction:
    def __init__(self, grads, small=None):
        self.keep = self.core = grads[0]
        self.small = None if small is None else lax.psum(small, BOTH)
        self.parts = [
            lax.psum_scatter(
                lax.psum_scatter(grad, "dp", scatter_dimension=0, tiled=True),
                "tensor",
                scatter_dimension=1,
                tiled=True,
            )
            for grad in grads
        ]

    def first(self, *earlier):
        pass

    second = first

    def result(self, *earlier):
        return self.parts, self.small


def reduce_products(fast, sums, spots, us, small=None):
    if fast:
        extra = [] if small is None else [small]
        keep, send = grad_blocks(sums, extra, spots, us)
        widths = [right.shape[1] // 4 for products in sums for right in products[0][1]]
        return Reduction(keep, send, widths, sum(term.shape[0] for term in extra))
    grads = []
    for products in sums:
        for i in range(len(products[0][1])):
            grads.append(sum(dot_tn(left, rights[i]) for left, rights in products))
    return PlainReduction(grads, small)


def pick(array, index, axis):
    return lax.dynamic_index_in_dim(array, index, axis, keepdims=False)


def body(
    query_stream,
    token_stream,
    encoder_states,
    token_segment,
    token_rank,
    source_segment,
    query_map,
    key_map,
    value_map,
    merge_map,
    cross_query,
    cross_key,
    cross_value,
    cross_merge,
    expand_map,
    reduce_map,
    expand_bias,
    reduce_bias,
    gain_first,
    bias_first,
    gain_second,
    bias_second,
    gain_third,
    bias_third,
    cotangent,
    fast,
):
    rows, source_count = query_stream.shape[0], encoder_states.shape[0]
    me_dp, me_t = lax.axis_index("dp"), lax.axis_index("tensor")
    spots = jnp.stack([me_dp, me_t]).astype(jnp.int32)
    sequence, half = me_t // 2, me_t % 2

    groups = (
        (query_map, key_map, value_map),
        (merge_map, cross_query, cross_key, cross_value),
        (cross_merge, expand_map, reduce_map),
    )
    width, hidden = query_stream.shape[1], expand_bias.shape[0]
    vectors = (
        expand_bias, reduce_bias, gain_first, bias_first, gain_second, bias_second, gain_third, bias_third,
    )
    if fast:
        own_one, own_rest, table = load((groups[0], groups[1] + groups[2]), vectors, width)
        line_one = spread_line(own_one)
        far_tokens = over_tensor(token_stream, 1)
        near_one = spread_plane(line_one)
        line_rest = spread_line(ordered(own_rest, *line_one))
        gathered_one = join(near_one)
        far_source = over_tensor(ordered(encoder_states, far_tokens), 1)
        split_at = sum(block.shape[1] for block in groups[1])
    else:
        far_tokens = over_tensor(token_stream, 1)
        far_source = over_tensor(encoder_states, 1)
        gathered_one, gathered_two = gather_plain(groups[0]), gather_plain(groups[1])
        w_cmerge, w_expand, w_reduce = gather_plain(groups[2])

    def halves(row, size):
        return lax.dynamic_slice_in_dim(row, half * size, size), lax.dynamic_slice_in_dim(
            row, (1 - half) * size, size
        )

    segment_row = pick(token_segment, sequence, 0)
    starts_row = jnp.concatenate([jnp.ones((1,), jnp.bool_), segment_row[1:] != segment_row[:-1]])
    own_segment, far_segment = halves(segment_row, rows)
    own_rank, far_rank = halves(pick(token_rank, sequence, 0), rows)
    key_segment = jnp.concatenate([own_segment, far_segment])
    key_rank = jnp.concatenate([own_rank, far_rank])
    key_start = jnp.concatenate(halves(starts_row, rows))
    source_row = jnp.concatenate(halves(pick(source_segment, sequence, 0), source_count))
    self_allowed = (own_segment[None, :] == key_segment[:, None]) & (
        (key_rank[:, None] < own_rank[None, :]) | key_start[:, None]
    )
    cross_allowed = own_segment[None, :] == source_row[:, None]
    self_bias = jnp.where(self_allowed, 0.0, -1e30).astype(jnp.float32)
    cross_bias = jnp.where(cross_allowed, 0.0, -1e30).astype(jnp.float32)
    self_near = near_tiles(own_segment, key_segment, SELF_TILE)
    cross_near = near_tiles(own_segment, source_row, CROSS_TILE)

    table_rows = sum(vector.shape[0] for vector in vectors) // width
    if not fast:
        (table,) = kernel_call(
            table_kernel, [((table_rows, width), jnp.float32)], 2, 1, "table", *vectors
        )
    small_rows = table_rows + -table_rows % 16
    square, column = ((rows, width), jnp.float32), ((rows, 1), jnp.float32)
    low_square = ((rows, width), LOW)

    mixture, self_total, queries, self_sides, (w_query, w_key, w_value) = self_forward(
        fast, spots, self_near, self_bias, (query_stream, token_stream, far_tokens), gathered_one,
        SELF_TILE, 16,
    )
    self_set = (self_near, self_bias, queries, self_sides)
    if fast:
        line_rest = [ordered(piece, mixture) for piece in line_rest]
        near_two = spread_plane([piece[:, :split_at] for piece in line_rest])
        gathered_two = join([ordered(piece, far_source) for piece in near_two])
        near_three = spread_plane(
            [ordered(piece[:, split_at:], near_two[3]) for piece in line_rest]
        )
    cross_outs, source_sides, (w_merge, w_cquery, w_ckey, w_cvalue) = cross_forward(
        fast, spots, cross_near, cross_bias, mixture, query_stream, (encoder_states, far_source), table,
        gathered_two, CROSS_TILE, 22,
    )
    cross_mix, cross_total, cross_rows, first_normed, first_inverse, first_low = cross_outs
    cross_set = (cross_near, cross_bias, cross_rows, source_sides)
    if fast:
        gathered_three = join([ordered(piece, cross_mix) for piece in near_three])
        w_cmerge, w_expand, w_reduce = place(groups[2], gathered_three, spots)
    if fast:
        grads = [((2 * width, hidden // 2), LOW)] * 2
    else:
        grads = [((width, hidden), jnp.float32)] * 2
    hidden_states, third_grad, pre_grad, second_normed, second_inverse, small_one, *grads = kernel_call(
        functools.partial(hidden_kernel, fast),
        [low_square, square, ((rows, hidden), LOW), square, column, ((small_rows, width), jnp.float32), *grads],
        30, 13, "hidden",
        spots, cross_mix, w_cmerge, first_normed, table, w_expand, w_reduce, cotangent,
        scalars=1,
        scratch=[pltpu.VMEM((rows, hidden), LOW), pltpu.VMEM((rows, hidden), jnp.float32)],
    )
    if fast:
        hidden_sum = Reduction(*grads, [hidden // 4] * 2)
    else:
        hidden_sum = PlainReduction(grads)
    second_in_grad, cross_out, cross_mix_grad, small_two = kernel_call(
        hidden_back_kernel, [square, low_square, low_square, ((8, width), jnp.float32)], 16, 3, "hidden_back",
        third_grad, pre_grad, w_expand, second_normed, second_inverse, table, w_cmerge,
    )
    cross_set = (*cross_set, cross_mix_grad, cross_mix, cross_total, CROSS_TILE)
    hidden_sum.first(cross_mix_grad)
    part = attend_back_part(*cross_set, 0, 2, (), 11)
    cross_rows_grad, *source_grads = attend_back_part(*cross_set, 2, 2, part, 11)
    keys_near, keys_far, values_near, values_far = source_grads
    source_back = over_tensor(
        (dot_nt(keys_far, w_ckey) + dot_nt(values_far, w_cvalue)).astype(LOW), 1
    )
    if fast:
        cross_rows_grad = ordered(cross_rows_grad, *hidden_sum.plane)
    stream_grad, self_out, mixture_grad, packed = kernel_call(
        first_back_kernel, [square, low_square, low_square, ((small_rows, width), jnp.float32)], 12, 2, "first_back",
        second_in_grad, cross_rows_grad, w_cquery, first_normed, first_inverse, table, w_merge, small_one, small_two,
    )
    hidden_sum.second(self_out)
    cross_sum = reduce_products(
        fast,
        [
            [(first_low, [cross_rows_grad])],
            [
                (encoder_states, [keys_near, values_near]),
                (far_source, [keys_far, values_far]),
            ],
            [(cross_out, [cross_mix])],
            [(self_out, [mixture])],
        ],
        spots,
        5,
        packed,
    )
    mixture_grad = ordered(mixture_grad, cross_sum.core)
    cross_sum.first()
    self_set = (*self_set, mixture_grad, mixture, self_total, SELF_TILE)
    part = attend_back_part(*self_set, 0, 2, (), 9)
    queries_grad, *token_grads = attend_back_part(*self_set, 2, 2, part, 9)
    if fast:
        queries_grad = ordered(queries_grad, source_back, *hidden_sum.line, *cross_sum.plane)
    source_sum = dot_nt(ordered(keys_near, queries_grad), w_ckey) + dot_nt(values_near, w_cvalue)
    keys_near, keys_far, values_near, values_far = token_grads
    self_sum = reduce_products(
        fast,
        [
            [(query_stream, [queries_grad])],
            [
                (token_stream, [keys_near, values_near]),
                (far_tokens, [keys_far, values_far]),
            ],
        ],
        spots,
        3,
    )
    keys_far = ordered(keys_far, self_sum.keep)
    token_back = over_tensor(
        (dot_nt(keys_far, w_key) + dot_nt(values_far, w_value)).astype(LOW), 1
    )
    token_sum = dot_nt(keys_near, w_key) + dot_nt(values_near, w_value)
    self_sum.first()
    cross_sum.second(self_sum.own if fast else self_sum.keep)
    self_sum.second()
    (expand_part, reduce_part), _ = hidden_sum.result(queries_grad)
    (*cross_parts, merge_part), summed = cross_sum.result()
    self_parts, _ = self_sum.result()
    summed = summed[:, :width].reshape(-1)
    small, at = [], 0
    for vector in vectors:
        small.append(summed[at : at + vector.shape[0]])
        at += vector.shape[0]
    return (
        hidden_states,
        (stream_grad + dot_nt(queries_grad, w_query)).astype(LOW),
        (token_sum + up(token_back)).astype(LOW),
        (source_sum + up(ordered(source_back, queries_grad))).astype(LOW),
        *self_parts,
        merge_part,
        *cross_parts,
        expand_part,
        reduce_part,
        *small,
    )


def solution(mesh):
    fast = mesh.shape["dp"] == 8 and mesh.shape["tensor"] == 4
    rows = P(BOTH, None)
    block = P("dp", "tensor")

    def program(*arguments):
        return body(*arguments, fast)

    return jax.shard_map(
        program,
        mesh=mesh,
        in_specs=(rows,) * 3 + (P("dp", None),) * 3 + (block,) * 10 + (P(),) * 8 + (rows,),
        out_specs=(rows,) * 4 + (block,) * 10 + (P(),) * 8,
        check_vma=False,
    )
```

```python
import functools

import jax
import jax.numpy as jnp
from jax import lax
from jax.sharding import PartitionSpec as P
from jax.experimental import pallas as pl
from jax.experimental.pallas import tpu as pltpu

EPSILON = 1e-05
GATE = 0.7978845608028654
CUBIC = 0.044715
LOG2E = 1.4426950408889634
UNIT = 128
PAIR = 128
TILE = 256
BOTH = ("dp", "tensor")
ANY = pl.BlockSpec(memory_space=pl.ANY)
WHOLE = pl.BlockSpec(memory_space=pltpu.VMEM)
SCALARS = pl.BlockSpec(memory_space=pltpu.SMEM)
LOW = jnp.bfloat16


def params(mib):
    return pltpu.CompilerParams(vmem_limit_bytes=mib * 1024 * 1024)


def lasting(us):
    return pl.CostEstimate(flops=int(us * 1.1e7), bytes_accessed=0, transcendentals=0)


def far_memory(value):
    return pltpu.with_memory_space_constraint(value, pltpu.HBM)


def up(value):
    return value.astype(jnp.float32)


def dot_nn(a, b):
    return lax.dot_general(a, b, (((1,), (0,)), ((), ())), preferred_element_type=jnp.float32)


def dot_nt(a, b):
    return lax.dot_general(a, b, (((1,), (1,)), ((), ())), preferred_element_type=jnp.float32)


def dot_tn(a, b):
    return lax.dot_general(a, b, (((0,), (0,)), ((), ())), preferred_element_type=jnp.float32)


REDUCE_BIAS, GAIN_ONE, BIAS_ONE, GAIN_TWO, BIAS_TWO, GAIN_THREE, BIAS_THREE = range(-7, 0)


def norm_rows(matrix):
    centred = matrix - jnp.mean(matrix, -1, keepdims=True)
    inverse = lax.rsqrt(jnp.mean(centred * centred, -1, keepdims=True) + EPSILON)
    return centred * inverse, inverse


def norm_back(outer_grad, normed, inverse, gains):
    spread = outer_grad * gains
    return inverse * (
        spread
        - jnp.mean(spread, -1, keepdims=True)
        - normed * jnp.mean(spread * normed, -1, keepdims=True)
    )


def down(matrix):
    return jnp.sum(matrix, 0, keepdims=True)


def table_row(table_ref, row):
    row += table_ref.shape[0]
    return table_ref[row : row + 1]


def hidden_kernel(
    fast, spots_ref, mix_ref, merge_ref, first_ref, table_ref, expand_ref, reduce_ref, cotangent_ref, *refs
):
    states_ref, third_ref, pre_ref, normed_ref, inverse_ref, small_ref, *grads = refs[:8]
    active_ref, slope_ref = refs[8:]
    row = functools.partial(table_row, table_ref)
    first_out = first_ref[...] * row(GAIN_ONE) + row(BIAS_ONE)
    normed, inverse = norm_rows(first_out + dot_nt(mix_ref[...], merge_ref[...]))
    normed_ref[...] = normed
    inverse_ref[...] = inverse
    second_out = normed * row(GAIN_TWO) + row(BIAS_TWO)
    second_low = second_out.astype(LOW)
    width = mix_ref.shape[1]
    chunks = expand_ref.shape[1] // width
    output = second_out + row(REDUCE_BIAS)
    for c in range(chunks):
        columns = slice(c * width, (c + 1) * width)
        x = dot_nn(second_low, expand_ref[:, columns]) + table_ref[c : c + 1]
        square = x * x
        bent = jnp.tanh(x * (GATE + (GATE * CUBIC) * square))
        halved = 0.5 + 0.5 * bent
        active = (x * halved).astype(LOW)
        slope_ref[:, columns] = halved + (0.5 * x) * (1.0 - bent * bent) * (
            GATE + (3.0 * GATE * CUBIC) * square
        )
        active_ref[:, columns] = active
        output = output + dot_nt(active, reduce_ref[:, columns])
    normed, inverse = norm_rows(output)
    states_ref[...] = (normed * row(GAIN_THREE) + row(BIAS_THREE)).astype(LOW)
    outer = up(cotangent_ref[...])
    third = norm_back(outer, normed, inverse, row(GAIN_THREE))
    third_ref[...] = third
    output_grad = third.astype(LOW)
    small_ref[...] = jnp.zeros(small_ref.shape, jnp.float32)
    at = table_ref.shape[0]
    small_ref[at + GAIN_THREE : at + GAIN_THREE + 1] = down(outer * normed)
    small_ref[at + BIAS_THREE : at + BIAS_THREE + 1] = down(outer)
    small_ref[at + REDUCE_BIAS : at + REDUCE_BIAS + 1] = down(up(output_grad))
    for c in range(chunks):
        columns = slice(c * width, (c + 1) * width)
        pre_grad = (dot_nn(output_grad, reduce_ref[:, columns]) * slope_ref[:, columns]).astype(LOW)
        pre_ref[:, columns] = pre_grad
        small_ref[c : c + 1] = down(up(pre_grad))
        parts = (dot_tn(second_low, pre_grad), dot_tn(output_grad, active_ref[:, columns]))
        for i, part in enumerate(parts):
            if fast:
                store_blocks(spots_ref, *grads, part.astype(LOW), (c,), i * width)
            else:
                grads[i][:, columns] = part


def hidden_back_kernel(
    third_ref, pre_ref, expand_ref, normed_ref, inverse_ref, table_ref, merge_ref, *refs
):
    inner_ref, low_ref, mix_ref, small_ref = refs
    normed = normed_ref[...]
    outer = third_ref[...] + dot_nt(pre_ref[...], expand_ref[...])
    inner = norm_back(outer, normed, inverse_ref[...], table_row(table_ref, GAIN_TWO))
    inner_ref[...] = inner
    low = inner.astype(LOW)
    low_ref[...] = low
    mix_ref[...] = dot_nn(low, merge_ref[...]).astype(LOW)
    small_ref[0:1] = down(outer * normed)
    small_ref[1:2] = down(outer)


def first_back_kernel(
    second_ref, rows_ref, query_ref, normed_ref, inverse_ref, table_ref, merge_ref, one_ref, two_ref, *refs
):
    inner_ref, low_ref, mix_ref, small_ref = refs
    normed = normed_ref[...]
    outer = second_ref[...] + dot_nt(rows_ref[...], query_ref[...])
    inner = norm_back(outer, normed, inverse_ref[...], table_row(table_ref, GAIN_ONE))
    inner_ref[...] = inner
    low = inner.astype(LOW)
    low_ref[...] = low
    mix_ref[...] = dot_nn(low, merge_ref[...]).astype(LOW)
    at = table_ref.shape[0]
    small_ref[...] = one_ref[...]
    small_ref[at + GAIN_TWO : at + BIAS_TWO + 1] = two_ref[0:2]
    small_ref[at + GAIN_ONE : at + GAIN_ONE + 1] = down(outer * normed)
    small_ref[at + BIAS_ONE : at + BIAS_ONE + 1] = down(outer)


def kernel_call(kernel, outs, mib, us, name, *operands, scalars=0, scratch=()):
    return pl.pallas_call(
        kernel,
        out_shape=[jax.ShapeDtypeStruct(*out) for out in outs],
        in_specs=[SCALARS] * scalars + [WHOLE] * (len(operands) - scalars),
        out_specs=[WHOLE] * len(outs),
        scratch_shapes=list(scratch),
        compiler_params=params(mib),
        cost_estimate=lasting(us),
        name=name,
    )(*operands)


def split_heads(rows):
    lane = lax.broadcasted_iota(jnp.int32, rows.shape, 1)
    zero = jnp.zeros_like(rows)
    return jnp.concatenate(
        [jnp.where(lane < PAIR // 2, rows, zero), jnp.where(lane < PAIR // 2, zero, rows)], 0
    )


def twice(row):
    return jnp.concatenate([row, row], 1)


def pair_columns(count):
    return [slice(p * PAIR, (p + 1) * PAIR) for p in range(count)]


def attend_all(near_ref, bias_ref, q_ref, sides, out_ref, lse_ref, scratch):
    k_near, k_far, v_near, v_far = sides
    turned, stacked, top, total, acc = scratch
    nq, nk = q_ref.shape[0] // TILE, k_near.shape[0] // TILE
    half = PAIR // 2
    columns = pair_columns(stacked.shape[0])
    for p, pair in enumerate(columns):
        turned[p, 0] = v_near[:, pair].T
        turned[p, 1] = v_far[:, pair].T
    for i in range(nq):
        q_rows = slice(i * TILE, (i + 1) * TILE)
        for p, pair in enumerate(columns):
            stacked[p] = split_heads(q_ref[q_rows, pair])
        top[...] = jnp.full(top.shape, -3e30, jnp.float32)
        total[...] = jnp.zeros(total.shape, jnp.float32)
        acc[...] = jnp.zeros(acc.shape, jnp.float32)
        for j in range(2 * nk):

            @pl.when(near_ref[i, j] != 0)
            def _(j=j, q_rows=q_rows):
                k_ref = k_far if j >= nk else k_near
                k_rows = slice(j % nk * TILE, (j % nk + 1) * TILE)
                bias = twice(bias_ref[j * TILE : (j + 1) * TILE, q_rows])
                products = [dot_nt(k_ref[k_rows, pair], stacked[p]) for p, pair in enumerate(columns)]
                for p, product in enumerate(products):
                    scores = product + bias
                    old = top[p]
                    peak = jnp.maximum(old, jnp.max(scores, 0, keepdims=True))
                    fade = jnp.exp2((old - peak) * LOG2E)
                    powers = jnp.exp2((scores - peak) * LOG2E)
                    top[p] = peak
                    total[p] = total[p] * fade + jnp.sum(powers, 0, keepdims=True)
                    acc[p] = acc[p] * fade + dot_nn(
                        turned[p, j // nk, :, k_rows], powers.astype(LOW)
                    )

        for p, pair in enumerate(columns):
            full = total[p]
            scaled = acc[p] * (1.0 / full)
            mixed = jnp.concatenate([scaled[:half, :TILE], scaled[half:, TILE:]], 0)
            out_ref[q_rows, pair] = mixed.T.astype(LOW)
            log_total = top[p] * LOG2E + jnp.log2(full)
            lse_ref[p, 0:1, q_rows] = log_total[:, :TILE]
            lse_ref[p, 1:2, q_rows] = log_total[:, TILE:]


def attend_scratch(pairs, lk):
    return [
        pltpu.VMEM((pairs, 2, PAIR, lk), LOW),
        pltpu.VMEM((pairs, 2 * TILE, PAIR), LOW),
        pltpu.VMEM((pairs, 1, 2 * TILE), jnp.float32),
        pltpu.VMEM((pairs, 1, 2 * TILE), jnp.float32),
        pltpu.VMEM((pairs, PAIR, 2 * TILE), jnp.float32),
    ]


def place_whole(spots_ref, pieces, out, at):
    me_dp, me_t = spots_ref[0], spots_ref[1]
    rows = pieces[0].shape[2]
    for piece, (dp_flips, t_flips) in zip(pieces, PIECES):
        for a, dp_flip in enumerate(dp_flips):
            row = pl.multiple_of(jnp.bitwise_xor(me_dp, dp_flip) * rows, rows)
            for b, t_flip in enumerate(t_flips):
                column = pl.multiple_of(jnp.bitwise_xor(me_t, t_flip) * PAIR, PAIR)
                out[pl.ds(row, rows), pl.ds(column, PAIR)] = piece[a, b, :, at : at + PAIR]


class Copies:
    def __init__(self, held, outs, sems):
        self.copies = [
            pltpu.make_async_copy(one, out, sems.at[i]) for i, (one, out) in enumerate(zip(held, outs))
        ]

    def start(self, *which):
        for i in which:
            self.copies[i].start()

    def wait(self):
        for copy in self.copies:
            copy.wait()


def self_kernel(
    fast, spots_ref, near_ref, bias_ref, query_ref, token_ref, far_ref, *refs
):
    cut = 2 if fast else 3
    n = 8 if fast else 5
    gathered, (out_ref, lse_ref), outs = refs[:cut], refs[cut : cut + 2], refs[cut + 2 : cut + 2 + n]
    scratch = refs[cut + 2 + n :]
    held, sems, scratch = scratch[:n], scratch[n], scratch[n + 1 :]
    copies = Copies(held, outs, sems)
    q_ref, sides, weights = held[0], held[1:5], held[5:]
    if fast:
        for i, weight in enumerate(weights):
            place_whole(spots_ref, gathered, weight, i * PAIR)
        copies.start(5, 6, 7)
    else:
        weights = gathered
    w_query, w_key, w_value = (weight[...] for weight in weights)
    q_ref[...] = (dot_nn(query_ref[...], w_query) * 0.125).astype(LOW)
    for i, (rows, weight) in enumerate(
        ((token_ref, w_key), (far_ref, w_key), (token_ref, w_value), (far_ref, w_value))
    ):
        sides[i][...] = dot_nn(rows[...], weight).astype(LOW)
    copies.start(0, 1, 2, 3, 4)
    attend_all(near_ref, bias_ref, q_ref, sides, out_ref, lse_ref, scratch)
    copies.wait()


def self_forward(fast, spots, near, bias, streams, gathered, us):
    lq, width = streams[0].shape
    lk, pairs = streams[1].shape[0], width // PAIR
    rows, keys, square = (((n, width), LOW) for n in (lq, lk, width))
    kept = [rows] + [keys] * 4 + ([square] * 3 if fast else [])
    results = pl.pallas_call(
        functools.partial(self_kernel, fast),
        in_specs=[SCALARS, SCALARS] + [WHOLE] * (4 + len(gathered)),
        out_specs=[WHOLE, WHOLE] + [ANY] * len(kept),
        out_shape=[
            jax.ShapeDtypeStruct(*rows),
            jax.ShapeDtypeStruct((pairs, 2, lq), jnp.float32),
            *(pltpu.HBM(*out) for out in kept),
        ],
        scratch_shapes=[pltpu.VMEM(*out) for out in kept]
        + [pltpu.SemaphoreType.DMA((len(kept),))]
        + attend_scratch(pairs, lk),
        compiler_params=params(24),
        cost_estimate=lasting(us),
        name="self_forward",
    )(spots, near, bias, *map(far_memory, streams), *gathered)
    mixture, lse, queries = results[:3]
    return mixture, lse, queries, results[3:7], results[7:] if fast else gathered


def cross_kernel(
    fast, spots_ref, near_ref, bias_ref, mix_ref, stream_ref, near_rows, far_rows, table_ref, *refs
):
    cut = 2 if fast else 4
    n = 12 if fast else 8
    gathered, (out_ref, lse_ref), outs = refs[:cut], refs[cut : cut + 2], refs[cut + 2 : cut + 2 + n]
    scratch = refs[cut + 2 + n :]
    held, sems, scratch = scratch[:n], scratch[n], scratch[n + 1 :]
    copies = Copies(held, outs, sems)
    rows_ref, normed_ref, inverse_ref, low_ref = held[:4]
    sides, weights = held[4:8], held[8:]
    if fast:
        for i, weight in enumerate(weights):
            place_whole(spots_ref, gathered, weight, i * PAIR)
        copies.start(8, 9, 10, 11)
    else:
        weights = gathered
    w_merge, w_query, w_key, w_value = weights
    normed, inverse = norm_rows(up(stream_ref[...]) + dot_nt(mix_ref[...], w_merge[...]))
    normed_ref[...] = normed
    inverse_ref[...] = inverse
    low = (normed * table_row(table_ref, GAIN_ONE) + table_row(table_ref, BIAS_ONE)).astype(LOW)
    low_ref[...] = low
    rows_ref[...] = (dot_nn(low, w_query[...]) * 0.125).astype(LOW)
    for i, (rows, weight) in enumerate(
        ((near_rows, w_key), (far_rows, w_key), (near_rows, w_value), (far_rows, w_value))
    ):
        sides[i][...] = dot_nn(rows[...], weight[...]).astype(LOW)
    copies.start(0, 1, 2, 3, 4, 5, 6, 7)
    attend_all(near_ref, bias_ref, rows_ref, sides, out_ref, lse_ref, scratch)
    copies.wait()


def cross_forward(fast, spots, near, bias, mixture, stream, sources, table, gathered, us):
    lq, width = mixture.shape
    lk, pairs = sources[0].shape[0], width // PAIR
    rows, keys, square = (((n, width), LOW) for n in (lq, lk, width))
    kept = [rows, ((lq, width), jnp.float32), ((lq, 1), jnp.float32), rows] + [keys] * 4
    if fast:
        kept += [square] * 4
    results = pl.pallas_call(
        functools.partial(cross_kernel, fast),
        in_specs=[SCALARS, SCALARS] + [WHOLE] * (6 + len(gathered)),
        out_specs=[WHOLE, WHOLE] + [ANY] * len(kept),
        out_shape=[
            jax.ShapeDtypeStruct(*rows),
            jax.ShapeDtypeStruct((pairs, 2, lq), jnp.float32),
            *(pltpu.HBM(*out) for out in kept),
        ],
        scratch_shapes=[pltpu.VMEM(*out) for out in kept]
        + [pltpu.SemaphoreType.DMA((len(kept),))]
        + attend_scratch(pairs, lk),
        compiler_params=params(30),
        cost_estimate=lasting(us),
        name="cross_forward",
    )(spots, near, bias, mixture, far_memory(stream), *map(far_memory, sources), table, *gathered)
    return results[:6], results[6:10], results[10:] if fast else gathered


def backward_kernel(near_ref, bias_ref, q_ref, m_ref, o_ref, lse_ref, *refs):
    k_near, k_far, v_near, v_far, dq_ref, *outs = refs[:9]
    stacked, grads, delta, log_total, dq_acc, dk_acc, dv_acc = refs[9:]
    nq, nk = q_ref.shape[0] // TILE, k_near.shape[0] // TILE
    half = PAIR // 2
    columns = pair_columns(stacked.shape[0])
    dk_acc[...] = jnp.zeros(dk_acc.shape, jnp.float32)
    dv_acc[...] = jnp.zeros(dv_acc.shape, jnp.float32)
    for i in range(nq):
        q_rows = slice(i * TILE, (i + 1) * TILE)
        for p, pair in enumerate(columns):
            stacked[p] = split_heads(q_ref[q_rows, pair])
            grads[p] = split_heads(m_ref[q_rows, pair])
            turned = (up(m_ref[q_rows, pair]) * up(o_ref[q_rows, pair])).T
            delta[p] = jnp.concatenate([down(turned[:half]), down(turned[half:])], 1)
            log_total[p] = jnp.concatenate([lse_ref[p, 0:1, q_rows], lse_ref[p, 1:2, q_rows]], 1)
        dq_acc[...] = jnp.zeros(dq_acc.shape, jnp.float32)
        for j in range(2 * nk):

            @pl.when(near_ref[i, j] != 0)
            def _(j=j, q_rows=q_rows):
                k_ref, v_ref = (k_far, v_far) if j >= nk else (k_near, v_near)
                k_rows = slice(j % nk * TILE, (j % nk + 1) * TILE)
                all_rows = slice(j * TILE, (j + 1) * TILE)
                bias = twice(bias_ref[all_rows, q_rows])
                scores = [dot_nt(k_ref[k_rows, pair], stacked[p]) for p, pair in enumerate(columns)]
                outer = [dot_nt(v_ref[k_rows, pair], grads[p]) for p, pair in enumerate(columns)]
                for p, pair in enumerate(columns):
                    weights = jnp.exp2(scores[p] * LOG2E + (bias - log_total[p]))
                    slope = (weights * (outer[p] - delta[p])).astype(LOW)
                    dv_acc[p, all_rows] += dot_nn(weights.astype(LOW), grads[p])
                    dk_acc[p, all_rows] += dot_nn(slope, stacked[p])
                    dq_acc[p] += dot_tn(slope, k_ref[k_rows, pair])

        lane = lax.broadcasted_iota(jnp.int32, (TILE, PAIR), 1)
        for p, pair in enumerate(columns):
            dq_ref[q_rows, pair] = (
                jnp.where(lane < half, dq_acc[p, :TILE], dq_acc[p, TILE:]) * 0.125
            ).astype(LOW)
    size = k_near.shape[0]
    for out, acc, side in zip(outs, (dk_acc, dk_acc, dv_acc, dv_acc), (0, 1, 0, 1)):
        for p, pair in enumerate(columns):
            out[:, pair] = acc[p, side * size : (side + 1) * size].astype(LOW)


def attend_back(near, bias, queries, sides, outer, mixed, lse, us):
    lq, width = queries.shape
    lk, pairs, wide = sides[0].shape[0], 2, 2 * PAIR
    column = lambda p: (0, p)
    q_spec, k_spec = pl.BlockSpec((lq, wide), column), pl.BlockSpec((lk, wide), column)
    return pl.pallas_call(
        backward_kernel,
        grid=(width // wide,),
        in_specs=[SCALARS, WHOLE, q_spec, q_spec, q_spec]
        + [pl.BlockSpec((pairs, 2, lq), lambda p: (p, 0, 0))]
        + [k_spec] * 4,
        out_specs=[q_spec] + [k_spec] * 4,
        out_shape=[jax.ShapeDtypeStruct((lq, width), LOW)]
        + [jax.ShapeDtypeStruct((lk, width), LOW)] * 4,
        scratch_shapes=[
            pltpu.VMEM((pairs, 2 * TILE, PAIR), LOW),
            pltpu.VMEM((pairs, 2 * TILE, PAIR), LOW),
            pltpu.VMEM((pairs, 1, 2 * TILE), jnp.float32),
            pltpu.VMEM((pairs, 1, 2 * TILE), jnp.float32),
            pltpu.VMEM((pairs, 2 * TILE, PAIR), jnp.float32),
            pltpu.VMEM((pairs, 2 * lk, PAIR), jnp.float32),
            pltpu.VMEM((pairs, 2 * lk, PAIR), jnp.float32),
        ],
        compiler_params=params(26),
        cost_estimate=lasting(us),
        name="attend_back",
    )(near, bias, queries, outer, mixed, lse, *sides)


def near_tiles(own, keys):
    own, keys = own.reshape(-1, TILE), keys.reshape(-1, TILE)
    return (
        (keys.min(1)[None] <= own.max(1)[:, None]) & (keys.max(1)[None] >= own.min(1)[:, None])
    ).astype(jnp.int32)


def over_dp(matrix, flip):
    return lax.ppermute(matrix, "dp", [(i, i ^ flip) for i in range(8)])


def over_tensor(matrix, flip):
    return lax.ppermute(matrix, "tensor", [(i, i ^ flip) for i in range(4)])


def ordered(value, *earlier):
    return lax.optimization_barrier((value, *earlier))[0] if earlier else value


PIECES = (((0, 2, 4, 6), (0, 1, 2, 3)), ((1, 3, 5, 7), (0, 1, 2, 3)))


def place_kernel(counts, spots_ref, *refs):
    n = len(counts)
    pieces, outs = refs[:-n], refs[-n:]
    me_dp, me_t = spots_ref[0], spots_ref[1]
    rows = pieces[0].shape[2]
    for piece, (dp_flips, t_flips) in zip(pieces, PIECES):
        for a, dp_flip in enumerate(dp_flips):
            row = pl.multiple_of(jnp.bitwise_xor(me_dp, dp_flip) * rows, rows)
            for b, t_flip in enumerate(t_flips):
                t = jnp.bitwise_xor(me_t, t_flip)
                at = 0
                for out, count in zip(outs, counts):
                    size = count * UNIT
                    column = pl.multiple_of(t * size, UNIT)
                    out[pl.ds(row, rows), pl.ds(column, size)] = piece[a, b, :, at : at + size]
                    at += size


def load_kernel(counts, *refs):
    n, n_vectors = sum(counts), 8
    blocks, vectors = list(refs[:n]), refs[n : n + n_vectors]
    outs, held, sems = refs[n + n_vectors : -2], refs[-2], refs[-1]
    copies = []

    def copy(source, target):
        copies.append(pltpu.make_async_copy(source, target, sems.at[len(copies)]))
        copies[-1].start()

    for out, count in zip(outs, counts):
        at = 0
        for _ in range(count):
            block = blocks.pop(0)
            copy(block, out.at[:, at : at + block.shape[1]])
            at += block.shape[1]
    at = 0
    for vector in vectors:
        copy(vector, held.at[at : at + vector.shape[0]])
        at += vector.shape[0]
    for one in copies:
        one.wait()
    table = outs[-1]
    width = table.shape[1]
    for i in range(table.shape[0]):
        table[i : i + 1] = up(held[i * width : (i + 1) * width]).reshape(1, width)


def load(groups, vectors, width):
    blocks = [block for group in groups for block in group]
    total = sum(vector.shape[0] for vector in vectors)
    return pl.pallas_call(
        functools.partial(load_kernel, [len(group) for group in groups]),
        out_shape=[
            jax.ShapeDtypeStruct((group[0].shape[0], sum(block.shape[1] for block in group)), LOW)
            for group in groups
        ]
        + [jax.ShapeDtypeStruct((total // width, width), jnp.float32)],
        in_specs=[ANY] * (len(blocks) + len(vectors)),
        out_specs=[WHOLE] * (len(groups) + 1),
        scratch_shapes=[
            pltpu.VMEM((total,), LOW),
            pltpu.SemaphoreType.DMA((len(blocks) + len(vectors),)),
        ],
        compiler_params=params(4),
        name="load",
    )(*map(far_memory, blocks), *map(far_memory, vectors))


def table_kernel(*refs):
    *vectors, out = refs
    width, at = out.shape[1], 0
    for vector in vectors:
        row = up(vector[...])
        for i in range(vector.shape[0] // width):
            out[at : at + 1] = row[i * width : (i + 1) * width].reshape(1, width)
            at += 1


def combine_kernel(keep_ref, core_ref, *outs):
    own, *messages, small = outs
    size = own.shape[0]
    n_small = keep_ref.shape[0] - 4 * size
    if n_small:
        total = (up(keep_ref[4 * size :]) + up(core_ref[4 * size :])).astype(LOW)
        small[...] = total
    own[...] = up(keep_ref[:size]) + up(core_ref[:size])
    for i, message in enumerate(messages, 1):
        rows = slice(i * size, (i + 1) * size)
        message[:size] = (up(keep_ref[rows]) + up(core_ref[rows])).astype(LOW)
        if n_small:
            message[size:] = total


def spread_line(own):
    return [own] + [over_tensor(own, flip) for flip in (1, 2, 3)]


def spread_plane(line):
    line = jnp.stack(line)
    return [line] + [over_dp(line, flip) for flip in (2, 4, 6)]


def join(near):
    near = jnp.stack(near)
    return [near, over_dp(near, 1)]


def place(blocks, pieces, spots):
    counts = [block.shape[1] // UNIT for block in blocks]
    rows = blocks[0].shape[0]
    outs = [((8 * rows, 4 * count * UNIT), LOW) for count in counts]
    return kernel_call(
        functools.partial(place_kernel, counts), outs, 18, 1, "place", spots, *pieces, scalars=1
    )


def gather_plain(blocks):
    return [
        lax.all_gather(
            lax.all_gather(block, "dp", axis=0, tiled=True), "tensor", axis=1, tiled=True
        )
        for block in blocks
    ]


def store_blocks(spots_ref, keep_ref, send_ref, full, ts, at):
    me_dp, me_t = spots_ref[0], spots_ref[1]
    rows, size = full.shape[0] // 8, full.shape[1] // len(ts)

    def store(flipped):
        for d in range(8):
            target = send_ref if (d % 2) != flipped else keep_ref
            near = jnp.bitwise_xor(me_dp, d) // 2
            for i, t in enumerate(ts):
                row = pl.multiple_of((near * 4 + jnp.bitwise_xor(me_t, t)) * rows, rows)
                target[pl.ds(row, rows), at : at + size] = full[
                    d * rows : (d + 1) * rows, i * size : (i + 1) * size
                ]

    pl.when(me_dp % 2 == 0)(functools.partial(store, 0))
    pl.when(me_dp % 2 == 1)(functools.partial(store, 1))


def grad_kernel(layout, n_small, spots_ref, *refs):
    keep_ref, send_ref = refs[-2:]
    refs = list(refs[:-2])
    if n_small:
        small = refs.pop()[...].astype(LOW)
        used = small.shape[1]
        for target in (keep_ref, send_ref):
            target[-n_small:] = jnp.zeros((n_small, target.shape[1]), LOW)
            target[-n_small:, :used] = small
    at = 0
    for n_products, n_right in layout:
        full = None
        for _ in range(n_products):
            left = refs.pop(0)[...]
            right = [refs.pop(0)[...] for _ in range(n_right)]
            product = dot_tn(left, jnp.concatenate(right, 1) if n_right > 1 else right[0])
            full = product if full is None else full + product
        full = full.astype(LOW)
        width = full.shape[1] // n_right
        for i in range(n_right):
            part = full[:, i * width : (i + 1) * width]
            store_blocks(spots_ref, keep_ref, send_ref, part, range(4), at)
            at += width // 4


def grad_blocks(sums, small, spots, us):
    layout = [(len(products), len(products[0][1])) for products in sums]
    rows = 2 * sums[0][0][0].shape[1]
    n_small = sum(term.shape[0] for term in small)
    width = sum(right.shape[1] for products in sums for right in products[0][1])
    operands = [
        matrix for products in sums for left, rights in products for matrix in (left, *rights)
    ]
    out = ((rows + n_small, width // 4), LOW)
    return kernel_call(
        functools.partial(grad_kernel, layout, n_small),
        [out, out],
        28,
        us,
        "grads",
        spots,
        *operands,
        *small,
        scalars=1,
    )


class Reduction:
    def __init__(self, keep, send, widths, n_small=0):
        self.keep, self.widths, self.n_small = keep, widths, n_small
        self.rows = (keep.shape[0] - n_small) // 16
        self.core = over_dp(send, 1)

    def split(self, matrix):
        cut = matrix.shape[0] - self.n_small
        return matrix[:cut], matrix[cut:]

    def message(self, blocks, small):
        return jnp.concatenate([blocks.astype(LOW), small], 0) if self.n_small else blocks.astype(LOW)

    def first(self, *earlier):
        size, width = 4 * self.rows, self.keep.shape[1]
        message = ((size + self.n_small, width), LOW)
        self.own, *messages, self.small = kernel_call(
            combine_kernel,
            [((size, width), jnp.float32)] + [message] * 3 + [((max(self.n_small, 16), width), LOW)],
            8, 1, "combine",
            self.keep, ordered(self.core, *earlier),
        )
        self.small = self.small[: self.n_small]
        self.plane = [over_dp(piece, 2 * i) for i, piece in enumerate(messages, 1)]

    def add(self, messages):
        (one, small_one), (two, small_two), (three, small_three) = map(self.split, messages)
        total = (self.own + up(one)) + (up(two) + up(three))
        small = (up(self.small) + up(small_one)) + (up(small_two) + up(small_three))
        return total, small

    def second(self, *earlier):
        line, small = self.add([ordered(message, *earlier) for message in self.plane])
        self.small = small.astype(LOW)
        size = self.rows
        self.own = line[:size]
        self.line = [
            over_tensor(self.message(line[i * size : (i + 1) * size], self.small), i)
            for i in (1, 2, 3)
        ]

    def result(self, *earlier):
        total, small = self.add([ordered(message, *earlier) for message in self.line])
        results, at = [], 0
        for width in self.widths:
            results.append(total[:, at : at + width])
            at += width
        return results, small


class PlainReduction:
    def __init__(self, grads, small=None):
        self.keep = self.core = grads[0]
        self.small = None if small is None else lax.psum(small, BOTH)
        self.parts = [
            lax.psum_scatter(
                lax.psum_scatter(grad, "dp", scatter_dimension=0, tiled=True),
                "tensor",
                scatter_dimension=1,
                tiled=True,
            )
            for grad in grads
        ]

    def first(self, *earlier):
        pass

    second = first

    def result(self, *earlier):
        return self.parts, self.small


def reduce_products(fast, sums, spots, us, small=None):
    if fast:
        extra = [] if small is None else [small]
        keep, send = grad_blocks(sums, extra, spots, us)
        widths = [right.shape[1] // 4 for products in sums for right in products[0][1]]
        return Reduction(keep, send, widths, sum(term.shape[0] for term in extra))
    grads = []
    for products in sums:
        for i in range(len(products[0][1])):
            grads.append(sum(dot_tn(left, rights[i]) for left, rights in products))
    return PlainReduction(grads, small)


def pick(array, index, axis):
    return lax.dynamic_index_in_dim(array, index, axis, keepdims=False)


def body(
    query_stream,
    token_stream,
    encoder_states,
    token_segment,
    token_rank,
    source_segment,
    query_map,
    key_map,
    value_map,
    merge_map,
    cross_query,
    cross_key,
    cross_value,
    cross_merge,
    expand_map,
    reduce_map,
    expand_bias,
    reduce_bias,
    gain_first,
    bias_first,
    gain_second,
    bias_second,
    gain_third,
    bias_third,
    cotangent,
    fast,
):
    rows, source_count = query_stream.shape[0], encoder_states.shape[0]
    me_dp, me_t = lax.axis_index("dp"), lax.axis_index("tensor")
    spots = jnp.stack([me_dp, me_t]).astype(jnp.int32)
    sequence, half = me_t // 2, me_t % 2

    groups = (
        (query_map, key_map, value_map),
        (merge_map, cross_query, cross_key, cross_value),
        (cross_merge, expand_map, reduce_map),
    )
    width, hidden = query_stream.shape[1], expand_bias.shape[0]
    vectors = (
        expand_bias, reduce_bias, gain_first, bias_first, gain_second, bias_second, gain_third, bias_third,
    )
    if fast:
        own_one, own_rest, table = load((groups[0], groups[1] + groups[2]), vectors, width)
        line_one = spread_line(own_one)
        far_tokens = over_tensor(token_stream, 1)
        near_one = spread_plane(line_one)
        line_rest = spread_line(ordered(own_rest, *line_one))
        gathered_one = join(near_one)
        far_source = over_tensor(ordered(encoder_states, far_tokens), 1)
        split_at = sum(block.shape[1] for block in groups[1])
    else:
        far_tokens = over_tensor(token_stream, 1)
        far_source = over_tensor(encoder_states, 1)
        gathered_one, gathered_two = gather_plain(groups[0]), gather_plain(groups[1])
        w_cmerge, w_expand, w_reduce = gather_plain(groups[2])

    def halves(row, size):
        return lax.dynamic_slice_in_dim(row, half * size, size), lax.dynamic_slice_in_dim(
            row, (1 - half) * size, size
        )

    segment_row = pick(token_segment, sequence, 0)
    starts_row = jnp.concatenate([jnp.ones((1,), jnp.bool_), segment_row[1:] != segment_row[:-1]])
    own_segment, far_segment = halves(segment_row, rows)
    own_rank, far_rank = halves(pick(token_rank, sequence, 0), rows)
    key_segment = jnp.concatenate([own_segment, far_segment])
    key_rank = jnp.concatenate([own_rank, far_rank])
    key_start = jnp.concatenate(halves(starts_row, rows))
    source_row = jnp.concatenate(halves(pick(source_segment, sequence, 0), source_count))
    self_allowed = (own_segment[None, :] == key_segment[:, None]) & (
        (key_rank[:, None] < own_rank[None, :]) | key_start[:, None]
    )
    cross_allowed = own_segment[None, :] == source_row[:, None]
    self_bias = jnp.where(self_allowed, 0.0, -1e30).astype(jnp.float32)
    cross_bias = jnp.where(cross_allowed, 0.0, -1e30).astype(jnp.float32)
    self_near = near_tiles(own_segment, key_segment)
    cross_near = near_tiles(own_segment, source_row)

    table_rows = sum(vector.shape[0] for vector in vectors) // width
    if not fast:
        (table,) = kernel_call(
            table_kernel, [((table_rows, width), jnp.float32)], 2, 1, "table", *vectors
        )
    small_rows = table_rows + -table_rows % 16
    square, column = ((rows, width), jnp.float32), ((rows, 1), jnp.float32)
    low_square = ((rows, width), LOW)

    mixture, self_total, queries, self_sides, (w_query, w_key, w_value) = self_forward(
        fast, spots, self_near, self_bias, (query_stream, token_stream, far_tokens), gathered_one,
        16,
    )
    self_set = (self_near, self_bias, queries, self_sides)
    if fast:
        line_rest = [ordered(piece, mixture) for piece in line_rest]
        near_two = spread_plane([piece[:, :split_at] for piece in line_rest])
        gathered_two = join([ordered(piece, far_source) for piece in near_two])
        near_three = spread_plane(
            [ordered(piece[:, split_at:], near_two[3]) for piece in line_rest]
        )
    cross_outs, source_sides, (w_merge, w_cquery, w_ckey, w_cvalue) = cross_forward(
        fast, spots, cross_near, cross_bias, mixture, query_stream, (encoder_states, far_source), table,
        gathered_two, 22,
    )
    cross_mix, cross_total, cross_rows, first_normed, first_inverse, first_low = cross_outs
    cross_set = (cross_near, cross_bias, cross_rows, source_sides)
    if fast:
        gathered_three = join([ordered(piece, cross_mix) for piece in near_three])
        w_cmerge, w_expand, w_reduce = place(groups[2], gathered_three, spots)
    if fast:
        grads = [((2 * width, hidden // 2), LOW)] * 2
    else:
        grads = [((width, hidden), jnp.float32)] * 2
    hidden_states, third_grad, pre_grad, second_normed, second_inverse, small_one, *grads = kernel_call(
        functools.partial(hidden_kernel, fast),
        [low_square, square, ((rows, hidden), LOW), square, column, ((small_rows, width), jnp.float32), *grads],
        30, 13, "hidden",
        spots, cross_mix, w_cmerge, first_normed, table, w_expand, w_reduce, cotangent,
        scalars=1,
        scratch=[pltpu.VMEM((rows, hidden), LOW), pltpu.VMEM((rows, hidden), jnp.float32)],
    )
    if fast:
        hidden_sum = Reduction(*grads, [hidden // 4] * 2)
    else:
        hidden_sum = PlainReduction(grads)
    second_in_grad, cross_out, cross_mix_grad, small_two = kernel_call(
        hidden_back_kernel, [square, low_square, low_square, ((8, width), jnp.float32)], 16, 3, "hidden_back",
        third_grad, pre_grad, w_expand, second_normed, second_inverse, table, w_cmerge,
    )
    hidden_sum.first(cross_mix_grad)
    cross_rows_grad, *source_grads = attend_back(
        *cross_set, cross_mix_grad, cross_mix, cross_total, 25
    )
    keys_near, keys_far, values_near, values_far = source_grads
    source_back = over_tensor(
        (dot_nt(keys_far, w_ckey) + dot_nt(values_far, w_cvalue)).astype(LOW), 1
    )
    if fast:
        cross_rows_grad = ordered(cross_rows_grad, *hidden_sum.plane)
    stream_grad, self_out, mixture_grad, packed = kernel_call(
        first_back_kernel, [square, low_square, low_square, ((small_rows, width), jnp.float32)], 12, 2, "first_back",
        second_in_grad, cross_rows_grad, w_cquery, first_normed, first_inverse, table, w_merge, small_one, small_two,
    )
    hidden_sum.second(self_out)
    cross_sum = reduce_products(
        fast,
        [
            [(first_low, [cross_rows_grad])],
            [
                (encoder_states, [keys_near, values_near]),
                (far_source, [keys_far, values_far]),
            ],
            [(cross_out, [cross_mix])],
            [(self_out, [mixture])],
        ],
        spots,
        5,
        packed,
    )
    mixture_grad = ordered(mixture_grad, cross_sum.core)
    cross_sum.first()
    queries_grad, *token_grads = attend_back(*self_set, mixture_grad, mixture, self_total, 16)
    if fast:
        queries_grad = ordered(queries_grad, source_back, *cross_sum.plane)
    source_sum = dot_nt(ordered(keys_near, queries_grad), w_ckey) + dot_nt(values_near, w_cvalue)
    keys_near, keys_far, values_near, values_far = token_grads
    self_sum = reduce_products(
        fast,
        [
            [(query_stream, [queries_grad])],
            [
                (token_stream, [keys_near, values_near]),
                (far_tokens, [keys_far, values_far]),
            ],
        ],
        spots,
        3,
    )
    keys_far = ordered(keys_far, self_sum.core)
    token_back = over_tensor(
        (dot_nt(keys_far, w_key) + dot_nt(values_far, w_value)).astype(LOW), 1
    )
    token_sum = dot_nt(keys_near, w_key) + dot_nt(values_near, w_value)
    if fast:
        self_sum.first(*hidden_sum.line)
    cross_sum.second(self_sum.own if fast else self_sum.keep)
    self_sum.second()
    (expand_part, reduce_part), _ = hidden_sum.result(queries_grad)
    (*cross_parts, merge_part), summed = cross_sum.result()
    self_parts, _ = self_sum.result()
    summed = summed[:, :width].reshape(-1)
    small, at = [], 0
    for vector in vectors:
        small.append(summed[at : at + vector.shape[0]])
        at += vector.shape[0]
    return (
        hidden_states,
        (stream_grad + dot_nt(queries_grad, w_query)).astype(LOW),
        (token_sum + up(token_back)).astype(LOW),
        (source_sum + up(ordered(source_back, queries_grad))).astype(LOW),
        *self_parts,
        merge_part,
        *cross_parts,
        expand_part,
        reduce_part,
        *small,
    )


def solution(mesh):
    fast = mesh.shape["dp"] == 8 and mesh.shape["tensor"] == 4
    rows = P(BOTH, None)
    block = P("dp", "tensor")

    def program(*arguments):
        return body(*arguments, fast)

    return jax.shard_map(
        program,
        mesh=mesh,
        in_specs=(rows,) * 3 + (P("dp", None),) * 3 + (block,) * 10 + (P(),) * 8 + (rows,),
        out_specs=(rows,) * 4 + (block,) * 10 + (P(),) * 8,
        check_vma=False,
    )
```

```python
import functools

import jax
import jax.numpy as jnp
from jax import lax
from jax.sharding import PartitionSpec as P
from jax.experimental import pallas as pl
from jax.experimental.pallas import tpu as pltpu

EPSILON = 1e-05
GATE = 0.7978845608028654
CUBIC = 0.044715
LOG2E = 1.4426950408889634
UNIT = 128
PAIR = 128
TILE = 256
BOTH = ("dp", "tensor")
ANY = pl.BlockSpec(memory_space=pl.ANY)
WHOLE = pl.BlockSpec(memory_space=pltpu.VMEM)
SCALARS = pl.BlockSpec(memory_space=pltpu.SMEM)
LOW = jnp.bfloat16


def params(mib):
    return pltpu.CompilerParams(vmem_limit_bytes=mib * 1024 * 1024)


def lasting(us):
    return pl.CostEstimate(flops=int(us * 1.1e7), bytes_accessed=0, transcendentals=0)


def far_memory(value):
    return pltpu.with_memory_space_constraint(value, pltpu.HBM)


def up(value):
    return value.astype(jnp.float32)


def dot_nn(a, b):
    return lax.dot_general(a, b, (((1,), (0,)), ((), ())), preferred_element_type=jnp.float32)


def dot_nt(a, b):
    return lax.dot_general(a, b, (((1,), (1,)), ((), ())), preferred_element_type=jnp.float32)


def dot_tn(a, b):
    return lax.dot_general(a, b, (((0,), (0,)), ((), ())), preferred_element_type=jnp.float32)


REDUCE_BIAS, GAIN_ONE, BIAS_ONE, GAIN_TWO, BIAS_TWO, GAIN_THREE, BIAS_THREE = range(-7, 0)


def norm_rows(matrix):
    centred = matrix - jnp.mean(matrix, -1, keepdims=True)
    inverse = lax.rsqrt(jnp.mean(centred * centred, -1, keepdims=True) + EPSILON)
    return centred * inverse, inverse


def norm_back(outer_grad, normed, inverse, gains):
    spread = outer_grad * gains
    return inverse * (
        spread
        - jnp.mean(spread, -1, keepdims=True)
        - normed * jnp.mean(spread * normed, -1, keepdims=True)
    )


def down(matrix):
    return jnp.sum(matrix, 0, keepdims=True)


def table_row(table_ref, row):
    row += table_ref.shape[0]
    return table_ref[row : row + 1]


def hidden_kernel(
    fast, spots_ref, mix_ref, merge_ref, first_ref, table_ref, expand_ref, reduce_ref, cotangent_ref, *refs
):
    states_ref, third_ref, pre_ref, normed_ref, inverse_ref, small_ref, *grads = refs[:8]
    active_ref, slope_ref, parts_ref = refs[8:]
    row = functools.partial(table_row, table_ref)
    first_out = first_ref[...] * row(GAIN_ONE) + row(BIAS_ONE)
    normed, inverse = norm_rows(first_out + dot_nt(mix_ref[...], merge_ref[...]))
    normed_ref[...] = normed
    inverse_ref[...] = inverse
    second_out = normed * row(GAIN_TWO) + row(BIAS_TWO)
    second_low = second_out.astype(LOW)
    width = mix_ref.shape[1]
    chunks = expand_ref.shape[1] // width
    output = second_out + row(REDUCE_BIAS)
    for c in range(chunks):
        columns = slice(c * width, (c + 1) * width)
        x = dot_nn(second_low, expand_ref[:, columns]) + table_ref[c : c + 1]
        square = x * x
        bent = jnp.tanh(x * (GATE + (GATE * CUBIC) * square))
        halved = 0.5 + 0.5 * bent
        active = (x * halved).astype(LOW)
        slope_ref[:, columns] = halved + (0.5 * x) * (1.0 - bent * bent) * (
            GATE + (3.0 * GATE * CUBIC) * square
        )
        active_ref[:, columns] = active
        output = output + dot_nt(active, reduce_ref[:, columns])
    normed, inverse = norm_rows(output)
    states_ref[...] = (normed * row(GAIN_THREE) + row(BIAS_THREE)).astype(LOW)
    outer = up(cotangent_ref[...])
    third = norm_back(outer, normed, inverse, row(GAIN_THREE))
    third_ref[...] = third
    output_grad = third.astype(LOW)
    small_ref[...] = jnp.zeros(small_ref.shape, jnp.float32)
    at = table_ref.shape[0]
    small_ref[at + GAIN_THREE : at + GAIN_THREE + 1] = down(outer * normed)
    small_ref[at + BIAS_THREE : at + BIAS_THREE + 1] = down(outer)
    small_ref[at + REDUCE_BIAS : at + REDUCE_BIAS + 1] = down(up(output_grad))
    second_turned, output_turned = second_low.T, output_grad.T
    for c in range(chunks):
        columns = slice(c * width, (c + 1) * width)
        pre_grad = (dot_nn(output_grad, reduce_ref[:, columns]) * slope_ref[:, columns]).astype(LOW)
        pre_ref[:, columns] = pre_grad
        small_ref[c : c + 1] = down(up(pre_grad))
        parts = (dot_nn(second_turned, pre_grad), dot_nn(output_turned, active_ref[:, columns]))
        for i, part in enumerate(parts):
            if fast:
                parts_ref[i, c] = part.astype(LOW)
            else:
                grads[i][:, columns] = part
    if fast:
        blocks = [(parts_ref[i, c], (c,), i * width) for i in range(2) for c in range(chunks)]
        store_blocks(spots_ref, *grads, blocks)


def hidden_back_kernel(
    third_ref, pre_ref, expand_ref, normed_ref, inverse_ref, table_ref, merge_ref, mixed_ref, *refs
):
    inner_ref, mix_ref, small_ref, grad_ref = refs
    normed = normed_ref[...]
    outer = third_ref[...] + dot_nt(pre_ref[...], expand_ref[...])
    inner = norm_back(outer, normed, inverse_ref[...], table_row(table_ref, GAIN_TWO))
    inner_ref[...] = inner
    low = inner.astype(LOW)
    mix_ref[...] = dot_nn(low, merge_ref[...]).astype(LOW)
    grad_ref[...] = dot_tn(low, mixed_ref[...]).astype(grad_ref.dtype)
    small_ref[0:1] = down(outer * normed)
    small_ref[1:2] = down(outer)


def first_back_kernel(
    second_ref, rows_ref, query_ref, normed_ref, inverse_ref, table_ref, merge_ref, one_ref, two_ref, *refs
):
    inner_ref, low_ref, mix_ref, small_ref = refs
    normed = normed_ref[...]
    outer = second_ref[...] + dot_nt(rows_ref[...], query_ref[...])
    inner = norm_back(outer, normed, inverse_ref[...], table_row(table_ref, GAIN_ONE))
    inner_ref[...] = inner
    low = inner.astype(LOW)
    low_ref[...] = low
    mix_ref[...] = dot_nn(low, merge_ref[...]).astype(LOW)
    at = table_ref.shape[0]
    small_ref[...] = one_ref[...]
    small_ref[at + GAIN_TWO : at + BIAS_TWO + 1] = two_ref[0:2]
    small_ref[at + GAIN_ONE : at + GAIN_ONE + 1] = down(outer * normed)
    small_ref[at + BIAS_ONE : at + BIAS_ONE + 1] = down(outer)


def kernel_call(kernel, outs, mib, us, name, *operands, scalars=0, scratch=()):
    return pl.pallas_call(
        kernel,
        out_shape=[jax.ShapeDtypeStruct(*out) for out in outs],
        in_specs=[SCALARS] * scalars + [WHOLE] * (len(operands) - scalars),
        out_specs=[WHOLE] * len(outs),
        scratch_shapes=list(scratch),
        compiler_params=params(mib),
        cost_estimate=lasting(us),
        name=name,
    )(*operands)


def split_heads(rows):
    lane = lax.broadcasted_iota(jnp.int32, rows.shape, 1)
    zero = jnp.zeros_like(rows)
    return jnp.concatenate(
        [jnp.where(lane < PAIR // 2, rows, zero), jnp.where(lane < PAIR // 2, zero, rows)], 0
    )


def twice(row):
    return jnp.concatenate([row, row], 1)


def pair_columns(count):
    return [slice(p * PAIR, (p + 1) * PAIR) for p in range(count)]


def attend_all(near_ref, bias_ref, q_ref, sides, out_ref, lse_ref, scratch):
    k_near, k_far, v_near, v_far = sides
    turned, stacked, top, total, acc = scratch
    nq, nk = q_ref.shape[0] // TILE, k_near.shape[0] // TILE
    half = PAIR // 2
    columns = pair_columns(stacked.shape[0])
    for p, pair in enumerate(columns):
        turned[p, 0] = v_near[:, pair].T
        turned[p, 1] = v_far[:, pair].T
    for i in range(nq):
        q_rows = slice(i * TILE, (i + 1) * TILE)
        for p, pair in enumerate(columns):
            stacked[p] = split_heads(q_ref[q_rows, pair])
        top[...] = jnp.full(top.shape, -3e30, jnp.float32)
        total[...] = jnp.zeros(total.shape, jnp.float32)
        acc[...] = jnp.zeros(acc.shape, jnp.float32)
        for j in range(2 * nk):

            @pl.when(near_ref[i, j] != 0)
            def _(j=j, q_rows=q_rows):
                k_ref = k_far if j >= nk else k_near
                k_rows = slice(j % nk * TILE, (j % nk + 1) * TILE)
                bias = twice(bias_ref[j * TILE : (j + 1) * TILE, q_rows])
                products = [dot_nt(k_ref[k_rows, pair], stacked[p]) for p, pair in enumerate(columns)]
                for p, product in enumerate(products):
                    scores = product + bias
                    old = top[p]
                    peak = jnp.maximum(old, jnp.max(scores, 0, keepdims=True))
                    fade = jnp.exp2((old - peak) * LOG2E)
                    powers = jnp.exp2((scores - peak) * LOG2E)
                    top[p] = peak
                    total[p] = total[p] * fade + jnp.sum(powers, 0, keepdims=True)
                    acc[p] = acc[p] * fade + dot_nn(
                        turned[p, j // nk, :, k_rows], powers.astype(LOW)
                    )

        for p, pair in enumerate(columns):
            full = total[p]
            scaled = acc[p] * (1.0 / full)
            mixed = jnp.concatenate([scaled[:half, :TILE], scaled[half:, TILE:]], 0)
            out_ref[q_rows, pair] = mixed.T.astype(LOW)
            log_total = top[p] * LOG2E + jnp.log2(full)
            lse_ref[p, 0:1, q_rows] = log_total[:, :TILE]
            lse_ref[p, 1:2, q_rows] = log_total[:, TILE:]


def attend_scratch(pairs, lk):
    return [
        pltpu.VMEM((pairs, 2, PAIR, lk), LOW),
        pltpu.VMEM((pairs, 2 * TILE, PAIR), LOW),
        pltpu.VMEM((pairs, 1, 2 * TILE), jnp.float32),
        pltpu.VMEM((pairs, 1, 2 * TILE), jnp.float32),
        pltpu.VMEM((pairs, PAIR, 2 * TILE), jnp.float32),
    ]


def place_whole(spots_ref, pieces, out, at):
    me_dp, me_t = spots_ref[0], spots_ref[1]
    rows = pieces[0].shape[2]
    for piece, (dp_flips, t_flips) in zip(pieces, PIECES):
        for a, dp_flip in enumerate(dp_flips):
            row = pl.multiple_of(jnp.bitwise_xor(me_dp, dp_flip) * rows, rows)
            for b, t_flip in enumerate(t_flips):
                column = pl.multiple_of(jnp.bitwise_xor(me_t, t_flip) * PAIR, PAIR)
                out[pl.ds(row, rows), pl.ds(column, PAIR)] = piece[a, b, :, at : at + PAIR]


class Copies:
    def __init__(self, held, outs, sems):
        self.copies = [
            pltpu.make_async_copy(one, out, sems.at[i]) for i, (one, out) in enumerate(zip(held, outs))
        ]

    def start(self, *which):
        for i in which:
            self.copies[i].start()

    def wait(self):
        for copy in self.copies:
            copy.wait()


def self_kernel(
    fast, spots_ref, near_ref, bias_ref, query_ref, token_ref, far_ref, *refs
):
    cut = 2 if fast else 3
    n = 8 if fast else 5
    gathered, (out_ref, lse_ref), outs = refs[:cut], refs[cut : cut + 2], refs[cut + 2 : cut + 2 + n]
    scratch = refs[cut + 2 + n :]
    held, sems, scratch = scratch[:n], scratch[n], scratch[n + 1 :]
    copies = Copies(held, outs, sems)
    q_ref, sides, weights = held[0], held[1:5], held[5:]
    if fast:
        for i, weight in enumerate(weights):
            place_whole(spots_ref, gathered, weight, i * PAIR)
        copies.start(5, 6, 7)
    else:
        weights = gathered
    w_query, w_key, w_value = (weight[...] for weight in weights)
    q_ref[...] = (dot_nn(query_ref[...], w_query) * 0.125).astype(LOW)
    for i, (rows, weight) in enumerate(
        ((token_ref, w_key), (far_ref, w_key), (token_ref, w_value), (far_ref, w_value))
    ):
        sides[i][...] = dot_nn(rows[...], weight).astype(LOW)
    copies.start(0, 1, 2, 3, 4)
    attend_all(near_ref, bias_ref, q_ref, sides, out_ref, lse_ref, scratch)
    copies.wait()


def self_forward(fast, spots, near, bias, streams, gathered, us):
    lq, width = streams[0].shape
    lk, pairs = streams[1].shape[0], width // PAIR
    rows, keys, square = (((n, width), LOW) for n in (lq, lk, width))
    kept = [rows] + [keys] * 4 + ([square] * 3 if fast else [])
    results = pl.pallas_call(
        functools.partial(self_kernel, fast),
        in_specs=[SCALARS, SCALARS] + [WHOLE] * (4 + len(gathered)),
        out_specs=[WHOLE, WHOLE] + [ANY] * len(kept),
        out_shape=[
            jax.ShapeDtypeStruct(*rows),
            jax.ShapeDtypeStruct((pairs, 2, lq), jnp.float32),
            *(pltpu.HBM(*out) for out in kept),
        ],
        scratch_shapes=[pltpu.VMEM(*out) for out in kept]
        + [pltpu.SemaphoreType.DMA((len(kept),))]
        + attend_scratch(pairs, lk),
        compiler_params=params(24),
        cost_estimate=lasting(us),
        name="self_forward",
    )(spots, near, bias, *map(far_memory, streams), *gathered)
    mixture, lse, queries = results[:3]
    return mixture, lse, queries, results[3:7], results[7:] if fast else gathered


def cross_kernel(
    fast, spots_ref, near_ref, bias_ref, mix_ref, stream_ref, near_rows, far_rows, table_ref, *refs
):
    cut = 2 if fast else 4
    n = 12 if fast else 8
    gathered, (out_ref, lse_ref), outs = refs[:cut], refs[cut : cut + 2], refs[cut + 2 : cut + 2 + n]
    scratch = refs[cut + 2 + n :]
    held, sems, scratch = scratch[:n], scratch[n], scratch[n + 1 :]
    copies = Copies(held, outs, sems)
    rows_ref, normed_ref, inverse_ref, low_ref = held[:4]
    sides, weights = held[4:8], held[8:]
    if fast:
        for i, weight in enumerate(weights):
            place_whole(spots_ref, gathered, weight, i * PAIR)
        copies.start(8, 9, 10, 11)
    else:
        weights = gathered
    w_merge, w_query, w_key, w_value = weights
    normed, inverse = norm_rows(up(stream_ref[...]) + dot_nt(mix_ref[...], w_merge[...]))
    normed_ref[...] = normed
    inverse_ref[...] = inverse
    low = (normed * table_row(table_ref, GAIN_ONE) + table_row(table_ref, BIAS_ONE)).astype(LOW)
    low_ref[...] = low
    rows_ref[...] = (dot_nn(low, w_query[...]) * 0.125).astype(LOW)
    for i, (rows, weight) in enumerate(
        ((near_rows, w_key), (far_rows, w_key), (near_rows, w_value), (far_rows, w_value))
    ):
        sides[i][...] = dot_nn(rows[...], weight[...]).astype(LOW)
    copies.start(0, 1, 2, 3, 4, 5, 6, 7)
    attend_all(near_ref, bias_ref, rows_ref, sides, out_ref, lse_ref, scratch)
    copies.wait()


def cross_forward(fast, spots, near, bias, mixture, stream, sources, table, gathered, us):
    lq, width = mixture.shape
    lk, pairs = sources[0].shape[0], width // PAIR
    rows, keys, square = (((n, width), LOW) for n in (lq, lk, width))
    kept = [rows, ((lq, width), jnp.float32), ((lq, 1), jnp.float32), rows] + [keys] * 4
    if fast:
        kept += [square] * 4
    results = pl.pallas_call(
        functools.partial(cross_kernel, fast),
        in_specs=[SCALARS, SCALARS] + [WHOLE] * (6 + len(gathered)),
        out_specs=[WHOLE, WHOLE] + [ANY] * len(kept),
        out_shape=[
            jax.ShapeDtypeStruct(*rows),
            jax.ShapeDtypeStruct((pairs, 2, lq), jnp.float32),
            *(pltpu.HBM(*out) for out in kept),
        ],
        scratch_shapes=[pltpu.VMEM(*out) for out in kept]
        + [pltpu.SemaphoreType.DMA((len(kept),))]
        + attend_scratch(pairs, lk),
        compiler_params=params(30),
        cost_estimate=lasting(us),
        name="cross_forward",
    )(spots, near, bias, mixture, far_memory(stream), *map(far_memory, sources), table, *gathered)
    return results[:6], results[6:10], results[10:] if fast else gathered


def backward_kernel(near_ref, bias_ref, q_ref, m_ref, o_ref, lse_ref, *refs):
    k_near, k_far, v_near, v_far, dq_ref, *outs = refs[:9]
    stacked, grads, delta, log_total, dq_acc, dk_acc, dv_acc = refs[9:]
    nq, nk = q_ref.shape[0] // TILE, k_near.shape[0] // TILE
    half = PAIR // 2
    columns = pair_columns(stacked.shape[0])
    dk_acc[...] = jnp.zeros(dk_acc.shape, jnp.float32)
    dv_acc[...] = jnp.zeros(dv_acc.shape, jnp.float32)
    for i in range(nq):
        q_rows = slice(i * TILE, (i + 1) * TILE)
        for p, pair in enumerate(columns):
            stacked[p] = split_heads(q_ref[q_rows, pair])
            grads[p] = split_heads(m_ref[q_rows, pair])
            turned = (up(m_ref[q_rows, pair]) * up(o_ref[q_rows, pair])).T
            delta[p] = jnp.concatenate([down(turned[:half]), down(turned[half:])], 1)
            log_total[p] = jnp.concatenate([lse_ref[p, 0:1, q_rows], lse_ref[p, 1:2, q_rows]], 1)
        dq_acc[...] = jnp.zeros(dq_acc.shape, jnp.float32)
        for j in range(2 * nk):

            @pl.when(near_ref[i, j] != 0)
            def _(j=j, q_rows=q_rows):
                k_ref, v_ref = (k_far, v_far) if j >= nk else (k_near, v_near)
                k_rows = slice(j % nk * TILE, (j % nk + 1) * TILE)
                all_rows = slice(j * TILE, (j + 1) * TILE)
                bias = twice(bias_ref[all_rows, q_rows])
                scores = [dot_nt(k_ref[k_rows, pair], stacked[p]) for p, pair in enumerate(columns)]
                outer = [dot_nt(v_ref[k_rows, pair], grads[p]) for p, pair in enumerate(columns)]
                for p, pair in enumerate(columns):
                    weights = jnp.exp2(scores[p] * LOG2E + (bias - log_total[p]))
                    slope = (weights * (outer[p] - delta[p])).astype(LOW)
                    dv_acc[p, all_rows] += dot_nn(weights.astype(LOW), grads[p])
                    dk_acc[p, all_rows] += dot_nn(slope, stacked[p])
                    dq_acc[p] += dot_tn(slope, k_ref[k_rows, pair])

        lane = lax.broadcasted_iota(jnp.int32, (TILE, PAIR), 1)
        for p, pair in enumerate(columns):
            dq_ref[q_rows, pair] = (
                jnp.where(lane < half, dq_acc[p, :TILE], dq_acc[p, TILE:]) * 0.125
            ).astype(LOW)
    size = k_near.shape[0]
    for out, acc, side in zip(outs, (dk_acc, dk_acc, dv_acc, dv_acc), (0, 1, 0, 1)):
        for p, pair in enumerate(columns):
            out[:, pair] = acc[p, side * size : (side + 1) * size].astype(LOW)


def attend_back(near, bias, queries, sides, outer, mixed, lse, us):
    lq, width = queries.shape
    lk, pairs, wide = sides[0].shape[0], 2, 2 * PAIR
    column = lambda p: (0, p)
    q_spec, k_spec = pl.BlockSpec((lq, wide), column), pl.BlockSpec((lk, wide), column)
    return pl.pallas_call(
        backward_kernel,
        grid=(width // wide,),
        in_specs=[SCALARS, WHOLE, q_spec, q_spec, q_spec]
        + [pl.BlockSpec((pairs, 2, lq), lambda p: (p, 0, 0))]
        + [k_spec] * 4,
        out_specs=[q_spec] + [k_spec] * 4,
        out_shape=[jax.ShapeDtypeStruct((lq, width), LOW)]
        + [jax.ShapeDtypeStruct((lk, width), LOW)] * 4,
        scratch_shapes=[
            pltpu.VMEM((pairs, 2 * TILE, PAIR), LOW),
            pltpu.VMEM((pairs, 2 * TILE, PAIR), LOW),
            pltpu.VMEM((pairs, 1, 2 * TILE), jnp.float32),
            pltpu.VMEM((pairs, 1, 2 * TILE), jnp.float32),
            pltpu.VMEM((pairs, 2 * TILE, PAIR), jnp.float32),
            pltpu.VMEM((pairs, 2 * lk, PAIR), jnp.float32),
            pltpu.VMEM((pairs, 2 * lk, PAIR), jnp.float32),
        ],
        compiler_params=params(26),
        cost_estimate=lasting(us),
        name="attend_back",
    )(near, bias, queries, outer, mixed, lse, *sides)


def near_tiles(own, keys):
    own, keys = own.reshape(-1, TILE), keys.reshape(-1, TILE)
    return (
        (keys.min(1)[None] <= own.max(1)[:, None]) & (keys.max(1)[None] >= own.min(1)[:, None])
    ).astype(jnp.int32)


def over_dp(matrix, flip):
    return lax.ppermute(matrix, "dp", [(i, i ^ flip) for i in range(8)])


def over_tensor(matrix, flip):
    return lax.ppermute(matrix, "tensor", [(i, i ^ flip) for i in range(4)])


def ordered(value, *earlier):
    return lax.optimization_barrier((value, *earlier))[0] if earlier else value


PIECES = (((0, 2, 4, 6), (0, 1, 2, 3)), ((1, 3, 5, 7), (0, 1, 2, 3)))


def place_kernel(counts, spots_ref, *refs):
    n = len(counts)
    pieces, outs = refs[:-n], refs[-n:]
    me_dp, me_t = spots_ref[0], spots_ref[1]
    rows = pieces[0].shape[2]
    for piece, (dp_flips, t_flips) in zip(pieces, PIECES):
        for a, dp_flip in enumerate(dp_flips):
            row = pl.multiple_of(jnp.bitwise_xor(me_dp, dp_flip) * rows, rows)
            for b, t_flip in enumerate(t_flips):
                t = jnp.bitwise_xor(me_t, t_flip)
                at = 0
                for out, count in zip(outs, counts):
                    size = count * UNIT
                    column = pl.multiple_of(t * size, UNIT)
                    out[pl.ds(row, rows), pl.ds(column, size)] = piece[a, b, :, at : at + size]
                    at += size


def load_kernel(counts, *refs):
    n, n_vectors = sum(counts), 8
    blocks, vectors = list(refs[:n]), refs[n : n + n_vectors]
    outs, held, sems = refs[n + n_vectors : -2], refs[-2], refs[-1]
    copies = []

    def copy(source, target):
        copies.append(pltpu.make_async_copy(source, target, sems.at[len(copies)]))
        copies[-1].start()

    for out, count in zip(outs, counts):
        at = 0
        for _ in range(count):
            block = blocks.pop(0)
            copy(block, out.at[:, at : at + block.shape[1]])
            at += block.shape[1]
    at = 0
    for vector in vectors:
        copy(vector, held.at[at : at + vector.shape[0]])
        at += vector.shape[0]
    for one in copies:
        one.wait()
    table = outs[-1]
    width = table.shape[1]
    for i in range(table.shape[0]):
        table[i : i + 1] = up(held[i * width : (i + 1) * width]).reshape(1, width)


def load(groups, vectors, width):
    blocks = [block for group in groups for block in group]
    total = sum(vector.shape[0] for vector in vectors)
    return pl.pallas_call(
        functools.partial(load_kernel, [len(group) for group in groups]),
        out_shape=[
            jax.ShapeDtypeStruct((group[0].shape[0], sum(block.shape[1] for block in group)), LOW)
            for group in groups
        ]
        + [jax.ShapeDtypeStruct((total // width, width), jnp.float32)],
        in_specs=[ANY] * (len(blocks) + len(vectors)),
        out_specs=[WHOLE] * (len(groups) + 1),
        scratch_shapes=[
            pltpu.VMEM((total,), LOW),
            pltpu.SemaphoreType.DMA((len(blocks) + len(vectors),)),
        ],
        compiler_params=params(4),
        name="load",
    )(*map(far_memory, blocks), *map(far_memory, vectors))


def table_kernel(*refs):
    *vectors, out = refs
    width, at = out.shape[1], 0
    for vector in vectors:
        row = up(vector[...])
        for i in range(vector.shape[0] // width):
            out[at : at + 1] = row[i * width : (i + 1) * width].reshape(1, width)
            at += 1


def combine_kernel(keep_ref, core_ref, *outs):
    own, *messages, small = outs
    size = own.shape[0]
    n_small = keep_ref.shape[0] - 4 * size
    if n_small:
        total = (up(keep_ref[4 * size :]) + up(core_ref[4 * size :])).astype(LOW)
        small[...] = total
    own[...] = up(keep_ref[:size]) + up(core_ref[:size])
    for i, message in enumerate(messages, 1):
        rows = slice(i * size, (i + 1) * size)
        message[:size] = (up(keep_ref[rows]) + up(core_ref[rows])).astype(LOW)
        if n_small:
            message[size:] = total


def spread_line(own):
    return [own] + [over_tensor(own, flip) for flip in (1, 2, 3)]


def spread_plane(line):
    line = jnp.stack(line)
    return [line] + [over_dp(line, flip) for flip in (2, 4, 6)]


def join(near):
    near = jnp.stack(near)
    return [near, over_dp(near, 1)]


def place(blocks, pieces, spots):
    counts = [block.shape[1] // UNIT for block in blocks]
    rows = blocks[0].shape[0]
    outs = [((8 * rows, 4 * count * UNIT), LOW) for count in counts]
    return kernel_call(
        functools.partial(place_kernel, counts), outs, 18, 1, "place", spots, *pieces, scalars=1
    )


def gather_plain(blocks):
    return [
        lax.all_gather(
            lax.all_gather(block, "dp", axis=0, tiled=True), "tensor", axis=1, tiled=True
        )
        for block in blocks
    ]


def store_blocks(spots_ref, keep_ref, send_ref, parts):
    me_dp, me_t = spots_ref[0], spots_ref[1]

    def store(flipped):
        for full, ts, at in parts:
            rows, size = full.shape[0] // 8, full.shape[1] // len(ts)
            for d in range(8):
                target = send_ref if (d % 2) != flipped else keep_ref
                near = jnp.bitwise_xor(me_dp, d) // 2
                for i, t in enumerate(ts):
                    index = near * 4 + jnp.bitwise_xor(me_t, t)
                    target[pl.ds(pl.multiple_of(index * rows, rows), rows), at : at + size] = full[
                        d * rows : (d + 1) * rows, i * size : (i + 1) * size
                    ]

    pl.when(me_dp % 2 == 0)(functools.partial(store, 0))
    pl.when(me_dp % 2 == 1)(functools.partial(store, 1))


def grad_kernel(layout, n_small, spots_ref, *refs):
    keep_ref, send_ref = refs[-2:]
    refs = list(refs[:-2])
    if n_small:
        small = refs.pop()[...].astype(LOW)
        used = small.shape[1]
        for target in (keep_ref, send_ref):
            target[-n_small:] = jnp.zeros((n_small, target.shape[1]), LOW)
            target[-n_small:, :used] = small
    at, parts = 0, []
    for n_products, n_right in layout:
        full = None if n_products else refs.pop(0)[...]
        for _ in range(n_products):
            left = refs.pop(0)[...]
            right = [refs.pop(0)[...] for _ in range(n_right)]
            product = dot_tn(left, jnp.concatenate(right, 1) if n_right > 1 else right[0])
            full = product if full is None else full + product
        full = full.astype(LOW)
        width = full.shape[1] // n_right
        for i in range(n_right):
            parts.append((full[:, i * width : (i + 1) * width], range(4), at))
            at += width // 4
    store_blocks(spots_ref, keep_ref, send_ref, parts)


def grad_blocks(sums, small, spots, us):
    layout = [
        (0 if products[0][0] is None else len(products), len(products[0][1])) for products in sums
    ]
    rows = 2 * sums[0][0][0].shape[1]
    n_small = sum(term.shape[0] for term in small)
    width = sum(right.shape[1] for products in sums for right in products[0][1])
    operands = [
        matrix
        for products in sums
        for left, rights in products
        for matrix in (left, *rights)
        if matrix is not None
    ]
    out = ((rows + n_small, width // 4), LOW)
    return kernel_call(
        functools.partial(grad_kernel, layout, n_small),
        [out, out],
        28,
        us,
        "grads",
        spots,
        *operands,
        *small,
        scalars=1,
    )


class Reduction:
    def __init__(self, keep, send, widths, n_small=0, halving=False):
        self.keep, self.widths, self.n_small, self.halving = keep, widths, n_small, halving
        self.rows = (keep.shape[0] - n_small) // 16
        self.core = over_dp(send, 1)

    def split(self, matrix):
        cut = matrix.shape[0] - self.n_small
        return matrix[:cut], matrix[cut:]

    def message(self, blocks, small):
        return jnp.concatenate([blocks.astype(LOW), small], 0) if self.n_small else blocks.astype(LOW)

    def first(self, *earlier):
        size, width = 4 * self.rows, self.keep.shape[1]
        message = ((size + self.n_small, width), LOW)
        self.own, *messages, self.small = kernel_call(
            combine_kernel,
            [((size, width), jnp.float32)] + [message] * 3 + [((max(self.n_small, 16), width), LOW)],
            8, 1, "combine",
            self.keep, ordered(self.core, *earlier),
        )
        self.small = self.small[: self.n_small]
        self.plane = [over_dp(piece, 2 * i) for i, piece in enumerate(messages, 1)]

    def add(self, messages):
        (one, small_one), (two, small_two), (three, small_three) = map(self.split, messages)
        total = (self.own + up(one)) + (up(two) + up(three))
        small = (up(self.small) + up(small_one)) + (up(small_two) + up(small_three))
        return total, small

    def second(self, *earlier):
        line, small = self.add([ordered(message, *earlier) for message in self.plane])
        self.small = small.astype(LOW)
        size = self.rows
        if self.halving:
            self.own = line[: 2 * size]
            self.line = [over_tensor(self.message(line[2 * size :], self.small), 2)]
            return
        self.own = line[:size]
        self.line = [
            over_tensor(self.message(line[i * size : (i + 1) * size], self.small), i)
            for i in (1, 2, 3)
        ]

    def add_one(self, message):
        total, small = self.split(message)
        return self.own + up(total), up(self.small) + up(small)

    def third(self, *earlier):
        pair, small = self.add_one(ordered(self.line[0], *earlier))
        self.small = small.astype(LOW)
        self.own = pair[: self.rows]
        self.line = [over_tensor(self.message(pair[self.rows :], self.small), 1)]

    def result(self, *earlier):
        messages = [ordered(message, *earlier) for message in self.line]
        total, small = self.add_one(messages[0]) if self.halving else self.add(messages)
        results, at = [], 0
        for width in self.widths:
            results.append(total[:, at : at + width])
            at += width
        return results, small


class PlainReduction:
    def __init__(self, grads, small=None):
        self.keep = self.core = grads[0]
        self.small = None if small is None else lax.psum(small, BOTH)
        self.parts = [
            lax.psum_scatter(
                lax.psum_scatter(grad, "dp", scatter_dimension=0, tiled=True),
                "tensor",
                scatter_dimension=1,
                tiled=True,
            )
            for grad in grads
        ]

    def first(self, *earlier):
        pass

    second = third = first

    def result(self, *earlier):
        return self.parts, self.small


def reduce_products(fast, sums, spots, us, small=None, halving=False):
    if fast:
        extra = [] if small is None else [small]
        keep, send = grad_blocks(sums, extra, spots, us)
        widths = [right.shape[1] // 4 for products in sums for right in products[0][1]]
        n_small = sum(term.shape[0] for term in extra)
        return Reduction(keep, send, widths, n_small, halving)
    grads = []
    for products in sums:
        for i in range(len(products[0][1])):
            grads.append(
                sum(rights[i] if left is None else dot_tn(left, rights[i]) for left, rights in products)
            )
    return PlainReduction(grads, small)


def pick(array, index, axis):
    return lax.dynamic_index_in_dim(array, index, axis, keepdims=False)


def body(
    query_stream,
    token_stream,
    encoder_states,
    token_segment,
    token_rank,
    source_segment,
    query_map,
    key_map,
    value_map,
    merge_map,
    cross_query,
    cross_key,
    cross_value,
    cross_merge,
    expand_map,
    reduce_map,
    expand_bias,
    reduce_bias,
    gain_first,
    bias_first,
    gain_second,
    bias_second,
    gain_third,
    bias_third,
    cotangent,
    fast,
):
    rows, source_count = query_stream.shape[0], encoder_states.shape[0]
    me_dp, me_t = lax.axis_index("dp"), lax.axis_index("tensor")
    spots = jnp.stack([me_dp, me_t]).astype(jnp.int32)
    sequence, half = me_t // 2, me_t % 2

    groups = (
        (query_map, key_map, value_map),
        (merge_map, cross_query, cross_key, cross_value),
        (cross_merge, expand_map, reduce_map),
    )
    width, hidden = query_stream.shape[1], expand_bias.shape[0]
    vectors = (
        expand_bias, reduce_bias, gain_first, bias_first, gain_second, bias_second, gain_third, bias_third,
    )
    if fast:
        own_one, own_rest, table = load((groups[0], groups[1] + groups[2]), vectors, width)
        line_one = spread_line(own_one)
        far_tokens = over_tensor(token_stream, 1)
        near_one = spread_plane(line_one)
        line_rest = spread_line(ordered(own_rest, *line_one))
        gathered_one = join(near_one)
        far_source = over_tensor(ordered(encoder_states, far_tokens), 1)
        split_at = sum(block.shape[1] for block in groups[1])
    else:
        far_tokens = over_tensor(token_stream, 1)
        far_source = over_tensor(encoder_states, 1)
        gathered_one, gathered_two = gather_plain(groups[0]), gather_plain(groups[1])
        w_cmerge, w_expand, w_reduce = gather_plain(groups[2])

    def halves(row, size):
        return lax.dynamic_slice_in_dim(row, half * size, size), lax.dynamic_slice_in_dim(
            row, (1 - half) * size, size
        )

    segment_row = pick(token_segment, sequence, 0)
    starts_row = jnp.concatenate([jnp.ones((1,), jnp.bool_), segment_row[1:] != segment_row[:-1]])
    own_segment, far_segment = halves(segment_row, rows)
    own_rank, far_rank = halves(pick(token_rank, sequence, 0), rows)
    key_segment = jnp.concatenate([own_segment, far_segment])
    key_rank = jnp.concatenate([own_rank, far_rank])
    key_start = jnp.concatenate(halves(starts_row, rows))
    source_row = jnp.concatenate(halves(pick(source_segment, sequence, 0), source_count))
    self_allowed = (own_segment[None, :] == key_segment[:, None]) & (
        (key_rank[:, None] < own_rank[None, :]) | key_start[:, None]
    )
    cross_allowed = own_segment[None, :] == source_row[:, None]
    self_bias = jnp.where(self_allowed, 0.0, -1e30).astype(jnp.float32)
    cross_bias = jnp.where(cross_allowed, 0.0, -1e30).astype(jnp.float32)
    self_near = near_tiles(own_segment, key_segment)
    cross_near = near_tiles(own_segment, source_row)

    table_rows = sum(vector.shape[0] for vector in vectors) // width
    if not fast:
        (table,) = kernel_call(
            table_kernel, [((table_rows, width), jnp.float32)], 2, 1, "table", *vectors
        )
    small_rows = table_rows + -table_rows % 16
    square, column = ((rows, width), jnp.float32), ((rows, 1), jnp.float32)
    low_square = ((rows, width), LOW)

    mixture, self_total, queries, self_sides, (w_query, w_key, w_value) = self_forward(
        fast, spots, self_near, self_bias, (query_stream, token_stream, far_tokens), gathered_one,
        16,
    )
    self_set = (self_near, self_bias, queries, self_sides)
    if fast:
        line_rest = [ordered(piece, mixture) for piece in line_rest]
        near_two = spread_plane([piece[:, :split_at] for piece in line_rest])
        gathered_two = join([ordered(piece, far_source) for piece in near_two])
        near_three = spread_plane(
            [ordered(piece[:, split_at:], near_two[3]) for piece in line_rest]
        )
    cross_outs, source_sides, (w_merge, w_cquery, w_ckey, w_cvalue) = cross_forward(
        fast, spots, cross_near, cross_bias, mixture, query_stream, (encoder_states, far_source), table,
        gathered_two, 22,
    )
    cross_mix, cross_total, cross_rows, first_normed, first_inverse, first_low = cross_outs
    cross_set = (cross_near, cross_bias, cross_rows, source_sides)
    if fast:
        gathered_three = join([ordered(piece, cross_mix) for piece in near_three])
        w_cmerge, w_expand, w_reduce = place(groups[2], gathered_three, spots)
    if fast:
        grads = [((2 * width, hidden // 2), LOW)] * 2
    else:
        grads = [((width, hidden), jnp.float32)] * 2
    hidden_states, third_grad, pre_grad, second_normed, second_inverse, small_one, *grads = kernel_call(
        functools.partial(hidden_kernel, fast),
        [low_square, square, ((rows, hidden), LOW), square, column, ((small_rows, width), jnp.float32), *grads],
        30, 13, "hidden",
        spots, cross_mix, w_cmerge, first_normed, table, w_expand, w_reduce, cotangent,
        scalars=1,
        scratch=[
            pltpu.VMEM((rows, hidden), LOW),
            pltpu.VMEM((rows, hidden), jnp.float32),
            pltpu.VMEM((2, hidden // width, width, width), LOW),
        ],
    )
    if fast:
        hidden_sum = Reduction(*grads, [hidden // 4] * 2, halving=True)
    else:
        hidden_sum = PlainReduction(grads)
    second_in_grad, cross_mix_grad, small_two, cross_merge_grad = kernel_call(
        hidden_back_kernel,
        [square, low_square, ((8, width), jnp.float32), ((width, width), LOW if fast else jnp.float32)],
        18, 3, "hidden_back",
        third_grad, pre_grad, w_expand, second_normed, second_inverse, table, w_cmerge, cross_mix,
    )
    hidden_sum.first(cross_mix_grad)
    cross_rows_grad, *source_grads = attend_back(
        *cross_set, cross_mix_grad, cross_mix, cross_total, 25
    )
    keys_near, keys_far, values_near, values_far = source_grads
    source_back = over_tensor(
        (dot_nt(keys_far, w_ckey) + dot_nt(values_far, w_cvalue)).astype(LOW), 1
    )
    stream_grad, self_out, mixture_grad, packed = kernel_call(
        first_back_kernel, [square, low_square, low_square, ((small_rows, width), jnp.float32)], 12, 2, "first_back",
        second_in_grad, cross_rows_grad, w_cquery, first_normed, first_inverse, table, w_merge, small_one, small_two,
    )
    hidden_sum.second(self_out)
    if fast:
        cross_merge_grad = ordered(cross_merge_grad, *hidden_sum.plane)
    cross_sum = reduce_products(
        fast,
        [
            [(first_low, [cross_rows_grad])],
            [
                (encoder_states, [keys_near, values_near]),
                (far_source, [keys_far, values_far]),
            ],
            [(None, [cross_merge_grad])],
            [(self_out, [mixture])],
        ],
        spots,
        5,
        packed,
        True,
    )
    mixture_grad = ordered(mixture_grad, cross_sum.core)
    cross_sum.first()
    queries_grad, *token_grads = attend_back(*self_set, mixture_grad, mixture, self_total, 16)
    if fast:
        queries_grad = ordered(queries_grad, *cross_sum.plane)
    source_sum = dot_nt(ordered(keys_near, queries_grad), w_ckey) + dot_nt(values_near, w_cvalue)
    keys_near, keys_far, values_near, values_far = token_grads
    self_sum = reduce_products(
        fast,
        [
            [(query_stream, [queries_grad])],
            [
                (token_stream, [keys_near, values_near]),
                (far_tokens, [keys_far, values_far]),
            ],
        ],
        spots,
        3,
    )
    keys_far = ordered(keys_far, self_sum.core)
    token_back = over_tensor(
        (dot_nt(keys_far, w_key) + dot_nt(values_far, w_value)).astype(LOW), 1
    )
    token_sum = dot_nt(keys_near, w_key) + dot_nt(values_near, w_value)
    self_sum.first(source_back)
    if fast:
        cross_sum.second(self_sum.core)
        hidden_sum.third(self_sum.core)
        self_sum.second(*cross_sum.line, *hidden_sum.line)
        cross_sum.third(self_sum.own)
    late = self_sum.plane[0] if fast else queries_grad
    (expand_part, reduce_part), _ = hidden_sum.result(queries_grad)
    (*cross_parts, merge_part), summed = cross_sum.result()
    self_parts, _ = self_sum.result(*(cross_sum.line if fast else ()))
    summed = summed[:, :width].reshape(-1)
    small, at = [], 0
    for vector in vectors:
        small.append(summed[at : at + vector.shape[0]])
        at += vector.shape[0]
    return (
        hidden_states,
        (stream_grad + dot_nt(queries_grad, w_query)).astype(LOW),
        (token_sum + up(token_back)).astype(LOW),
        (source_sum + up(ordered(source_back, late))).astype(LOW),
        *self_parts,
        merge_part,
        *cross_parts,
        expand_part,
        reduce_part,
        *small,
    )


def solution(mesh):
    fast = mesh.shape["dp"] == 8 and mesh.shape["tensor"] == 4
    rows = P(BOTH, None)
    block = P("dp", "tensor")

    def program(*arguments):
        return body(*arguments, fast)

    return jax.shard_map(
        program,
        mesh=mesh,
        in_specs=(rows,) * 3 + (P("dp", None),) * 3 + (block,) * 10 + (P(),) * 8 + (rows,),
        out_specs=(rows,) * 4 + (block,) * 10 + (P(),) * 8,
        check_vma=False,
    )
```

```python
import functools

import jax
import jax.numpy as jnp
from jax import lax
from jax.sharding import PartitionSpec as P
from jax.experimental import pallas as pl
from jax.experimental.pallas import tpu as pltpu

EPSILON = 1e-05
GATE = 0.7978845608028654
CUBIC = 0.044715
LOG2E = 1.4426950408889634
UNIT = 128
PAIR = 128
TILE = 256
BOTH = ("dp", "tensor")
ANY = pl.BlockSpec(memory_space=pl.ANY)
WHOLE = pl.BlockSpec(memory_space=pltpu.VMEM)
SCALARS = pl.BlockSpec(memory_space=pltpu.SMEM)
LOW = jnp.bfloat16


def params(mib):
    return pltpu.CompilerParams(vmem_limit_bytes=mib * 1024 * 1024)


def lasting(us):
    return pl.CostEstimate(flops=int(us * 1.1e7), bytes_accessed=0, transcendentals=0)


def far_memory(value):
    return pltpu.with_memory_space_constraint(value, pltpu.HBM)


def up(value):
    return value.astype(jnp.float32)


def dot_nn(a, b):
    return lax.dot_general(a, b, (((1,), (0,)), ((), ())), preferred_element_type=jnp.float32)


def dot_nt(a, b):
    return lax.dot_general(a, b, (((1,), (1,)), ((), ())), preferred_element_type=jnp.float32)


def dot_tn(a, b):
    return lax.dot_general(a, b, (((0,), (0,)), ((), ())), preferred_element_type=jnp.float32)


REDUCE_BIAS, GAIN_ONE, BIAS_ONE, GAIN_TWO, BIAS_TWO, GAIN_THREE, BIAS_THREE = range(-7, 0)


def norm_rows(matrix):
    centred = matrix - jnp.mean(matrix, -1, keepdims=True)
    inverse = lax.rsqrt(jnp.mean(centred * centred, -1, keepdims=True) + EPSILON)
    return centred * inverse, inverse


def norm_back(outer_grad, normed, inverse, gains):
    spread = outer_grad * gains
    return inverse * (
        spread
        - jnp.mean(spread, -1, keepdims=True)
        - normed * jnp.mean(spread * normed, -1, keepdims=True)
    )


def down(matrix):
    return jnp.sum(matrix, 0, keepdims=True)


def table_row(table_ref, row):
    row += table_ref.shape[0]
    return table_ref[row : row + 1]


def hidden_kernel(
    fast, spots_ref, mix_ref, merge_ref, first_ref, table_ref, expand_ref, reduce_ref, cotangent_ref, *refs
):
    states_ref, third_ref, pre_ref, normed_ref, inverse_ref, small_ref, *grads = refs[:8]
    active_ref, slope_ref, parts_ref = refs[8:]
    row = functools.partial(table_row, table_ref)
    first_out = first_ref[...] * row(GAIN_ONE) + row(BIAS_ONE)
    normed, inverse = norm_rows(first_out + dot_nt(mix_ref[...], merge_ref[...]))
    normed_ref[...] = normed
    inverse_ref[...] = inverse
    second_out = normed * row(GAIN_TWO) + row(BIAS_TWO)
    second_low = second_out.astype(LOW)
    width = mix_ref.shape[1]
    chunks = expand_ref.shape[1] // width
    output = second_out + row(REDUCE_BIAS)
    for c in range(chunks):
        columns = slice(c * width, (c + 1) * width)
        x = dot_nn(second_low, expand_ref[:, columns]) + table_ref[c : c + 1]
        square = x * x
        bent = jnp.tanh(x * (GATE + (GATE * CUBIC) * square))
        halved = 0.5 + 0.5 * bent
        active = (x * halved).astype(LOW)
        slope_ref[:, columns] = halved + (0.5 * x) * (1.0 - bent * bent) * (
            GATE + (3.0 * GATE * CUBIC) * square
        )
        active_ref[:, columns] = active
        output = output + dot_nt(active, reduce_ref[:, columns])
    normed, inverse = norm_rows(output)
    states_ref[...] = (normed * row(GAIN_THREE) + row(BIAS_THREE)).astype(LOW)
    outer = up(cotangent_ref[...])
    third = norm_back(outer, normed, inverse, row(GAIN_THREE))
    third_ref[...] = third
    output_grad = third.astype(LOW)
    small_ref[...] = jnp.zeros(small_ref.shape, jnp.float32)
    at = table_ref.shape[0]
    small_ref[at + GAIN_THREE : at + GAIN_THREE + 1] = down(outer * normed)
    small_ref[at + BIAS_THREE : at + BIAS_THREE + 1] = down(outer)
    small_ref[at + REDUCE_BIAS : at + REDUCE_BIAS + 1] = down(up(output_grad))
    second_turned, output_turned = second_low.T, output_grad.T
    for c in range(chunks):
        columns = slice(c * width, (c + 1) * width)
        pre_grad = (dot_nn(output_grad, reduce_ref[:, columns]) * slope_ref[:, columns]).astype(LOW)
        pre_ref[:, columns] = pre_grad
        small_ref[c : c + 1] = down(up(pre_grad))
        parts = (dot_nn(second_turned, pre_grad), dot_nn(output_turned, active_ref[:, columns]))
        for i, part in enumerate(parts):
            if fast:
                parts_ref[i, c] = part.astype(LOW)
            else:
                grads[i][:, columns] = part
    if fast:
        blocks = [(parts_ref[i, c], (c,), i * width) for i in range(2) for c in range(chunks)]
        store_blocks(spots_ref, *grads, blocks)


def hidden_back_kernel(
    third_ref, pre_ref, expand_ref, normed_ref, inverse_ref, table_ref, merge_ref, mixed_ref, *refs
):
    inner_ref, mix_ref, small_ref, grad_ref = refs
    normed = normed_ref[...]
    outer = third_ref[...] + dot_nt(pre_ref[...], expand_ref[...])
    inner = norm_back(outer, normed, inverse_ref[...], table_row(table_ref, GAIN_TWO))
    inner_ref[...] = inner
    low = inner.astype(LOW)
    mix_ref[...] = dot_nn(low, merge_ref[...]).astype(LOW)
    grad_ref[...] = dot_tn(low, mixed_ref[...]).astype(grad_ref.dtype)
    small_ref[0:1] = down(outer * normed)
    small_ref[1:2] = down(outer)


def first_back_kernel(
    second_ref, rows_ref, query_ref, normed_ref, inverse_ref, table_ref, merge_ref, one_ref, two_ref, *refs
):
    inner_ref, low_ref, mix_ref, small_ref = refs
    normed = normed_ref[...]
    outer = second_ref[...] + dot_nt(rows_ref[...], query_ref[...])
    inner = norm_back(outer, normed, inverse_ref[...], table_row(table_ref, GAIN_ONE))
    inner_ref[...] = inner
    low = inner.astype(LOW)
    low_ref[...] = low
    mix_ref[...] = dot_nn(low, merge_ref[...]).astype(LOW)
    at = table_ref.shape[0]
    small_ref[...] = one_ref[...]
    small_ref[at + GAIN_TWO : at + BIAS_TWO + 1] = two_ref[0:2]
    small_ref[at + GAIN_ONE : at + GAIN_ONE + 1] = down(outer * normed)
    small_ref[at + BIAS_ONE : at + BIAS_ONE + 1] = down(outer)


def kernel_call(kernel, outs, mib, us, name, *operands, scalars=0, scratch=()):
    return pl.pallas_call(
        kernel,
        out_shape=[jax.ShapeDtypeStruct(*out) for out in outs],
        in_specs=[SCALARS] * scalars + [WHOLE] * (len(operands) - scalars),
        out_specs=[WHOLE] * len(outs),
        scratch_shapes=list(scratch),
        compiler_params=params(mib),
        cost_estimate=lasting(us),
        name=name,
    )(*operands)


def split_heads(rows):
    lane = lax.broadcasted_iota(jnp.int32, rows.shape, 1)
    zero = jnp.zeros_like(rows)
    return jnp.concatenate(
        [jnp.where(lane < PAIR // 2, rows, zero), jnp.where(lane < PAIR // 2, zero, rows)], 0
    )


def twice(row):
    return jnp.concatenate([row, row], 1)


def pair_columns(count):
    return [slice(p * PAIR, (p + 1) * PAIR) for p in range(count)]


def attend_all(near_ref, bias_ref, q_ref, sides, out_ref, lse_ref, scratch):
    k_near, k_far, v_near, v_far = sides
    turned, stacked, top, total, acc = scratch
    nq, nk = q_ref.shape[0] // TILE, k_near.shape[0] // TILE
    half = PAIR // 2
    columns = pair_columns(stacked.shape[0])
    for p, pair in enumerate(columns):
        turned[p, 0] = v_near[:, pair].T
        turned[p, 1] = v_far[:, pair].T
    for i in range(nq):
        q_rows = slice(i * TILE, (i + 1) * TILE)
        for p, pair in enumerate(columns):
            stacked[p] = split_heads(q_ref[q_rows, pair])
        top[...] = jnp.full(top.shape, -3e30, jnp.float32)
        total[...] = jnp.zeros(total.shape, jnp.float32)
        acc[...] = jnp.zeros(acc.shape, jnp.float32)
        for j in range(2 * nk):

            @pl.when(near_ref[i, j] != 0)
            def _(j=j, q_rows=q_rows):
                k_ref = k_far if j >= nk else k_near
                k_rows = slice(j % nk * TILE, (j % nk + 1) * TILE)
                bias = twice(bias_ref[j * TILE : (j + 1) * TILE, q_rows])
                products = [dot_nt(k_ref[k_rows, pair], stacked[p]) for p, pair in enumerate(columns)]
                for p, product in enumerate(products):
                    scores = product + bias
                    old = top[p]
                    peak = jnp.maximum(old, jnp.max(scores, 0, keepdims=True))
                    fade = jnp.exp2((old - peak) * LOG2E)
                    powers = jnp.exp2((scores - peak) * LOG2E)
                    top[p] = peak
                    total[p] = total[p] * fade + jnp.sum(powers, 0, keepdims=True)
                    acc[p] = acc[p] * fade + dot_nn(
                        turned[p, j // nk, :, k_rows], powers.astype(LOW)
                    )

        for p, pair in enumerate(columns):
            full = total[p]
            scaled = acc[p] * (1.0 / full)
            mixed = jnp.concatenate([scaled[:half, :TILE], scaled[half:, TILE:]], 0)
            out_ref[q_rows, pair] = mixed.T.astype(LOW)
            log_total = top[p] * LOG2E + jnp.log2(full)
            lse_ref[p, 0:1, q_rows] = log_total[:, :TILE]
            lse_ref[p, 1:2, q_rows] = log_total[:, TILE:]


def attend_scratch(pairs, lk):
    return [
        pltpu.VMEM((pairs, 2, PAIR, lk), LOW),
        pltpu.VMEM((pairs, 2 * TILE, PAIR), LOW),
        pltpu.VMEM((pairs, 1, 2 * TILE), jnp.float32),
        pltpu.VMEM((pairs, 1, 2 * TILE), jnp.float32),
        pltpu.VMEM((pairs, PAIR, 2 * TILE), jnp.float32),
    ]


def place_whole(spots_ref, pieces, out, at):
    me_dp, me_t = spots_ref[0], spots_ref[1]
    rows = pieces[0].shape[2]
    for piece, (dp_flips, t_flips) in zip(pieces, PIECES):
        for a, dp_flip in enumerate(dp_flips):
            row = pl.multiple_of(jnp.bitwise_xor(me_dp, dp_flip) * rows, rows)
            for b, t_flip in enumerate(t_flips):
                column = pl.multiple_of(jnp.bitwise_xor(me_t, t_flip) * PAIR, PAIR)
                out[pl.ds(row, rows), pl.ds(column, PAIR)] = piece[a, b, :, at : at + PAIR]


class Copies:
    def __init__(self, held, outs, sems):
        self.copies = [
            pltpu.make_async_copy(one, out, sems.at[i]) for i, (one, out) in enumerate(zip(held, outs))
        ]

    def start(self, *which):
        for i in which:
            self.copies[i].start()

    def wait(self):
        for copy in self.copies:
            copy.wait()


def self_kernel(
    fast, spots_ref, near_ref, bias_ref, query_ref, token_ref, far_ref, *refs
):
    cut = 2 if fast else 3
    n = 8 if fast else 5
    gathered, (out_ref, lse_ref), outs = refs[:cut], refs[cut : cut + 2], refs[cut + 2 : cut + 2 + n]
    scratch = refs[cut + 2 + n :]
    held, sems, scratch = scratch[:n], scratch[n], scratch[n + 1 :]
    copies = Copies(held, outs, sems)
    q_ref, sides, weights = held[0], held[1:5], held[5:]
    if fast:
        for i, weight in enumerate(weights):
            place_whole(spots_ref, gathered, weight, i * PAIR)
        copies.start(5, 6, 7)
    else:
        weights = gathered
    w_query, w_key, w_value = (weight[...] for weight in weights)
    q_ref[...] = (dot_nn(query_ref[...], w_query) * 0.125).astype(LOW)
    for i, (rows, weight) in enumerate(
        ((token_ref, w_key), (far_ref, w_key), (token_ref, w_value), (far_ref, w_value))
    ):
        sides[i][...] = dot_nn(rows[...], weight).astype(LOW)
    copies.start(0, 1, 2, 3, 4)
    attend_all(near_ref, bias_ref, q_ref, sides, out_ref, lse_ref, scratch)
    copies.wait()


def self_forward(fast, spots, near, bias, streams, gathered, us):
    lq, width = streams[0].shape
    lk, pairs = streams[1].shape[0], width // PAIR
    rows, keys, square = (((n, width), LOW) for n in (lq, lk, width))
    kept = [rows] + [keys] * 4 + ([square] * 3 if fast else [])
    results = pl.pallas_call(
        functools.partial(self_kernel, fast),
        in_specs=[SCALARS, SCALARS] + [WHOLE] * (4 + len(gathered)),
        out_specs=[WHOLE, WHOLE] + [ANY] * len(kept),
        out_shape=[
            jax.ShapeDtypeStruct(*rows),
            jax.ShapeDtypeStruct((pairs, 2, lq), jnp.float32),
            *(pltpu.HBM(*out) for out in kept),
        ],
        scratch_shapes=[pltpu.VMEM(*out) for out in kept]
        + [pltpu.SemaphoreType.DMA((len(kept),))]
        + attend_scratch(pairs, lk),
        compiler_params=params(24),
        cost_estimate=lasting(us),
        name="self_forward",
    )(spots, near, bias, *map(far_memory, streams), *gathered)
    mixture, lse, queries = results[:3]
    return mixture, lse, queries, results[3:7], results[7:] if fast else gathered


def cross_kernel(
    fast, spots_ref, near_ref, bias_ref, mix_ref, stream_ref, near_rows, far_rows, table_ref, *refs
):
    cut = 2 if fast else 4
    n = 12 if fast else 8
    gathered, (out_ref, lse_ref), outs = refs[:cut], refs[cut : cut + 2], refs[cut + 2 : cut + 2 + n]
    scratch = refs[cut + 2 + n :]
    held, sems, scratch = scratch[:n], scratch[n], scratch[n + 1 :]
    copies = Copies(held, outs, sems)
    rows_ref, normed_ref, inverse_ref, low_ref = held[:4]
    sides, weights = held[4:8], held[8:]
    if fast:
        for i, weight in enumerate(weights):
            place_whole(spots_ref, gathered, weight, i * PAIR)
        copies.start(8, 9, 10, 11)
    else:
        weights = gathered
    w_merge, w_query, w_key, w_value = weights
    normed, inverse = norm_rows(up(stream_ref[...]) + dot_nt(mix_ref[...], w_merge[...]))
    normed_ref[...] = normed
    inverse_ref[...] = inverse
    low = (normed * table_row(table_ref, GAIN_ONE) + table_row(table_ref, BIAS_ONE)).astype(LOW)
    low_ref[...] = low
    rows_ref[...] = (dot_nn(low, w_query[...]) * 0.125).astype(LOW)
    for i, (rows, weight) in enumerate(
        ((near_rows, w_key), (far_rows, w_key), (near_rows, w_value), (far_rows, w_value))
    ):
        sides[i][...] = dot_nn(rows[...], weight[...]).astype(LOW)
    copies.start(0, 1, 2, 3, 4, 5, 6, 7)
    attend_all(near_ref, bias_ref, rows_ref, sides, out_ref, lse_ref, scratch)
    copies.wait()


def cross_forward(fast, spots, near, bias, mixture, stream, sources, table, gathered, us):
    lq, width = mixture.shape
    lk, pairs = sources[0].shape[0], width // PAIR
    rows, keys, square = (((n, width), LOW) for n in (lq, lk, width))
    kept = [rows, ((lq, width), jnp.float32), ((lq, 1), jnp.float32), rows] + [keys] * 4
    if fast:
        kept += [square] * 4
    results = pl.pallas_call(
        functools.partial(cross_kernel, fast),
        in_specs=[SCALARS, SCALARS] + [WHOLE] * (6 + len(gathered)),
        out_specs=[WHOLE, WHOLE] + [ANY] * len(kept),
        out_shape=[
            jax.ShapeDtypeStruct(*rows),
            jax.ShapeDtypeStruct((pairs, 2, lq), jnp.float32),
            *(pltpu.HBM(*out) for out in kept),
        ],
        scratch_shapes=[pltpu.VMEM(*out) for out in kept]
        + [pltpu.SemaphoreType.DMA((len(kept),))]
        + attend_scratch(pairs, lk),
        compiler_params=params(30),
        cost_estimate=lasting(us),
        name="cross_forward",
    )(spots, near, bias, mixture, far_memory(stream), *map(far_memory, sources), table, *gathered)
    return results[:6], results[6:10], results[10:] if fast else gathered


def backward_kernel(near_ref, bias_ref, q_ref, m_ref, o_ref, lse_ref, *refs):
    k_near, k_far, v_near, v_far, dq_ref, *outs = refs[:9]
    stacked, grads, delta, log_total, dq_acc, dk_acc, dv_acc = refs[9:]
    nq, nk = q_ref.shape[0] // TILE, k_near.shape[0] // TILE
    half = PAIR // 2
    columns = pair_columns(stacked.shape[0])
    dk_acc[...] = jnp.zeros(dk_acc.shape, jnp.float32)
    dv_acc[...] = jnp.zeros(dv_acc.shape, jnp.float32)
    for i in range(nq):
        q_rows = slice(i * TILE, (i + 1) * TILE)
        for p, pair in enumerate(columns):
            stacked[p] = split_heads(q_ref[q_rows, pair])
            grads[p] = split_heads(m_ref[q_rows, pair])
            turned = (up(m_ref[q_rows, pair]) * up(o_ref[q_rows, pair])).T
            delta[p] = jnp.concatenate([down(turned[:half]), down(turned[half:])], 1)
            log_total[p] = jnp.concatenate([lse_ref[p, 0:1, q_rows], lse_ref[p, 1:2, q_rows]], 1)
        dq_acc[...] = jnp.zeros(dq_acc.shape, jnp.float32)
        for j in range(2 * nk):

            @pl.when(near_ref[i, j] != 0)
            def _(j=j, q_rows=q_rows):
                k_ref, v_ref = (k_far, v_far) if j >= nk else (k_near, v_near)
                k_rows = slice(j % nk * TILE, (j % nk + 1) * TILE)
                all_rows = slice(j * TILE, (j + 1) * TILE)
                bias = twice(bias_ref[all_rows, q_rows])
                scores = [dot_nt(k_ref[k_rows, pair], stacked[p]) for p, pair in enumerate(columns)]
                outer = [dot_nt(v_ref[k_rows, pair], grads[p]) for p, pair in enumerate(columns)]
                for p, pair in enumerate(columns):
                    weights = jnp.exp2(scores[p] * LOG2E + (bias - log_total[p]))
                    slope = (weights * (outer[p] - delta[p])).astype(LOW)
                    dv_acc[p, all_rows] += dot_nn(weights.astype(LOW), grads[p])
                    dk_acc[p, all_rows] += dot_nn(slope, stacked[p])
                    dq_acc[p] += dot_tn(slope, k_ref[k_rows, pair])

        lane = lax.broadcasted_iota(jnp.int32, (TILE, PAIR), 1)
        for p, pair in enumerate(columns):
            dq_ref[q_rows, pair] = (
                jnp.where(lane < half, dq_acc[p, :TILE], dq_acc[p, TILE:]) * 0.125
            ).astype(LOW)
    size = k_near.shape[0]
    for out, acc, side in zip(outs, (dk_acc, dk_acc, dv_acc, dv_acc), (0, 1, 0, 1)):
        for p, pair in enumerate(columns):
            out[:, pair] = acc[p, side * size : (side + 1) * size].astype(LOW)


def attend_back(near, bias, queries, sides, outer, mixed, lse, us):
    lq, width = queries.shape
    lk, pairs, wide = sides[0].shape[0], 2, 2 * PAIR
    column = lambda p: (0, p)
    q_spec, k_spec = pl.BlockSpec((lq, wide), column), pl.BlockSpec((lk, wide), column)
    return pl.pallas_call(
        backward_kernel,
        grid=(width // wide,),
        in_specs=[SCALARS, WHOLE, q_spec, q_spec, q_spec]
        + [pl.BlockSpec((pairs, 2, lq), lambda p: (p, 0, 0))]
        + [k_spec] * 4,
        out_specs=[q_spec] + [k_spec] * 4,
        out_shape=[jax.ShapeDtypeStruct((lq, width), LOW)]
        + [jax.ShapeDtypeStruct((lk, width), LOW)] * 4,
        scratch_shapes=[
            pltpu.VMEM((pairs, 2 * TILE, PAIR), LOW),
            pltpu.VMEM((pairs, 2 * TILE, PAIR), LOW),
            pltpu.VMEM((pairs, 1, 2 * TILE), jnp.float32),
            pltpu.VMEM((pairs, 1, 2 * TILE), jnp.float32),
            pltpu.VMEM((pairs, 2 * TILE, PAIR), jnp.float32),
            pltpu.VMEM((pairs, 2 * lk, PAIR), jnp.float32),
            pltpu.VMEM((pairs, 2 * lk, PAIR), jnp.float32),
        ],
        compiler_params=params(26),
        cost_estimate=lasting(us),
        name="attend_back",
    )(near, bias, queries, outer, mixed, lse, *sides)


def near_tiles(own, keys):
    own, keys = own.reshape(-1, TILE), keys.reshape(-1, TILE)
    return (
        (keys.min(1)[None] <= own.max(1)[:, None]) & (keys.max(1)[None] >= own.min(1)[:, None])
    ).astype(jnp.int32)


def over_dp(matrix, flip):
    return lax.ppermute(matrix, "dp", [(i, i ^ flip) for i in range(8)])


def over_tensor(matrix, flip):
    return lax.ppermute(matrix, "tensor", [(i, i ^ flip) for i in range(4)])


def ordered(value, *earlier):
    return lax.optimization_barrier((value, *earlier))[0] if earlier else value


PIECES = (((0, 2, 4, 6), (0, 1, 2, 3)), ((1, 3, 5, 7), (0, 1, 2, 3)))


def place_kernel(counts, spots_ref, *refs):
    n = len(counts)
    pieces, outs = refs[:-n], refs[-n:]
    me_dp, me_t = spots_ref[0], spots_ref[1]
    rows = pieces[0].shape[2]
    for piece, (dp_flips, t_flips) in zip(pieces, PIECES):
        for a, dp_flip in enumerate(dp_flips):
            row = pl.multiple_of(jnp.bitwise_xor(me_dp, dp_flip) * rows, rows)
            for b, t_flip in enumerate(t_flips):
                t = jnp.bitwise_xor(me_t, t_flip)
                at = 0
                for out, count in zip(outs, counts):
                    size = count * UNIT
                    column = pl.multiple_of(t * size, UNIT)
                    out[pl.ds(row, rows), pl.ds(column, size)] = piece[a, b, :, at : at + size]
                    at += size


def load_kernel(n, n_vectors, *refs):
    blocks, vectors, out = refs[:n], refs[n : n + n_vectors], refs[n + n_vectors]
    held, sems = refs[-2:]
    copies = []

    def copy(source, target):
        copies.append(pltpu.make_async_copy(source, target, sems.at[len(copies)]))
        copies[-1].start()

    at = 0
    for block in blocks:
        copy(block, out.at[:, at : at + block.shape[1]])
        at += block.shape[1]
    at = 0
    for vector in vectors:
        copy(vector, held.at[at : at + vector.shape[0]])
        at += vector.shape[0]
    for one in copies:
        one.wait()
    if vectors:
        table = refs[-3]
        width = table.shape[1]
        for i in range(table.shape[0]):
            table[i : i + 1] = up(held[i * width : (i + 1) * width]).reshape(1, width)


def load(blocks, vectors=(), width=1):
    total = sum(vector.shape[0] for vector in vectors)
    outs = [((blocks[0].shape[0], sum(block.shape[1] for block in blocks)), LOW)]
    if vectors:
        outs.append(((total // width, width), jnp.float32))
    return pl.pallas_call(
        functools.partial(load_kernel, len(blocks), len(vectors)),
        out_shape=[jax.ShapeDtypeStruct(*out) for out in outs],
        in_specs=[ANY] * (len(blocks) + len(vectors)),
        out_specs=[WHOLE] * len(outs),
        scratch_shapes=[
            pltpu.VMEM((max(total, 1024),), LOW),
            pltpu.SemaphoreType.DMA((len(blocks) + len(vectors),)),
        ],
        compiler_params=params(4),
        name="load",
    )(*map(far_memory, blocks), *map(far_memory, vectors))


def table_kernel(*refs):
    *vectors, out = refs
    width, at = out.shape[1], 0
    for vector in vectors:
        row = up(vector[...])
        for i in range(vector.shape[0] // width):
            out[at : at + 1] = row[i * width : (i + 1) * width].reshape(1, width)
            at += 1


def combine_kernel(keep_ref, core_ref, *outs):
    own, *messages, small = outs
    size = own.shape[0]
    n_small = keep_ref.shape[0] - 4 * size
    if n_small:
        total = (up(keep_ref[4 * size :]) + up(core_ref[4 * size :])).astype(LOW)
        small[...] = total
    own[...] = up(keep_ref[:size]) + up(core_ref[:size])
    for i, message in enumerate(messages, 1):
        rows = slice(i * size, (i + 1) * size)
        message[:size] = (up(keep_ref[rows]) + up(core_ref[rows])).astype(LOW)
        if n_small:
            message[size:] = total


def spread_line(own):
    return [own] + [over_tensor(own, flip) for flip in (1, 2, 3)]


def cut_kernel(*refs):
    *pieces, first, second = refs
    width = first.shape[2]
    for i, piece in enumerate(pieces):
        first[i] = piece[:, :width]
        second[i] = piece[:, width:]


def cut_line(line, width):
    rows, total = line[0].shape
    outs = [((len(line), rows, size), LOW) for size in (width, total - width)]
    return kernel_call(cut_kernel, outs, 8, 1, "cut", *line)


def spread_plane(line):
    return [line] + [over_dp(line, flip) for flip in (2, 4, 6)]


def join(near):
    near = jnp.stack(near)
    return [near, over_dp(near, 1)]


def place(blocks, pieces, spots):
    counts = [block.shape[1] // UNIT for block in blocks]
    rows = blocks[0].shape[0]
    outs = [((8 * rows, 4 * count * UNIT), LOW) for count in counts]
    return kernel_call(
        functools.partial(place_kernel, counts), outs, 18, 1, "place", spots, *pieces, scalars=1
    )


def gather_plain(blocks):
    return [
        lax.all_gather(
            lax.all_gather(block, "dp", axis=0, tiled=True), "tensor", axis=1, tiled=True
        )
        for block in blocks
    ]


def store_blocks(spots_ref, keep_ref, send_ref, parts):
    me_dp, me_t = spots_ref[0], spots_ref[1]

    def store(flipped):
        for full, ts, at in parts:
            rows, size = full.shape[0] // 8, full.shape[1] // len(ts)
            for d in range(8):
                target = send_ref if (d % 2) != flipped else keep_ref
                near = jnp.bitwise_xor(me_dp, d) // 2
                for i, t in enumerate(ts):
                    index = near * 4 + jnp.bitwise_xor(me_t, t)
                    target[pl.ds(pl.multiple_of(index * rows, rows), rows), at : at + size] = full[
                        d * rows : (d + 1) * rows, i * size : (i + 1) * size
                    ]

    pl.when(me_dp % 2 == 0)(functools.partial(store, 0))
    pl.when(me_dp % 2 == 1)(functools.partial(store, 1))


def grad_kernel(layout, n_small, spots_ref, *refs):
    keep_ref, send_ref = refs[-2:]
    refs = list(refs[:-2])
    if n_small:
        small = refs.pop()[...].astype(LOW)
        used = small.shape[1]
        for target in (keep_ref, send_ref):
            target[-n_small:] = jnp.zeros((n_small, target.shape[1]), LOW)
            target[-n_small:, :used] = small
    at, parts = 0, []
    for n_products, n_right in layout:
        full = None if n_products else refs.pop(0)[...]
        for _ in range(n_products):
            left = refs.pop(0)[...]
            right = [refs.pop(0)[...] for _ in range(n_right)]
            product = dot_tn(left, jnp.concatenate(right, 1) if n_right > 1 else right[0])
            full = product if full is None else full + product
        full = full.astype(LOW)
        width = full.shape[1] // n_right
        for i in range(n_right):
            parts.append((full[:, i * width : (i + 1) * width], range(4), at))
            at += width // 4
    store_blocks(spots_ref, keep_ref, send_ref, parts)


def grad_blocks(sums, small, spots, us):
    layout = [
        (0 if products[0][0] is None else len(products), len(products[0][1])) for products in sums
    ]
    rows = 2 * sums[0][0][0].shape[1]
    n_small = sum(term.shape[0] for term in small)
    width = sum(right.shape[1] for products in sums for right in products[0][1])
    operands = [
        matrix
        for products in sums
        for left, rights in products
        for matrix in (left, *rights)
        if matrix is not None
    ]
    out = ((rows + n_small, width // 4), LOW)
    return kernel_call(
        functools.partial(grad_kernel, layout, n_small),
        [out, out],
        28,
        us,
        "grads",
        spots,
        *operands,
        *small,
        scalars=1,
    )


class Reduction:
    def __init__(self, keep, send, widths, n_small=0, halving=False):
        self.keep, self.widths, self.n_small, self.halving = keep, widths, n_small, halving
        self.rows = (keep.shape[0] - n_small) // 16
        self.core = over_dp(send, 1)

    def split(self, matrix):
        cut = matrix.shape[0] - self.n_small
        return matrix[:cut], matrix[cut:]

    def message(self, blocks, small):
        return jnp.concatenate([blocks.astype(LOW), small], 0) if self.n_small else blocks.astype(LOW)

    def first(self, *earlier):
        size, width = 4 * self.rows, self.keep.shape[1]
        message = ((size + self.n_small, width), LOW)
        self.own, *messages, self.small = kernel_call(
            combine_kernel,
            [((size, width), jnp.float32)] + [message] * 3 + [((max(self.n_small, 16), width), LOW)],
            8, 1, "combine",
            self.keep, ordered(self.core, *earlier),
        )
        self.small = self.small[: self.n_small]
        self.plane = [over_dp(piece, 2 * i) for i, piece in enumerate(messages, 1)]

    def add(self, messages):
        (one, small_one), (two, small_two), (three, small_three) = map(self.split, messages)
        total = (self.own + up(one)) + (up(two) + up(three))
        small = (up(self.small) + up(small_one)) + (up(small_two) + up(small_three))
        return total, small

    def second(self, *earlier):
        line, small = self.add([ordered(message, *earlier) for message in self.plane])
        self.small = small.astype(LOW)
        size = self.rows
        if self.halving:
            self.own = line[: 2 * size]
            self.line = [over_tensor(self.message(line[2 * size :], self.small), 2)]
            return
        self.own = line[:size]
        self.line = [
            over_tensor(self.message(line[i * size : (i + 1) * size], self.small), i)
            for i in (1, 2, 3)
        ]

    def add_one(self, message):
        total, small = self.split(message)
        return self.own + up(total), up(self.small) + up(small)

    def third(self, *earlier):
        pair, small = self.add_one(ordered(self.line[0], *earlier))
        self.small = small.astype(LOW)
        self.own = pair[: self.rows]
        self.line = [over_tensor(self.message(pair[self.rows :], self.small), 1)]

    def result(self, *earlier):
        messages = [ordered(message, *earlier) for message in self.line]
        total, small = self.add_one(messages[0]) if self.halving else self.add(messages)
        results, at = [], 0
        for width in self.widths:
            results.append(total[:, at : at + width])
            at += width
        return results, small


class PlainReduction:
    def __init__(self, grads, small=None):
        self.keep = self.core = grads[0]
        self.small = None if small is None else lax.psum(small, BOTH)
        self.parts = [
            lax.psum_scatter(
                lax.psum_scatter(grad, "dp", scatter_dimension=0, tiled=True),
                "tensor",
                scatter_dimension=1,
                tiled=True,
            )
            for grad in grads
        ]

    def first(self, *earlier):
        pass

    second = third = first

    def result(self, *earlier):
        return self.parts, self.small


def reduce_products(fast, sums, spots, us, small=None, halving=False):
    if fast:
        extra = [] if small is None else [small]
        keep, send = grad_blocks(sums, extra, spots, us)
        widths = [right.shape[1] // 4 for products in sums for right in products[0][1]]
        n_small = sum(term.shape[0] for term in extra)
        return Reduction(keep, send, widths, n_small, halving)
    grads = []
    for products in sums:
        for i in range(len(products[0][1])):
            grads.append(
                sum(rights[i] if left is None else dot_tn(left, rights[i]) for left, rights in products)
            )
    return PlainReduction(grads, small)


def pick(array, index, axis):
    return lax.dynamic_index_in_dim(array, index, axis, keepdims=False)


def body(
    query_stream,
    token_stream,
    encoder_states,
    token_segment,
    token_rank,
    source_segment,
    query_map,
    key_map,
    value_map,
    merge_map,
    cross_query,
    cross_key,
    cross_value,
    cross_merge,
    expand_map,
    reduce_map,
    expand_bias,
    reduce_bias,
    gain_first,
    bias_first,
    gain_second,
    bias_second,
    gain_third,
    bias_third,
    cotangent,
    fast,
):
    rows, source_count = query_stream.shape[0], encoder_states.shape[0]
    me_dp, me_t = lax.axis_index("dp"), lax.axis_index("tensor")
    spots = jnp.stack([me_dp, me_t]).astype(jnp.int32)
    sequence, half = me_t // 2, me_t % 2

    groups = (
        (query_map, key_map, value_map),
        (merge_map, cross_query, cross_key, cross_value),
        (cross_merge, expand_map, reduce_map),
    )
    width, hidden = query_stream.shape[1], expand_bias.shape[0]
    vectors = (
        expand_bias, reduce_bias, gain_first, bias_first, gain_second, bias_second, gain_third, bias_third,
    )
    if fast:
        (own_one,) = load(groups[0])
        own_rest, table = load(groups[1] + groups[2], vectors, width)
        line_one = spread_line(own_one)
        far_tokens = over_tensor(token_stream, 1)
        near_one = spread_plane(jnp.stack(line_one))
        token_segment, token_rank, source_segment = (
            ordered(row, *line_one) for row in (token_segment, token_rank, source_segment)
        )
        line_rest = spread_line(ordered(own_rest, *line_one))
        gathered_one = join(near_one)
        far_source = over_tensor(ordered(encoder_states, far_tokens), 1)
        split_at = sum(block.shape[1] for block in groups[1])
    else:
        far_tokens = over_tensor(token_stream, 1)
        far_source = over_tensor(encoder_states, 1)
        gathered_one, gathered_two = gather_plain(groups[0]), gather_plain(groups[1])
        w_cmerge, w_expand, w_reduce = gather_plain(groups[2])

    def halves(row, size):
        return lax.dynamic_slice_in_dim(row, half * size, size), lax.dynamic_slice_in_dim(
            row, (1 - half) * size, size
        )

    segment_row = pick(token_segment, sequence, 0)
    starts_row = jnp.concatenate([jnp.ones((1,), jnp.bool_), segment_row[1:] != segment_row[:-1]])
    own_segment, far_segment = halves(segment_row, rows)
    own_rank, far_rank = halves(pick(token_rank, sequence, 0), rows)
    key_segment = jnp.concatenate([own_segment, far_segment])
    key_rank = jnp.concatenate([own_rank, far_rank])
    key_start = jnp.concatenate(halves(starts_row, rows))
    source_row = jnp.concatenate(halves(pick(source_segment, sequence, 0), source_count))
    self_allowed = (own_segment[None, :] == key_segment[:, None]) & (
        (key_rank[:, None] < own_rank[None, :]) | key_start[:, None]
    )
    cross_allowed = own_segment[None, :] == source_row[:, None]
    self_bias = jnp.where(self_allowed, 0.0, -1e30).astype(jnp.float32)
    cross_bias = jnp.where(cross_allowed, 0.0, -1e30).astype(jnp.float32)
    self_near = near_tiles(own_segment, key_segment)
    cross_near = near_tiles(own_segment, source_row)

    table_rows = sum(vector.shape[0] for vector in vectors) // width
    if not fast:
        (table,) = kernel_call(
            table_kernel, [((table_rows, width), jnp.float32)], 2, 1, "table", *vectors
        )
    small_rows = table_rows + -table_rows % 16
    square, column = ((rows, width), jnp.float32), ((rows, 1), jnp.float32)
    low_square = ((rows, width), LOW)

    mixture, self_total, queries, self_sides, (w_query, w_key, w_value) = self_forward(
        fast, spots, self_near, self_bias, (query_stream, token_stream, far_tokens), gathered_one,
        16,
    )
    self_set = (self_near, self_bias, queries, self_sides)
    if fast:
        line_two, line_three = cut_line([ordered(piece, mixture) for piece in line_rest], split_at)
        near_two = spread_plane(line_two)
        gathered_two = join([ordered(piece, far_source) for piece in near_two])
        near_three = spread_plane(ordered(line_three, near_two[3]))
    cross_outs, source_sides, (w_merge, w_cquery, w_ckey, w_cvalue) = cross_forward(
        fast, spots, cross_near, cross_bias, mixture, query_stream, (encoder_states, far_source), table,
        gathered_two, 22,
    )
    cross_mix, cross_total, cross_rows, first_normed, first_inverse, first_low = cross_outs
    cross_set = (cross_near, cross_bias, cross_rows, source_sides)
    if fast:
        gathered_three = join([ordered(piece, cross_mix) for piece in near_three])
        w_cmerge, w_expand, w_reduce = place(groups[2], gathered_three, spots)
    if fast:
        grads = [((2 * width, hidden // 2), LOW)] * 2
    else:
        grads = [((width, hidden), jnp.float32)] * 2
    hidden_states, third_grad, pre_grad, second_normed, second_inverse, small_one, *grads = kernel_call(
        functools.partial(hidden_kernel, fast),
        [low_square, square, ((rows, hidden), LOW), square, column, ((small_rows, width), jnp.float32), *grads],
        30, 13, "hidden",
        spots, cross_mix, w_cmerge, first_normed, table, w_expand, w_reduce, cotangent,
        scalars=1,
        scratch=[
            pltpu.VMEM((rows, hidden), LOW),
            pltpu.VMEM((rows, hidden), jnp.float32),
            pltpu.VMEM((2, hidden // width, width, width), LOW),
        ],
    )
    if fast:
        hidden_sum = Reduction(*grads, [hidden // 4] * 2, halving=True)
    else:
        hidden_sum = PlainReduction(grads)
    second_in_grad, cross_mix_grad, small_two, cross_merge_grad = kernel_call(
        hidden_back_kernel,
        [square, low_square, ((8, width), jnp.float32), ((width, width), LOW if fast else jnp.float32)],
        18, 3, "hidden_back",
        third_grad, pre_grad, w_expand, second_normed, second_inverse, table, w_cmerge, cross_mix,
    )
    hidden_sum.first(cross_mix_grad)
    cross_rows_grad, *source_grads = attend_back(
        *cross_set, cross_mix_grad, cross_mix, cross_total, 25
    )
    keys_near, keys_far, values_near, values_far = source_grads
    source_back = over_tensor(
        (dot_nt(keys_far, w_ckey) + dot_nt(values_far, w_cvalue)).astype(LOW), 1
    )
    stream_grad, self_out, mixture_grad, packed = kernel_call(
        first_back_kernel, [square, low_square, low_square, ((small_rows, width), jnp.float32)], 12, 2, "first_back",
        second_in_grad, cross_rows_grad, w_cquery, first_normed, first_inverse, table, w_merge, small_one, small_two,
    )
    hidden_sum.second(self_out)
    if fast:
        cross_merge_grad = ordered(cross_merge_grad, *hidden_sum.plane)
    cross_sum = reduce_products(
        fast,
        [
            [(first_low, [cross_rows_grad])],
            [
                (encoder_states, [keys_near, values_near]),
                (far_source, [keys_far, values_far]),
            ],
            [(None, [cross_merge_grad])],
            [(self_out, [mixture])],
        ],
        spots,
        5,
        packed,
        True,
    )
    mixture_grad = ordered(mixture_grad, cross_sum.core)
    cross_sum.first()
    queries_grad, *token_grads = attend_back(*self_set, mixture_grad, mixture, self_total, 16)
    if fast:
        queries_grad = ordered(queries_grad, *cross_sum.plane)
    source_sum = dot_nt(ordered(keys_near, queries_grad), w_ckey) + dot_nt(values_near, w_cvalue)
    keys_near, keys_far, values_near, values_far = token_grads
    self_sum = reduce_products(
        fast,
        [
            [(query_stream, [queries_grad])],
            [
                (token_stream, [keys_near, values_near]),
                (far_tokens, [keys_far, values_far]),
            ],
        ],
        spots,
        3,
    )
    keys_far = ordered(keys_far, self_sum.core)
    token_back = over_tensor(
        (dot_nt(keys_far, w_key) + dot_nt(values_far, w_value)).astype(LOW), 1
    )
    token_sum = dot_nt(keys_near, w_key) + dot_nt(values_near, w_value)
    self_sum.first(source_back)
    if fast:
        cross_sum.second(self_sum.core)
        hidden_sum.third(self_sum.core)
        self_sum.second(*cross_sum.line, *hidden_sum.line)
        cross_sum.third(self_sum.own)
    late = self_sum.plane[0] if fast else queries_grad
    (expand_part, reduce_part), _ = hidden_sum.result(queries_grad)
    (*cross_parts, merge_part), summed = cross_sum.result()
    self_parts, _ = self_sum.result(*(cross_sum.line if fast else ()))
    summed = summed[:, :width].reshape(-1)
    small, at = [], 0
    for vector in vectors:
        small.append(summed[at : at + vector.shape[0]])
        at += vector.shape[0]
    return (
        hidden_states,
        (stream_grad + dot_nt(queries_grad, w_query)).astype(LOW),
        (token_sum + up(token_back)).astype(LOW),
        (source_sum + up(ordered(source_back, late))).astype(LOW),
        *self_parts,
        merge_part,
        *cross_parts,
        expand_part,
        reduce_part,
        *small,
    )


def solution(mesh):
    fast = mesh.shape["dp"] == 8 and mesh.shape["tensor"] == 4
    rows = P(BOTH, None)
    block = P("dp", "tensor")

    def program(*arguments):
        return body(*arguments, fast)

    return jax.shard_map(
        program,
        mesh=mesh,
        in_specs=(rows,) * 3 + (P("dp", None),) * 3 + (block,) * 10 + (P(),) * 8 + (rows,),
        out_specs=(rows,) * 4 + (block,) * 10 + (P(),) * 8,
        check_vma=False,
    )
```

```python
import functools

import jax
import jax.numpy as jnp
from jax import lax
from jax.sharding import PartitionSpec as P
from jax.experimental import pallas as pl
from jax.experimental.pallas import tpu as pltpu

EPSILON = 1e-05
GATE = 0.7978845608028654
CUBIC = 0.044715
LOG2E = 1.4426950408889634
UNIT = 128
PAIR = 128
TILE = 256
BOTH = ("dp", "tensor")
ANY = pl.BlockSpec(memory_space=pl.ANY)
WHOLE = pl.BlockSpec(memory_space=pltpu.VMEM)
SCALARS = pl.BlockSpec(memory_space=pltpu.SMEM)
LOW = jnp.bfloat16


def params(mib):
    return pltpu.CompilerParams(vmem_limit_bytes=mib * 1024 * 1024)


def lasting(us):
    return pl.CostEstimate(flops=int(us * 1.1e7), bytes_accessed=0, transcendentals=0)


def far_memory(value):
    return pltpu.with_memory_space_constraint(value, pltpu.HBM)


def up(value):
    return value.astype(jnp.float32)


def dot_nn(a, b):
    return lax.dot_general(a, b, (((1,), (0,)), ((), ())), preferred_element_type=jnp.float32)


def dot_nt(a, b):
    return lax.dot_general(a, b, (((1,), (1,)), ((), ())), preferred_element_type=jnp.float32)


def dot_tn(a, b):
    return lax.dot_general(a, b, (((0,), (0,)), ((), ())), preferred_element_type=jnp.float32)


REDUCE_BIAS, GAIN_ONE, BIAS_ONE, GAIN_TWO, BIAS_TWO, GAIN_THREE, BIAS_THREE = range(-7, 0)


def norm_rows(matrix):
    centred = matrix - jnp.mean(matrix, -1, keepdims=True)
    inverse = lax.rsqrt(jnp.mean(centred * centred, -1, keepdims=True) + EPSILON)
    return centred * inverse, inverse


def norm_back(outer_grad, normed, inverse, gains):
    spread = outer_grad * gains
    return inverse * (
        spread
        - jnp.mean(spread, -1, keepdims=True)
        - normed * jnp.mean(spread * normed, -1, keepdims=True)
    )


def down(matrix):
    return jnp.sum(matrix, 0, keepdims=True)


def table_row(table_ref, row):
    row += table_ref.shape[0]
    return table_ref[row : row + 1]


def hidden_kernel(
    fast, spots_ref, mix_ref, merge_ref, first_ref, table_ref, expand_ref, reduce_ref, cotangent_ref, *refs
):
    states_ref, third_ref, pre_ref, normed_ref, inverse_ref, small_ref, *grads = refs[:8]
    active_ref, slope_ref, parts_ref = refs[8:]
    row = functools.partial(table_row, table_ref)
    first_out = first_ref[...] * row(GAIN_ONE) + row(BIAS_ONE)
    normed, inverse = norm_rows(first_out + dot_nt(mix_ref[...], merge_ref[...]))
    normed_ref[...] = normed
    inverse_ref[...] = inverse
    second_out = normed * row(GAIN_TWO) + row(BIAS_TWO)
    second_low = second_out.astype(LOW)
    width = mix_ref.shape[1]
    chunks = expand_ref.shape[1] // width
    output = second_out + row(REDUCE_BIAS)
    for c in range(chunks):
        columns = slice(c * width, (c + 1) * width)
        x = dot_nn(second_low, expand_ref[:, columns]) + table_ref[c : c + 1]
        square = x * x
        bent = jnp.tanh(x * (GATE + (GATE * CUBIC) * square))
        halved = 0.5 + 0.5 * bent
        active = (x * halved).astype(LOW)
        slope = halved + (0.5 * x) * (1.0 - bent * bent) * (
            GATE + (3.0 * GATE * CUBIC) * square
        )
        slope_ref[:, columns] = slope.astype(LOW)
        active_ref[:, columns] = active
        output = output + dot_nt(active, reduce_ref[:, columns])
    normed, inverse = norm_rows(output)
    states_ref[...] = (normed * row(GAIN_THREE) + row(BIAS_THREE)).astype(LOW)
    outer = up(cotangent_ref[...])
    third = norm_back(outer, normed, inverse, row(GAIN_THREE))
    third_ref[...] = third
    output_grad = third.astype(LOW)
    small_ref[...] = jnp.zeros(small_ref.shape, jnp.float32)
    at = table_ref.shape[0]
    small_ref[at + GAIN_THREE : at + GAIN_THREE + 1] = down(outer * normed)
    small_ref[at + BIAS_THREE : at + BIAS_THREE + 1] = down(outer)
    small_ref[at + REDUCE_BIAS : at + REDUCE_BIAS + 1] = down(up(output_grad))
    second_turned, output_turned = second_low.T, output_grad.T
    for c in range(chunks):
        columns = slice(c * width, (c + 1) * width)
        pre_grad = (dot_nn(output_grad, reduce_ref[:, columns]) * up(slope_ref[:, columns])).astype(LOW)
        pre_ref[:, columns] = pre_grad
        small_ref[c : c + 1] = down(up(pre_grad))
        parts = (dot_nn(second_turned, pre_grad), dot_nn(output_turned, active_ref[:, columns]))
        for i, part in enumerate(parts):
            if fast:
                parts_ref[i, c] = part.astype(LOW)
            else:
                grads[i][:, columns] = part
    if fast:
        blocks = [(parts_ref[i, c], (c,), i * width) for i in range(2) for c in range(chunks)]
        store_blocks(spots_ref, *grads, blocks)


def hidden_back_kernel(
    third_ref, pre_ref, expand_ref, normed_ref, inverse_ref, table_ref, merge_ref, mixed_ref, *refs
):
    inner_ref, mix_ref, small_ref, grad_ref = refs
    normed = normed_ref[...]
    outer = third_ref[...] + dot_nt(pre_ref[...], expand_ref[...])
    inner = norm_back(outer, normed, inverse_ref[...], table_row(table_ref, GAIN_TWO))
    inner_ref[...] = inner
    low = inner.astype(LOW)
    mix_ref[...] = dot_nn(low, merge_ref[...]).astype(LOW)
    grad_ref[...] = dot_tn(low, mixed_ref[...]).astype(grad_ref.dtype)
    small_ref[0:1] = down(outer * normed)
    small_ref[1:2] = down(outer)


def first_back_kernel(
    second_ref, rows_ref, query_ref, normed_ref, inverse_ref, table_ref, merge_ref, one_ref, two_ref, *refs
):
    inner_ref, low_ref, mix_ref, small_ref = refs
    normed = normed_ref[...]
    outer = second_ref[...] + dot_nt(rows_ref[...], query_ref[...])
    inner = norm_back(outer, normed, inverse_ref[...], table_row(table_ref, GAIN_ONE))
    inner_ref[...] = inner
    low = inner.astype(LOW)
    low_ref[...] = low
    mix_ref[...] = dot_nn(low, merge_ref[...]).astype(LOW)
    at = table_ref.shape[0]
    small_ref[...] = one_ref[...]
    small_ref[at + GAIN_TWO : at + BIAS_TWO + 1] = two_ref[0:2]
    small_ref[at + GAIN_ONE : at + GAIN_ONE + 1] = down(outer * normed)
    small_ref[at + BIAS_ONE : at + BIAS_ONE + 1] = down(outer)


def kernel_call(kernel, outs, mib, us, name, *operands, scalars=0, scratch=()):
    return pl.pallas_call(
        kernel,
        out_shape=[jax.ShapeDtypeStruct(*out) for out in outs],
        in_specs=[SCALARS] * scalars + [WHOLE] * (len(operands) - scalars),
        out_specs=[WHOLE] * len(outs),
        scratch_shapes=list(scratch),
        compiler_params=params(mib),
        cost_estimate=lasting(us),
        name=name,
    )(*operands)


def split_heads(rows):
    lane = lax.broadcasted_iota(jnp.int32, rows.shape, 1)
    zero = jnp.zeros_like(rows)
    return jnp.concatenate(
        [jnp.where(lane < PAIR // 2, rows, zero), jnp.where(lane < PAIR // 2, zero, rows)], 0
    )


def twice(row):
    return jnp.concatenate([row, row], 1)


def pair_columns(count):
    return [slice(p * PAIR, (p + 1) * PAIR) for p in range(count)]


def attend_all(near_ref, bias_ref, q_ref, sides, out_ref, lse_ref, scratch):
    k_near, k_far, v_near, v_far = sides
    turned, stacked, top, total, acc = scratch
    nq, nk = q_ref.shape[0] // TILE, k_near.shape[0] // TILE
    half = PAIR // 2
    columns = pair_columns(stacked.shape[0])
    for p, pair in enumerate(columns):
        turned[p, 0] = v_near[:, pair].T
        turned[p, 1] = v_far[:, pair].T
    for i in range(nq):
        q_rows = slice(i * TILE, (i + 1) * TILE)
        for p, pair in enumerate(columns):
            stacked[p] = split_heads(q_ref[q_rows, pair])
        top[...] = jnp.full(top.shape, -3e30, jnp.float32)
        total[...] = jnp.zeros(total.shape, jnp.float32)
        acc[...] = jnp.zeros(acc.shape, jnp.float32)
        for j in range(2 * nk):

            @pl.when(near_ref[i, j] != 0)
            def _(j=j, q_rows=q_rows):
                k_ref = k_far if j >= nk else k_near
                k_rows = slice(j % nk * TILE, (j % nk + 1) * TILE)
                bias = twice(bias_ref[j * TILE : (j + 1) * TILE, q_rows])
                products = [dot_nt(k_ref[k_rows, pair], stacked[p]) for p, pair in enumerate(columns)]
                for p, product in enumerate(products):
                    scores = product + bias
                    old = top[p]
                    peak = jnp.maximum(old, jnp.max(scores, 0, keepdims=True))
                    fade = jnp.exp2((old - peak) * LOG2E)
                    powers = jnp.exp2((scores - peak) * LOG2E)
                    top[p] = peak
                    total[p] = total[p] * fade + jnp.sum(powers, 0, keepdims=True)
                    acc[p] = acc[p] * fade + dot_nn(
                        turned[p, j // nk, :, k_rows], powers.astype(LOW)
                    )

        for p, pair in enumerate(columns):
            full = total[p]
            scaled = acc[p] * (1.0 / full)
            mixed = jnp.concatenate([scaled[:half, :TILE], scaled[half:, TILE:]], 0)
            out_ref[q_rows, pair] = mixed.T.astype(LOW)
            log_total = top[p] * LOG2E + jnp.log2(full)
            lse_ref[p, 0:1, q_rows] = log_total[:, :TILE]
            lse_ref[p, 1:2, q_rows] = log_total[:, TILE:]


def attend_scratch(pairs, lk):
    return [
        pltpu.VMEM((pairs, 2, PAIR, lk), LOW),
        pltpu.VMEM((pairs, 2 * TILE, PAIR), LOW),
        pltpu.VMEM((pairs, 1, 2 * TILE), jnp.float32),
        pltpu.VMEM((pairs, 1, 2 * TILE), jnp.float32),
        pltpu.VMEM((pairs, PAIR, 2 * TILE), jnp.float32),
    ]


def place_whole(spots_ref, pieces, out, at):
    me_dp, me_t = spots_ref[0], spots_ref[1]
    rows = pieces[0].shape[2]
    for piece, (dp_flips, t_flips) in zip(pieces, PIECES):
        for a, dp_flip in enumerate(dp_flips):
            row = pl.multiple_of(jnp.bitwise_xor(me_dp, dp_flip) * rows, rows)
            for b, t_flip in enumerate(t_flips):
                column = pl.multiple_of(jnp.bitwise_xor(me_t, t_flip) * PAIR, PAIR)
                out[pl.ds(row, rows), pl.ds(column, PAIR)] = piece[a, b, :, at : at + PAIR]


class Copies:
    def __init__(self, held, outs, sems):
        self.copies = [
            pltpu.make_async_copy(one, out, sems.at[i]) for i, (one, out) in enumerate(zip(held, outs))
        ]

    def start(self, *which):
        for i in which:
            self.copies[i].start()

    def wait(self):
        for copy in self.copies:
            copy.wait()


def self_kernel(
    fast, spots_ref, near_ref, bias_ref, query_ref, token_ref, far_ref, *refs
):
    cut = 2 if fast else 3
    n = 8 if fast else 5
    gathered, (out_ref, lse_ref), outs = refs[:cut], refs[cut : cut + 2], refs[cut + 2 : cut + 2 + n]
    scratch = refs[cut + 2 + n :]
    held, sems, scratch = scratch[:n], scratch[n], scratch[n + 1 :]
    copies = Copies(held, outs, sems)
    q_ref, sides, weights = held[0], held[1:5], held[5:]
    if fast:
        for i, weight in enumerate(weights):
            place_whole(spots_ref, gathered, weight, i * PAIR)
        copies.start(5, 6, 7)
    else:
        weights = gathered
    w_query, w_key, w_value = (weight[...] for weight in weights)
    q_ref[...] = (dot_nn(query_ref[...], w_query) * 0.125).astype(LOW)
    for i, (rows, weight) in enumerate(
        ((token_ref, w_key), (far_ref, w_key), (token_ref, w_value), (far_ref, w_value))
    ):
        sides[i][...] = dot_nn(rows[...], weight).astype(LOW)
    copies.start(0, 1, 2, 3, 4)
    attend_all(near_ref, bias_ref, q_ref, sides, out_ref, lse_ref, scratch)
    copies.wait()


def self_forward(fast, spots, near, bias, streams, gathered, us):
    lq, width = streams[0].shape
    lk, pairs = streams[1].shape[0], width // PAIR
    rows, keys, square = (((n, width), LOW) for n in (lq, lk, width))
    kept = [rows] + [keys] * 4 + ([square] * 3 if fast else [])
    results = pl.pallas_call(
        functools.partial(self_kernel, fast),
        in_specs=[SCALARS, SCALARS] + [WHOLE] * (4 + len(gathered)),
        out_specs=[WHOLE, WHOLE] + [ANY] * len(kept),
        out_shape=[
            jax.ShapeDtypeStruct(*rows),
            jax.ShapeDtypeStruct((pairs, 2, lq), jnp.float32),
            *(pltpu.HBM(*out) for out in kept),
        ],
        scratch_shapes=[pltpu.VMEM(*out) for out in kept]
        + [pltpu.SemaphoreType.DMA((len(kept),))]
        + attend_scratch(pairs, lk),
        compiler_params=params(24),
        cost_estimate=lasting(us),
        name="self_forward",
    )(spots, near, bias, *map(far_memory, streams), *gathered)
    mixture, lse, queries = results[:3]
    return mixture, lse, queries, results[3:7], results[7:] if fast else gathered


def cross_kernel(
    fast, spots_ref, near_ref, bias_ref, mix_ref, stream_ref, near_rows, far_rows, table_ref, *refs
):
    cut = 2 if fast else 4
    n = 12 if fast else 8
    gathered, (out_ref, lse_ref), outs = refs[:cut], refs[cut : cut + 2], refs[cut + 2 : cut + 2 + n]
    scratch = refs[cut + 2 + n :]
    held, sems, scratch = scratch[:n], scratch[n], scratch[n + 1 :]
    copies = Copies(held, outs, sems)
    rows_ref, normed_ref, inverse_ref, low_ref = held[:4]
    sides, weights = held[4:8], held[8:]
    if fast:
        for i, weight in enumerate(weights):
            place_whole(spots_ref, gathered, weight, i * PAIR)
        copies.start(8, 9, 10, 11)
    else:
        weights = gathered
    w_merge, w_query, w_key, w_value = weights
    normed, inverse = norm_rows(up(stream_ref[...]) + dot_nt(mix_ref[...], w_merge[...]))
    normed_ref[...] = normed
    inverse_ref[...] = inverse
    low = (normed * table_row(table_ref, GAIN_ONE) + table_row(table_ref, BIAS_ONE)).astype(LOW)
    low_ref[...] = low
    rows_ref[...] = (dot_nn(low, w_query[...]) * 0.125).astype(LOW)
    for i, (rows, weight) in enumerate(
        ((near_rows, w_key), (far_rows, w_key), (near_rows, w_value), (far_rows, w_value))
    ):
        sides[i][...] = dot_nn(rows[...], weight[...]).astype(LOW)
    copies.start(0, 1, 2, 3, 4, 5, 6, 7)
    attend_all(near_ref, bias_ref, rows_ref, sides, out_ref, lse_ref, scratch)
    copies.wait()


def cross_forward(fast, spots, near, bias, mixture, stream, sources, table, gathered, us):
    lq, width = mixture.shape
    lk, pairs = sources[0].shape[0], width // PAIR
    rows, keys, square = (((n, width), LOW) for n in (lq, lk, width))
    kept = [rows, ((lq, width), jnp.float32), ((lq, 1), jnp.float32), rows] + [keys] * 4
    if fast:
        kept += [square] * 4
    results = pl.pallas_call(
        functools.partial(cross_kernel, fast),
        in_specs=[SCALARS, SCALARS] + [WHOLE] * (6 + len(gathered)),
        out_specs=[WHOLE, WHOLE] + [ANY] * len(kept),
        out_shape=[
            jax.ShapeDtypeStruct(*rows),
            jax.ShapeDtypeStruct((pairs, 2, lq), jnp.float32),
            *(pltpu.HBM(*out) for out in kept),
        ],
        scratch_shapes=[pltpu.VMEM(*out) for out in kept]
        + [pltpu.SemaphoreType.DMA((len(kept),))]
        + attend_scratch(pairs, lk),
        compiler_params=params(30),
        cost_estimate=lasting(us),
        name="cross_forward",
    )(spots, near, bias, mixture, far_memory(stream), *map(far_memory, sources), table, *gathered)
    return results[:6], results[6:10], results[10:] if fast else gathered


def backward_kernel(near_ref, bias_ref, q_ref, m_ref, o_ref, lse_ref, *refs):
    k_near, k_far, v_near, v_far, dq_ref, *outs = refs[:9]
    stacked, grads, delta, log_total, dq_acc, dk_acc, dv_acc = refs[9:]
    nq, nk = q_ref.shape[0] // TILE, k_near.shape[0] // TILE
    half = PAIR // 2
    columns = pair_columns(stacked.shape[0])
    dk_acc[...] = jnp.zeros(dk_acc.shape, jnp.float32)
    dv_acc[...] = jnp.zeros(dv_acc.shape, jnp.float32)
    for i in range(nq):
        q_rows = slice(i * TILE, (i + 1) * TILE)
        for p, pair in enumerate(columns):
            stacked[p] = split_heads(q_ref[q_rows, pair])
            grads[p] = split_heads(m_ref[q_rows, pair])
            turned = (up(m_ref[q_rows, pair]) * up(o_ref[q_rows, pair])).T
            delta[p] = jnp.concatenate([down(turned[:half]), down(turned[half:])], 1)
            log_total[p] = jnp.concatenate([lse_ref[p, 0:1, q_rows], lse_ref[p, 1:2, q_rows]], 1)
        dq_acc[...] = jnp.zeros(dq_acc.shape, jnp.float32)
        for j in range(2 * nk):

            @pl.when(near_ref[i, j] != 0)
            def _(j=j, q_rows=q_rows):
                k_ref, v_ref = (k_far, v_far) if j >= nk else (k_near, v_near)
                k_rows = slice(j % nk * TILE, (j % nk + 1) * TILE)
                all_rows = slice(j * TILE, (j + 1) * TILE)
                bias = twice(bias_ref[all_rows, q_rows])
                scores = [dot_nt(k_ref[k_rows, pair], stacked[p]) for p, pair in enumerate(columns)]
                outer = [dot_nt(v_ref[k_rows, pair], grads[p]) for p, pair in enumerate(columns)]
                for p, pair in enumerate(columns):
                    weights = jnp.exp2(scores[p] * LOG2E + (bias - log_total[p]))
                    slope = (weights * (outer[p] - delta[p])).astype(LOW)
                    dv_acc[p, all_rows] += dot_nn(weights.astype(LOW), grads[p])
                    dk_acc[p, all_rows] += dot_nn(slope, stacked[p])
                    dq_acc[p] += dot_tn(slope, k_ref[k_rows, pair])

        lane = lax.broadcasted_iota(jnp.int32, (TILE, PAIR), 1)
        for p, pair in enumerate(columns):
            dq_ref[q_rows, pair] = (
                jnp.where(lane < half, dq_acc[p, :TILE], dq_acc[p, TILE:]) * 0.125
            ).astype(LOW)
    size = k_near.shape[0]
    for out, acc, side in zip(outs, (dk_acc, dk_acc, dv_acc, dv_acc), (0, 1, 0, 1)):
        for p, pair in enumerate(columns):
            out[:, pair] = acc[p, side * size : (side + 1) * size].astype(LOW)


def attend_back(near, bias, queries, sides, outer, mixed, lse, us):
    lq, width = queries.shape
    lk, pairs, wide = sides[0].shape[0], 2, 2 * PAIR
    column = lambda p: (0, p)
    q_spec, k_spec = pl.BlockSpec((lq, wide), column), pl.BlockSpec((lk, wide), column)
    return pl.pallas_call(
        backward_kernel,
        grid=(width // wide,),
        in_specs=[SCALARS, WHOLE, q_spec, q_spec, q_spec]
        + [pl.BlockSpec((pairs, 2, lq), lambda p: (p, 0, 0))]
        + [k_spec] * 4,
        out_specs=[q_spec] + [k_spec] * 4,
        out_shape=[jax.ShapeDtypeStruct((lq, width), LOW)]
        + [jax.ShapeDtypeStruct((lk, width), LOW)] * 4,
        scratch_shapes=[
            pltpu.VMEM((pairs, 2 * TILE, PAIR), LOW),
            pltpu.VMEM((pairs, 2 * TILE, PAIR), LOW),
            pltpu.VMEM((pairs, 1, 2 * TILE), jnp.float32),
            pltpu.VMEM((pairs, 1, 2 * TILE), jnp.float32),
            pltpu.VMEM((pairs, 2 * TILE, PAIR), jnp.float32),
            pltpu.VMEM((pairs, 2 * lk, PAIR), jnp.float32),
            pltpu.VMEM((pairs, 2 * lk, PAIR), jnp.float32),
        ],
        compiler_params=params(26),
        cost_estimate=lasting(us),
        name="attend_back",
    )(near, bias, queries, outer, mixed, lse, *sides)


def near_tiles(own, keys):
    own, keys = own.reshape(-1, TILE), keys.reshape(-1, TILE)
    return (
        (keys.min(1)[None] <= own.max(1)[:, None]) & (keys.max(1)[None] >= own.min(1)[:, None])
    ).astype(jnp.int32)


def over_dp(matrix, flip):
    return lax.ppermute(matrix, "dp", [(i, i ^ flip) for i in range(8)])


def over_tensor(matrix, flip):
    return lax.ppermute(matrix, "tensor", [(i, i ^ flip) for i in range(4)])


def ordered(value, *earlier):
    return lax.optimization_barrier((value, *earlier))[0] if earlier else value


PIECES = (((0, 2, 4, 6), (0, 1, 2, 3)), ((1, 3, 5, 7), (0, 1, 2, 3)))


def place_kernel(counts, spots_ref, *refs):
    n = len(counts)
    pieces, outs = refs[:-n], refs[-n:]
    me_dp, me_t = spots_ref[0], spots_ref[1]
    rows = pieces[0].shape[2]
    for piece, (dp_flips, t_flips) in zip(pieces, PIECES):
        for a, dp_flip in enumerate(dp_flips):
            row = pl.multiple_of(jnp.bitwise_xor(me_dp, dp_flip) * rows, rows)
            for b, t_flip in enumerate(t_flips):
                t = jnp.bitwise_xor(me_t, t_flip)
                at = 0
                for out, count in zip(outs, counts):
                    size = count * UNIT
                    column = pl.multiple_of(t * size, UNIT)
                    out[pl.ds(row, rows), pl.ds(column, size)] = piece[a, b, :, at : at + size]
                    at += size


def load_kernel(n, n_vectors, *refs):
    blocks, vectors, out = refs[:n], refs[n : n + n_vectors], refs[n + n_vectors]
    held, sems = refs[-2:]
    copies = []

    def copy(source, target):
        copies.append(pltpu.make_async_copy(source, target, sems.at[len(copies)]))
        copies[-1].start()

    at = 0
    for block in blocks:
        copy(block, out.at[:, at : at + block.shape[1]])
        at += block.shape[1]
    at = 0
    for vector in vectors:
        copy(vector, held.at[at : at + vector.shape[0]])
        at += vector.shape[0]
    for one in copies:
        one.wait()
    if vectors:
        table = refs[-3]
        width = table.shape[1]
        for i in range(table.shape[0]):
            table[i : i + 1] = up(held[i * width : (i + 1) * width]).reshape(1, width)


def load(blocks, vectors=(), width=1):
    total = sum(vector.shape[0] for vector in vectors)
    outs = [((blocks[0].shape[0], sum(block.shape[1] for block in blocks)), LOW)]
    if vectors:
        outs.append(((total // width, width), jnp.float32))
    return pl.pallas_call(
        functools.partial(load_kernel, len(blocks), len(vectors)),
        out_shape=[jax.ShapeDtypeStruct(*out) for out in outs],
        in_specs=[ANY] * (len(blocks) + len(vectors)),
        out_specs=[WHOLE] * len(outs),
        scratch_shapes=[
            pltpu.VMEM((max(total, 1024),), LOW),
            pltpu.SemaphoreType.DMA((len(blocks) + len(vectors),)),
        ],
        compiler_params=params(4),
        name="load",
    )(*map(far_memory, blocks), *map(far_memory, vectors))


def table_kernel(*refs):
    *vectors, out = refs
    width, at = out.shape[1], 0
    for vector in vectors:
        row = up(vector[...])
        for i in range(vector.shape[0] // width):
            out[at : at + 1] = row[i * width : (i + 1) * width].reshape(1, width)
            at += 1


def combine_kernel(keep_ref, core_ref, *outs):
    own, *messages, small = outs
    size = own.shape[0]
    n_small = keep_ref.shape[0] - 4 * size
    if n_small:
        total = (up(keep_ref[4 * size :]) + up(core_ref[4 * size :])).astype(LOW)
        small[...] = total
    own[...] = up(keep_ref[:size]) + up(core_ref[:size])
    for i, message in enumerate(messages, 1):
        rows = slice(i * size, (i + 1) * size)
        message[:size] = (up(keep_ref[rows]) + up(core_ref[rows])).astype(LOW)
        if n_small:
            message[size:] = total


def spread_line(own):
    return [own] + [over_tensor(own, flip) for flip in (1, 2, 3)]


def cut_kernel(*refs):
    *pieces, first, second = refs
    width = first.shape[2]
    for i, piece in enumerate(pieces):
        first[i] = piece[:, :width]
        second[i] = piece[:, width:]


def cut_line(line, width):
    rows, total = line[0].shape
    outs = [((len(line), rows, size), LOW) for size in (width, total - width)]
    return kernel_call(cut_kernel, outs, 8, 1, "cut", *line)


def spread_plane(line):
    return [line] + [over_dp(line, flip) for flip in (2, 4, 6)]


def join(near):
    near = jnp.stack(near)
    return [near, over_dp(near, 1)]


def place(blocks, pieces, spots):
    counts = [block.shape[1] // UNIT for block in blocks]
    rows = blocks[0].shape[0]
    outs = [((8 * rows, 4 * count * UNIT), LOW) for count in counts]
    return kernel_call(
        functools.partial(place_kernel, counts), outs, 18, 1, "place", spots, *pieces, scalars=1
    )


def gather_plain(blocks):
    return [
        lax.all_gather(
            lax.all_gather(block, "dp", axis=0, tiled=True), "tensor", axis=1, tiled=True
        )
        for block in blocks
    ]


def store_blocks(spots_ref, keep_ref, send_ref, parts):
    me_dp, me_t = spots_ref[0], spots_ref[1]

    def store(flipped):
        for full, ts, at in parts:
            rows, size = full.shape[0] // 8, full.shape[1] // len(ts)
            for d in range(8):
                target = send_ref if (d % 2) != flipped else keep_ref
                near = jnp.bitwise_xor(me_dp, d) // 2
                for i, t in enumerate(ts):
                    index = near * 4 + jnp.bitwise_xor(me_t, t)
                    target[pl.ds(pl.multiple_of(index * rows, rows), rows), at : at + size] = full[
                        d * rows : (d + 1) * rows, i * size : (i + 1) * size
                    ]

    pl.when(me_dp % 2 == 0)(functools.partial(store, 0))
    pl.when(me_dp % 2 == 1)(functools.partial(store, 1))


def grad_kernel(layout, n_small, spots_ref, *refs):
    keep_ref, send_ref = refs[-2:]
    refs = list(refs[:-2])
    if n_small:
        small = refs.pop()[...].astype(LOW)
        used = small.shape[1]
        for target in (keep_ref, send_ref):
            target[-n_small:] = jnp.zeros((n_small, target.shape[1]), LOW)
            target[-n_small:, :used] = small
    at, parts = 0, []
    for n_products, n_right in layout:
        full = None if n_products else refs.pop(0)[...]
        for _ in range(n_products):
            left = refs.pop(0)[...]
            right = [refs.pop(0)[...] for _ in range(n_right)]
            product = dot_tn(left, jnp.concatenate(right, 1) if n_right > 1 else right[0])
            full = product if full is None else full + product
        full = full.astype(LOW)
        width = full.shape[1] // n_right
        for i in range(n_right):
            parts.append((full[:, i * width : (i + 1) * width], range(4), at))
            at += width // 4
    store_blocks(spots_ref, keep_ref, send_ref, parts)


def grad_blocks(sums, small, spots, us):
    layout = [
        (0 if products[0][0] is None else len(products), len(products[0][1])) for products in sums
    ]
    rows = 2 * sums[0][0][0].shape[1]
    n_small = sum(term.shape[0] for term in small)
    width = sum(right.shape[1] for products in sums for right in products[0][1])
    operands = [
        matrix
        for products in sums
        for left, rights in products
        for matrix in (left, *rights)
        if matrix is not None
    ]
    out = ((rows + n_small, width // 4), LOW)
    return kernel_call(
        functools.partial(grad_kernel, layout, n_small),
        [out, out],
        28,
        us,
        "grads",
        spots,
        *operands,
        *small,
        scalars=1,
    )


class Reduction:
    def __init__(self, keep, send, widths, n_small=0, halving=False):
        self.keep, self.widths, self.n_small, self.halving = keep, widths, n_small, halving
        self.rows = (keep.shape[0] - n_small) // 16
        self.core = over_dp(send, 1)

    def split(self, matrix):
        cut = matrix.shape[0] - self.n_small
        return matrix[:cut], matrix[cut:]

    def message(self, blocks, small):
        return jnp.concatenate([blocks.astype(LOW), small], 0) if self.n_small else blocks.astype(LOW)

    def first(self, *earlier):
        size, width = 4 * self.rows, self.keep.shape[1]
        message = ((size + self.n_small, width), LOW)
        self.own, *messages, self.small = kernel_call(
            combine_kernel,
            [((size, width), jnp.float32)] + [message] * 3 + [((max(self.n_small, 16), width), LOW)],
            8, 1, "combine",
            self.keep, ordered(self.core, *earlier),
        )
        self.small = self.small[: self.n_small]
        self.plane = [over_dp(piece, 2 * i) for i, piece in enumerate(messages, 1)]

    def add(self, messages):
        (one, small_one), (two, small_two), (three, small_three) = map(self.split, messages)
        total = (self.own + up(one)) + (up(two) + up(three))
        small = (up(self.small) + up(small_one)) + (up(small_two) + up(small_three))
        return total, small

    def second(self, *earlier):
        line, small = self.add([ordered(message, *earlier) for message in self.plane])
        self.small = small.astype(LOW)
        size = self.rows
        if self.halving:
            self.own = line[: 2 * size]
            self.line = [over_tensor(self.message(line[2 * size :], self.small), 2)]
            return
        self.own = line[:size]
        self.line = [
            over_tensor(self.message(line[i * size : (i + 1) * size], self.small), i)
            for i in (1, 2, 3)
        ]

    def add_one(self, message):
        total, small = self.split(message)
        return self.own + up(total), up(self.small) + up(small)

    def third(self, *earlier):
        pair, small = self.add_one(ordered(self.line[0], *earlier))
        self.small = small.astype(LOW)
        self.own = pair[: self.rows]
        self.line = [over_tensor(self.message(pair[self.rows :], self.small), 1)]

    def result(self, *earlier):
        messages = [ordered(message, *earlier) for message in self.line]
        total, small = self.add_one(messages[0]) if self.halving else self.add(messages)
        results, at = [], 0
        for width in self.widths:
            results.append(total[:, at : at + width])
            at += width
        return results, small


class PlainReduction:
    def __init__(self, grads, small=None):
        self.keep = self.core = grads[0]
        self.small = None if small is None else lax.psum(small, BOTH)
        self.parts = [
            lax.psum_scatter(
                lax.psum_scatter(grad, "dp", scatter_dimension=0, tiled=True),
                "tensor",
                scatter_dimension=1,
                tiled=True,
            )
            for grad in grads
        ]

    def first(self, *earlier):
        pass

    second = third = first

    def result(self, *earlier):
        return self.parts, self.small


def reduce_products(fast, sums, spots, us, small=None, halving=False):
    if fast:
        extra = [] if small is None else [small]
        keep, send = grad_blocks(sums, extra, spots, us)
        widths = [right.shape[1] // 4 for products in sums for right in products[0][1]]
        n_small = sum(term.shape[0] for term in extra)
        return Reduction(keep, send, widths, n_small, halving)
    grads = []
    for products in sums:
        for i in range(len(products[0][1])):
            grads.append(
                sum(rights[i] if left is None else dot_tn(left, rights[i]) for left, rights in products)
            )
    return PlainReduction(grads, small)


def pick(array, index, axis):
    return lax.dynamic_index_in_dim(array, index, axis, keepdims=False)


def body(
    query_stream,
    token_stream,
    encoder_states,
    token_segment,
    token_rank,
    source_segment,
    query_map,
    key_map,
    value_map,
    merge_map,
    cross_query,
    cross_key,
    cross_value,
    cross_merge,
    expand_map,
    reduce_map,
    expand_bias,
    reduce_bias,
    gain_first,
    bias_first,
    gain_second,
    bias_second,
    gain_third,
    bias_third,
    cotangent,
    fast,
):
    rows, source_count = query_stream.shape[0], encoder_states.shape[0]
    me_dp, me_t = lax.axis_index("dp"), lax.axis_index("tensor")
    spots = jnp.stack([me_dp, me_t]).astype(jnp.int32)
    sequence, half = me_t // 2, me_t % 2

    groups = (
        (query_map, key_map, value_map),
        (merge_map, cross_query, cross_key, cross_value),
        (cross_merge, expand_map, reduce_map),
    )
    width, hidden = query_stream.shape[1], expand_bias.shape[0]
    vectors = (
        expand_bias, reduce_bias, gain_first, bias_first, gain_second, bias_second, gain_third, bias_third,
    )
    if fast:
        (own_one,) = load(groups[0])
        own_rest, table = load(groups[1] + groups[2], vectors, width)
        line_one = spread_line(own_one)
        far_tokens = over_tensor(token_stream, 1)
        near_one = spread_plane(jnp.stack(line_one))
        token_segment, token_rank, source_segment = (
            ordered(row, *line_one) for row in (token_segment, token_rank, source_segment)
        )
        line_rest = spread_line(ordered(own_rest, *line_one))
        gathered_one = join(near_one)
        far_source = over_tensor(ordered(encoder_states, far_tokens), 1)
        split_at = sum(block.shape[1] for block in groups[1])
    else:
        far_tokens = over_tensor(token_stream, 1)
        far_source = over_tensor(encoder_states, 1)
        gathered_one, gathered_two = gather_plain(groups[0]), gather_plain(groups[1])
        w_cmerge, w_expand, w_reduce = gather_plain(groups[2])

    def halves(row, size):
        return lax.dynamic_slice_in_dim(row, half * size, size), lax.dynamic_slice_in_dim(
            row, (1 - half) * size, size
        )

    segment_row = pick(token_segment, sequence, 0)
    starts_row = jnp.concatenate([jnp.ones((1,), jnp.bool_), segment_row[1:] != segment_row[:-1]])
    own_segment, far_segment = halves(segment_row, rows)
    own_rank, far_rank = halves(pick(token_rank, sequence, 0), rows)
    key_segment = jnp.concatenate([own_segment, far_segment])
    key_rank = jnp.concatenate([own_rank, far_rank])
    key_start = jnp.concatenate(halves(starts_row, rows))
    source_row = jnp.concatenate(halves(pick(source_segment, sequence, 0), source_count))
    self_allowed = (own_segment[None, :] == key_segment[:, None]) & (
        (key_rank[:, None] < own_rank[None, :]) | key_start[:, None]
    )
    cross_allowed = own_segment[None, :] == source_row[:, None]
    self_bias = jnp.where(self_allowed, 0.0, -1e30).astype(jnp.float32)
    cross_bias = jnp.where(cross_allowed, 0.0, -1e30).astype(jnp.float32)
    self_near = near_tiles(own_segment, key_segment)
    cross_near = near_tiles(own_segment, source_row)

    table_rows = sum(vector.shape[0] for vector in vectors) // width
    if not fast:
        (table,) = kernel_call(
            table_kernel, [((table_rows, width), jnp.float32)], 2, 1, "table", *vectors
        )
    small_rows = table_rows + -table_rows % 16
    square, column = ((rows, width), jnp.float32), ((rows, 1), jnp.float32)
    low_square = ((rows, width), LOW)

    mixture, self_total, queries, self_sides, (w_query, w_key, w_value) = self_forward(
        fast, spots, self_near, self_bias, (query_stream, token_stream, far_tokens), gathered_one,
        16,
    )
    self_set = (self_near, self_bias, queries, self_sides)
    if fast:
        line_two, line_three = cut_line([ordered(piece, mixture) for piece in line_rest], split_at)
        near_two = spread_plane(line_two)
        gathered_two = join([ordered(piece, far_source) for piece in near_two])
        near_three = spread_plane(ordered(line_three, near_two[3]))
    cross_outs, source_sides, (w_merge, w_cquery, w_ckey, w_cvalue) = cross_forward(
        fast, spots, cross_near, cross_bias, mixture, query_stream, (encoder_states, far_source), table,
        gathered_two, 22,
    )
    cross_mix, cross_total, cross_rows, first_normed, first_inverse, first_low = cross_outs
    cross_set = (cross_near, cross_bias, cross_rows, source_sides)
    if fast:
        gathered_three = join([ordered(piece, cross_mix) for piece in near_three])
        w_cmerge, w_expand, w_reduce = place(groups[2], gathered_three, spots)
    if fast:
        grads = [((2 * width, hidden // 2), LOW)] * 2
    else:
        grads = [((width, hidden), jnp.float32)] * 2
    hidden_states, third_grad, pre_grad, second_normed, second_inverse, small_one, *grads = kernel_call(
        functools.partial(hidden_kernel, fast),
        [low_square, square, ((rows, hidden), LOW), square, column, ((small_rows, width), jnp.float32), *grads],
        30, 13, "hidden",
        spots, cross_mix, w_cmerge, first_normed, table, w_expand, w_reduce, cotangent,
        scalars=1,
        scratch=[
            pltpu.VMEM((rows, hidden), LOW),
            pltpu.VMEM((rows, hidden), LOW),
            pltpu.VMEM((2, hidden // width, width, width), LOW),
        ],
    )
    if fast:
        hidden_sum = Reduction(*grads, [hidden // 4] * 2, halving=True)
    else:
        hidden_sum = PlainReduction(grads)
    second_in_grad, cross_mix_grad, small_two, cross_merge_grad = kernel_call(
        hidden_back_kernel,
        [square, low_square, ((8, width), jnp.float32), ((width, width), LOW if fast else jnp.float32)],
        18, 3, "hidden_back",
        third_grad, pre_grad, w_expand, second_normed, second_inverse, table, w_cmerge, cross_mix,
    )
    hidden_sum.first(cross_mix_grad)
    cross_rows_grad, *source_grads = attend_back(
        *cross_set, cross_mix_grad, cross_mix, cross_total, 25
    )
    keys_near, keys_far, values_near, values_far = source_grads
    source_back = over_tensor(
        (dot_nt(keys_far, w_ckey) + dot_nt(values_far, w_cvalue)).astype(LOW), 1
    )
    stream_grad, self_out, mixture_grad, packed = kernel_call(
        first_back_kernel, [square, low_square, low_square, ((small_rows, width), jnp.float32)], 12, 2, "first_back",
        second_in_grad, cross_rows_grad, w_cquery, first_normed, first_inverse, table, w_merge, small_one, small_two,
    )
    hidden_sum.second(self_out)
    if fast:
        cross_merge_grad = ordered(cross_merge_grad, *hidden_sum.plane)
    cross_sum = reduce_products(
        fast,
        [
            [(first_low, [cross_rows_grad])],
            [
                (encoder_states, [keys_near, values_near]),
                (far_source, [keys_far, values_far]),
            ],
            [(None, [cross_merge_grad])],
            [(self_out, [mixture])],
        ],
        spots,
        5,
        packed,
        True,
    )
    mixture_grad = ordered(mixture_grad, cross_sum.core)
    cross_sum.first()
    queries_grad, *token_grads = attend_back(*self_set, mixture_grad, mixture, self_total, 16)
    if fast:
        queries_grad = ordered(queries_grad, *cross_sum.plane)
    source_sum = dot_nt(ordered(keys_near, queries_grad), w_ckey) + dot_nt(values_near, w_cvalue)
    keys_near, keys_far, values_near, values_far = token_grads
    self_sum = reduce_products(
        fast,
        [
            [(query_stream, [queries_grad])],
            [
                (token_stream, [keys_near, values_near]),
                (far_tokens, [keys_far, values_far]),
            ],
        ],
        spots,
        3,
    )
    keys_far = ordered(keys_far, self_sum.core)
    token_back = over_tensor(
        (dot_nt(keys_far, w_key) + dot_nt(values_far, w_value)).astype(LOW), 1
    )
    token_sum = dot_nt(keys_near, w_key) + dot_nt(values_near, w_value)
    self_sum.first(source_back)
    if fast:
        cross_sum.second(self_sum.core)
        hidden_sum.third(self_sum.core)
        self_sum.second(*cross_sum.line, *hidden_sum.line)
        cross_sum.third(self_sum.own)
    late = self_sum.plane[0] if fast else queries_grad
    (expand_part, reduce_part), _ = hidden_sum.result(queries_grad)
    (*cross_parts, merge_part), summed = cross_sum.result()
    self_parts, _ = self_sum.result(*(cross_sum.line if fast else ()))
    summed = summed[:, :width].reshape(-1)
    small, at = [], 0
    for vector in vectors:
        small.append(summed[at : at + vector.shape[0]])
        at += vector.shape[0]
    return (
        hidden_states,
        (stream_grad + dot_nt(queries_grad, w_query)).astype(LOW),
        (token_sum + up(token_back)).astype(LOW),
        (source_sum + up(ordered(source_back, late))).astype(LOW),
        *self_parts,
        merge_part,
        *cross_parts,
        expand_part,
        reduce_part,
        *small,
    )


def solution(mesh):
    fast = mesh.shape["dp"] == 8 and mesh.shape["tensor"] == 4
    rows = P(BOTH, None)
    block = P("dp", "tensor")

    def program(*arguments):
        return body(*arguments, fast)

    return jax.shard_map(
        program,
        mesh=mesh,
        in_specs=(rows,) * 3 + (P("dp", None),) * 3 + (block,) * 10 + (P(),) * 8 + (rows,),
        out_specs=(rows,) * 4 + (block,) * 10 + (P(),) * 8,
        check_vma=False,
    )
```
